32 devices in a mesh: expert: 4 (over z), context: 2 (over y), dp: 4 (over x, core).
Axes of the slice: x: 2, y: 2, z: 4, core: 2. Of those that a mesh axis runs over, the one named last changes fastest.
Arguments:
- prompt_in: bfloat16 [16, 128, 2048], P(('expert', 'dp'), 'context'), may hold values from -6 to 6
- cont_in: bfloat16 [16, 2, 128, 2048], P(('expert', 'dp'), 'context'), may hold values from -6 to 6
- prompt_cot: bfloat16 [16, 128, 2048], P(('expert', 'dp'), 'context'), may hold values from -6 to 6
- cont_cot: bfloat16 [16, 2, 128, 2048], P(('expert', 'dp'), 'context'), may hold values from -6 to 6
- prompt_routes: int32 [16, 128, 8], P(('expert', 'dp'), 'context'), may hold values from 0 to 15, all different within a row; in each aligned block of 64 rows (0 to 63, 64 to 127, ..., all dimensions but the last counted through in order) at most 36 rows name the same one
- cont_routes: int32 [16, 2, 128, 8], P(('expert', 'dp'), 'context'), may hold values from 0 to 15, all different within a row; in each aligned block of 128 rows (0 to 127, 128 to 255, ..., all dimensions but the last counted through in order) at most 72 rows name the same one
- prefix: int32 [16, 2], P(('expert', 'dp'), 'context'), may hold values from 1 to 128, as said below
- attn_gain: bfloat16 [2048], P('context'), may hold values from 0.099609375 to 1.8984375
- query_gain: bfloat16 [2048], P('context'), may hold values from 0.099609375 to 1.8984375
- key_gain: bfloat16 [2048], P('context'), may hold values from 0.099609375 to 1.8984375
- ffn_gain: bfloat16 [2048], P('context'), may hold values from 0.099609375 to 1.8984375
- w_query: bfloat16 [2048, 2048], P('context'), may hold values from -0.125 to 0.125
- w_key: bfloat16 [2048, 2048], P('context'), may hold values from -0.125 to 0.125
- w_value: bfloat16 [2048, 2048], P('context'), may hold values from -0.125 to 0.125
- w_output: bfloat16 [2048, 2048], P('context'), may hold values from -1 to 1
- w_router: bfloat16 [2048, 16], P('context'), may hold values from -0.0625 to 0.0625
- expert_gate: bfloat16 [16, 1024, 2048], P(('expert', 'dp')), may hold values from -0.125 to 0.125
- expert_up: bfloat16 [16, 1024, 2048], P(('expert', 'dp')), may hold values from -0.125 to 0.125
- expert_down: bfloat16 [16, 1024, 2048], P(('expert', 'dp')), may hold values from -0.375 to 0.375
Outputs:
- prompt_out: bfloat16 [16, 128, 2048], P(('expert', 'dp'), 'context')
- cont_out: bfloat16 [16, 2, 128, 2048], P(('expert', 'dp'), 'context')
- prompt_grad: float32 [16, 128, 2048], P(('expert', 'dp'), 'context')
- cont_grad: float32 [16, 2, 128, 2048], P(('expert', 'dp'), 'context')
- attn_gain_grad: float32 [2048], P(('expert', 'context', 'dp'))
- query_gain_grad: float32 [2048], P(('expert', 'context', 'dp'))
- key_gain_grad: float32 [2048], P(('expert', 'context', 'dp'))
- ffn_gain_grad: float32 [2048], P(('expert', 'context', 'dp'))
- query_grad: float32 [2048, 2048], P(('expert', 'context', 'dp'))
- key_grad: float32 [2048, 2048], P(('expert', 'context', 'dp'))
- value_grad: float32 [2048, 2048], P(('expert', 'context', 'dp'))
- output_grad: float32 [2048, 2048], P(('expert', 'context', 'dp'))
- router_grad: float32 [2048, 16], P(('expert', 'context', 'dp'))
- gate_grad: float32 [16, 1024, 2048], P(('expert', 'dp'), 'context')
- up_grad: float32 [16, 1024, 2048], P(('expert', 'dp'), 'context')
- down_grad: float32 [16, 1024, 2048], P(('expert', 'dp'), 'context')
The draws below stay inside these ranges and needn't reach their ends.
Inputs may be any that keep to these rules, and one draw needn't show every extreme that they name: `prompt_routes`: each token names 8 different experts; among the prompt tokens of one device no expert is named more than 36 times, and some expert exactly that often. `cont_routes`: each token names 8 different experts; among the continuation tokens of one device no expert is named more than 72 times, and some expert exactly that often. `prefix`: in every group one continuation follows the whole prompt.
All inputs are finite; a program needn't handle non-finite values.
Results may differ from the reference program's by a relative error of at most 0.02.
Values may be sent and summed in bfloat16 or wider, within the bound.
No kernel may reach another device: no remote copies, remote signals or barrier semaphores. Data moves between devices by JAX's collectives and lax.ppermute only.
A program may use at most 320 MiB of HBM per device.

```python
import math
import jax
import jax.numpy as jnp
import numpy as np
from jax import lax

D = 2048
HEADS = 16
HEAD_DIM = 128
FF = 1024
TOP = 8
PROMPT_DEV = 64
CONT_LEN = 128
EXPERTS = 16
GROUPS = 16
PROMPT = 128
NCONT = 2
MOST_P = 36
MOST_C = 72


def draw_prefix(key, part):
    key = jax.random.fold_in(key, 7)
    first_key, second_key = jax.random.split(key)
    lengths = jax.random.randint(first_key, (GROUPS, NCONT), 1, PROMPT + 1)
    chosen = jax.random.randint(second_key, (GROUPS, 1), 0, NCONT)
    columns = jnp.arange(NCONT, dtype=jnp.int32)[None, :]
    return jnp.where(columns == chosen, PROMPT, lengths).astype(jnp.int32)


def block_scale(key, shape, cuts, smallest, high):
    def one(axis_at, shards_of):
        draws = jax.random.uniform(jax.random.fold_in(jax.random.fold_in(key, 6), axis_at), (shards_of,), jnp.float32, smallest / len(cuts), high / len(cuts))
        return jnp.repeat(jnp.exp(draws), shape[axis_at] // shards_of).reshape((-1,) + (1,) * (len(shape) - axis_at - 1))

    factor_of = one(*cuts[0])
    for cut in cuts[1:]:
        factor_of = factor_of * one(*cut)
    return factor_of


def assign_block(stream_key, own, number, rows, count, top, most, slope):
    sequence = jax.random.permutation(stream_key, count)
    packed, usual = portions_of(count, rows * top, most, slope, True), portions_of(count, rows * top, most, slope, False)
    places = jnp.arange(count)

    def named(sizes, turn):
        used = int((sizes > 0).sum())
        fixed = max(1, used // 4)
        moved = fixed + (places - fixed + turn * (used - fixed)) % max(1, count - fixed)
        return jnp.zeros((count,), jnp.int32).at[sequence[jnp.where(places < fixed, places, moved)]].set(jnp.asarray(sizes, jnp.int32))

    sizes = jnp.where(number % 4 == 0, named(packed, number // 4), named(usual, number - number // 4 - 1))
    mixed = jax.random.permutation(jax.random.fold_in(own, 3), count)
    donor, taker = mixed[0:count // 2 * 2:2], mixed[1:count // 2 * 2:2]
    room = jnp.minimum(sizes[donor] - 1, most - sizes[taker]) // 2
    room = jnp.where((donor == sequence[0]) | (taker == sequence[0]) | (sizes[taker] == 0), 0, jnp.maximum(room, 0))
    moved = jax.random.randint(jax.random.fold_in(own, 4), (count // 2,), 0, 1 << 20) % (room + 1)
    sizes = sizes.at[donor].add(-moved).at[taker].add(moved)
    items = jnp.searchsorted(jnp.cumsum(sizes), jnp.arange(rows * top), side="right").astype(jnp.int32)
    grid = items.reshape(top, rows).T
    grid = grid[jax.random.permutation(jax.random.fold_in(own, 1), rows)]
    turn = jax.random.randint(jax.random.fold_in(own, 2), (rows, 1), 0, top)
    return jnp.take_along_axis(grid, (jnp.arange(top)[None, :] + turn) % top, axis=1)


def portions_of(amount, total, limit, slope, full):
    portions = [(1 << 20) // math.isqrt(grade ** slope) + 1 for grade in range(1, amount + 1)]
    largest = limit if full else min(limit, max(-(-total // amount), total * portions[0] // sum(portions)))
    least = 1 if total - largest >= amount - 1 else 0
    counts, rest = [largest] + [least] * (amount - 1), total - largest - least * (amount - 1)
    while rest > 0:
        free = [i for i in range(1, amount) if counts[i] < largest] or [i for i in range(1, amount) if counts[i] < limit]
        pool, remaining = sum([portions[i] for i in free]), rest
        for i in free:
            extra = min(limit - counts[i], max(1, remaining * portions[i] // pool), rest)
            counts[i] = counts[i] + extra
            rest = rest - extra
    return np.array(counts)


def bell_draw(key, shape, width, bound, cuts=(), kind=jnp.bfloat16):
    values = jax.random.normal(key, shape, jnp.float32) * width
    if len(cuts) > 0:
        values = block_scale(key, shape, cuts, -0.22, 0.18) * values
    return jnp.clip(values, min=-bound, max=bound).astype(kind)


def setup_inputs(seed: int = 0) -> dict:
    splits = jax.random.split(jax.random.key(seed), 20)
    prompt_in = bell_draw(splits[0], (GROUPS, PROMPT, D), 1.0, 6.0, ((0, 16), (1, 2)))
    cont_in = bell_draw(splits[1], (GROUPS, NCONT, CONT_LEN, D), 1.0, 6.0, ((0, 16), (1, 2)))
    prompt_cot = bell_draw(splits[2], (GROUPS, PROMPT, D), 1.0, 6.0, ((0, 16), (1, 2)))
    cont_cot = bell_draw(splits[3], (GROUPS, NCONT, CONT_LEN, D), 1.0, 6.0, ((0, 16), (1, 2)))
    prompt_routes_keys = jax.random.split(jax.random.fold_in(splits[4], 1), GROUPS * PROMPT // PROMPT_DEV)
    prompt_routes_turns = jax.random.permutation(jax.random.fold_in(splits[4], 3), GROUPS * PROMPT // PROMPT_DEV)
    prompt_routes = jax.vmap(lambda own, number: assign_block(jax.random.fold_in(splits[4], 2), own, number, PROMPT_DEV, EXPERTS, TOP, MOST_P, 1))(prompt_routes_keys, prompt_routes_turns).reshape((GROUPS, PROMPT, TOP))
    cont_routes_keys = jax.random.split(jax.random.fold_in(splits[5], 1), GROUPS * NCONT * CONT_LEN // CONT_LEN)
    cont_routes_turns = jax.random.permutation(jax.random.fold_in(splits[5], 3), GROUPS * NCONT * CONT_LEN // CONT_LEN)
    cont_routes = jax.vmap(lambda own, number: assign_block(jax.random.fold_in(splits[5], 2), own, number, CONT_LEN, EXPERTS, TOP, MOST_C, 1))(cont_routes_keys, cont_routes_turns).reshape((GROUPS, NCONT, CONT_LEN, TOP))
    prefix = draw_prefix(jax.random.fold_in(splits[19], 71), 0)
    attn_gain = jnp.clip(1.0 + 0.18 * jax.random.normal(splits[7], (D,), jnp.float32), 0.099609375, 1.8984375).astype(jnp.bfloat16)
    query_gain = jnp.clip(1.0 + 0.18 * jax.random.normal(splits[8], (D,), jnp.float32), 0.099609375, 1.8984375).astype(jnp.bfloat16)
    key_gain = jnp.clip(1.0 + 0.18 * jax.random.normal(splits[9], (D,), jnp.float32), 0.099609375, 1.8984375).astype(jnp.bfloat16)
    ffn_gain = jnp.clip(1.0 + 0.18 * jax.random.normal(splits[10], (D,), jnp.float32), 0.099609375, 1.8984375).astype(jnp.bfloat16)
    w_query = bell_draw(splits[11], (D, D), D ** -0.5, 0.125, ((0, 2),))
    w_key = bell_draw(splits[12], (D, D), D ** -0.5, 0.125, ((0, 2),))
    w_value = bell_draw(splits[13], (D, D), D ** -0.5, 0.125, ((0, 2),))
    w_output = bell_draw(splits[14], (D, D), (D // 64) ** -0.5, 1.0, ((0, 2),))
    w_router = bell_draw(splits[15], (D, EXPERTS), (4 * D) ** -0.5, 0.0625, ((0, 2),))
    expert_gate = bell_draw(splits[16], (EXPERTS, FF, D), D ** -0.5, 0.125, ((0, 16),))
    expert_up = bell_draw(splits[17], (EXPERTS, FF, D), D ** -0.5, 0.125, ((0, 16),))
    expert_down = bell_draw(splits[18], (EXPERTS, FF, D), (FF // 4) ** -0.5, 0.375, ((0, 16),))
    return dict(prompt_in=prompt_in, cont_in=cont_in, prompt_cot=prompt_cot, cont_cot=cont_cot, prompt_routes=prompt_routes, cont_routes=cont_routes, prefix=prefix, attn_gain=attn_gain, query_gain=query_gain, key_gain=key_gain, ffn_gain=ffn_gain, w_query=w_query, w_key=w_key, w_value=w_value, w_output=w_output, w_router=w_router, expert_gate=expert_gate, expert_up=expert_up, expert_down=expert_down)


EPSILON = 1e-05
NEG_LARGE = -1e+30
HIGHEST = lax.Precision.HIGHEST

@jax.custom_vjp
def low(v):
    return lax.optimization_barrier(v.astype(jnp.bfloat16)).astype(jnp.float32)

@jax.custom_vjp
def low_back(v):
    return v

def low_keep(v):
    return (low(v), None)

def low_pass(kept, grad):
    return (grad,)

def back_keep(v):
    return (v, None)

def back_low(kept, grad):
    return (low(grad),)
low.defvjp(low_keep, low_pass)
low_back.defvjp(back_keep, back_low)

def matmul(left, right):
    return jnp.dot(left, right, precision=HIGHEST)

def rms_scale(values, gain_row):
    inverse = lax.rsqrt(lax.optimization_barrier(jnp.mean(values * values, axis=-1, keepdims=True)) + EPSILON)
    return values * inverse * gain_row

def angle_table(positions, head_dim):
    half_index = jnp.arange(head_dim // 2, dtype=jnp.float32)
    frequency = 10000.0 ** (-2.0 * half_index / head_dim)
    return positions.astype(jnp.float32)[:, None] * frequency[None, :]

def rotate(values, angles, head_count):
    row_count = values.shape[0]
    shaped = values.reshape(row_count, head_count, -1)
    half_size = shaped.shape[-1] // 2
    first_half = shaped[..., :half_size]
    second = shaped[..., half_size:]
    cosine = jnp.cos(angles)[:, None, :]
    sine_part = jnp.sin(angles)[:, None, :]
    turned = jnp.concatenate([first_half * cosine - second * sine_part, second * cosine + first_half * sine_part], axis=-1)
    return turned.reshape(row_count, -1)

def qk_post(raw_rows, gain_row, angles, head_count):
    return rotate(rms_scale(raw_rows, gain_row), angles, head_count)

def build_mask(prompt_pos, start_len, prompt_total, cont_len):
    key_prompt = jnp.arange(prompt_total, dtype=jnp.int32)[None, :]
    prompt_rows = jnp.concatenate([key_prompt <= prompt_pos[:, None], jnp.zeros((prompt_pos.shape[0], cont_len), dtype=jnp.bool_)], axis=1)
    own_index = jnp.arange(cont_len, dtype=jnp.int32)
    cont_rows = jnp.concatenate([jnp.broadcast_to(key_prompt < start_len, (cont_len, prompt_total)), own_index[None, :] <= own_index[:, None]], axis=1)
    return jnp.concatenate([prompt_rows, cont_rows], axis=0)

def attend(queries, key_set, value_set, read_mask):
    row_count = queries.shape[0]
    q_heads = queries.reshape(row_count, HEADS, HEAD_DIM)
    k_heads = key_set.reshape(key_set.shape[0], HEADS, HEAD_DIM)
    v_heads = value_set.reshape(value_set.shape[0], HEADS, HEAD_DIM)
    raw_scores = jnp.einsum('qhd,khd->hqk', q_heads, k_heads, precision=HIGHEST)
    scores = jnp.where(read_mask[None], low_back(raw_scores) * HEAD_DIM ** (-0.5), NEG_LARGE)
    top_score = lax.optimization_barrier(jnp.max(scores, axis=-1, keepdims=True))
    exponent = jnp.exp(scores - top_score)
    weights = low(exponent / lax.optimization_barrier(jnp.sum(exponent, axis=-1, keepdims=True)))
    return jnp.einsum('hqk,khd->qhd', weights, v_heads, precision=HIGHEST).reshape(row_count, D)

def group_attention(queries, key_rows, value_rows, start_lens):
    prompt_keys = key_rows[:PROMPT]
    prompt_values = value_rows[:PROMPT]
    prompt_queries = queries[:PROMPT].reshape(NCONT, PROMPT_DEV, D)
    cont_queries = queries[PROMPT:].reshape(NCONT, CONT_LEN, D)
    cont_keys = key_rows[PROMPT:].reshape(NCONT, CONT_LEN, D)
    cont_values = value_rows[PROMPT:].reshape(NCONT, CONT_LEN, D)

    def piece(items):
        index, part_queries, own_queries, own_keys, own_values, start_len = items
        prompt_pos = index * PROMPT_DEV + jnp.arange(PROMPT_DEV, dtype=jnp.int32)
        read_mask = build_mask(prompt_pos, start_len, PROMPT, CONT_LEN)
        return attend(jnp.concatenate([part_queries, own_queries], axis=0), jnp.concatenate([prompt_keys, own_keys], axis=0), jnp.concatenate([prompt_values, own_values], axis=0), read_mask)
    pieces = lax.map(jax.checkpoint(piece), (jnp.arange(NCONT, dtype=jnp.int32), prompt_queries, cont_queries, cont_keys, cont_values, start_lens))
    return jnp.concatenate([pieces[:, :PROMPT_DEV].reshape(PROMPT, D), pieces[:, PROMPT_DEV:].reshape(NCONT * CONT_LEN, D)], axis=0)

def group_pass(items):
    return group_attention(items[0], items[1], items[2], items[3])

def reference(prompt_in, cont_in, prompt_cot, cont_cot, prompt_routes, cont_routes, prefix, attn_gain, query_gain, key_gain, ffn_gain, w_query, w_key, w_value, w_output, w_router, expert_gate, expert_up, expert_down):
    group_len = PROMPT + NCONT * CONT_LEN
    routes_all = jnp.concatenate([prompt_routes, cont_routes.reshape(GROUPS, NCONT * CONT_LEN, TOP)], axis=1).reshape(-1, TOP)
    member = lax.optimization_barrier(jnp.sum((routes_all[:, :, None] == jnp.arange(EXPERTS, dtype=jnp.int32)[None, None, :]).astype(jnp.float32), axis=1))
    prompt_pos = jnp.broadcast_to(jnp.arange(PROMPT, dtype=jnp.int32)[None, :], (GROUPS, PROMPT))
    cont_pos = prefix[:, :, None] + jnp.arange(CONT_LEN, dtype=jnp.int32)[None, None, :]
    positions = jnp.concatenate([prompt_pos, cont_pos.reshape(GROUPS, -1)], axis=1).reshape(-1)
    angles = angle_table(positions, HEAD_DIM)

    def forward(prompt_x, cont_x, gain_attn, gain_query, gain_key, gain_ffn, full_query, full_key, full_value, full_output, full_router, gate_all, up_all, down_all):
        x_rows = jnp.concatenate([prompt_x, cont_x.reshape(GROUPS, NCONT * CONT_LEN, D)], axis=1).reshape(-1, D)
        normed_low = low(rms_scale(x_rows, gain_attn))
        query_low = low(qk_post(low_back(matmul(normed_low, full_query)), gain_query, angles, HEADS))
        key_low = low(qk_post(low_back(matmul(normed_low, full_key)), gain_key, angles, HEADS))
        value_low = low(low_back(matmul(normed_low, full_value)))
        attended = lax.map(group_pass, (query_low.reshape(GROUPS, group_len, D), key_low.reshape(GROUPS, group_len, D), value_low.reshape(GROUPS, group_len, D), prefix))
        attended_low = low(low_back(attended.reshape(-1, D)))
        mixed_rows = x_rows + low_back(matmul(attended_low, full_output))
        normed2_low = low(rms_scale(mixed_rows, gain_ffn))
        logits = low_back(matmul(normed2_low, full_router))
        shifted = jnp.exp(logits - lax.optimization_barrier(jnp.max(logits, axis=1, keepdims=True)))
        router_probs = shifted / lax.optimization_barrier(jnp.sum(shifted, axis=1, keepdims=True))
        gates = router_probs * member

        def expert_pass(carry, items):
            gate_w, up_w, down_w, column = items
            expert_in = low_back(normed2_low)
            gate_pre = low_back(jnp.einsum('td,fd->tf', expert_in, gate_w, precision=HIGHEST))
            up_pre = low_back(jnp.einsum('td,fd->tf', expert_in, up_w, precision=HIGHEST))
            act_low = low(gate_pre * jax.nn.sigmoid(gate_pre) * up_pre)
            result = low(low_back(matmul(act_low, down_w)))
            return (carry + column[:, None] * result, None)
        moe_rows, _ = lax.scan(jax.checkpoint(expert_pass), jnp.zeros_like(mixed_rows), (gate_all, up_all, down_all, gates.T))
        out_rows = (mixed_rows + moe_rows).reshape(GROUPS, group_len, D)
        return (out_rows[:, :PROMPT], out_rows[:, PROMPT:].reshape(GROUPS, NCONT, CONT_LEN, D))
    float_args = tuple((array_in.astype(jnp.float32) for array_in in (prompt_in, cont_in, attn_gain, query_gain, key_gain, ffn_gain, w_query, w_key, w_value, w_output, w_router, expert_gate, expert_up, expert_down)))
    outputs, pull_back = jax.vjp(forward, *float_args)
    gradients = pull_back((prompt_cot.astype(jnp.float32), cont_cot.astype(jnp.float32)))
    return (outputs[0].astype(jnp.bfloat16), outputs[1].astype(jnp.bfloat16), gradients[0], gradients[1], gradients[2], gradients[3], gradients[4], gradients[5], gradients[6], gradients[7], gradients[8], gradients[9], gradients[10], gradients[11], gradients[12], gradients[13])
```

```python
import functools

import jax
import jax.numpy as jnp
from jax import lax
from jax.experimental import pallas as pl
from jax.experimental.pallas import tpu as pltpu
from jax.sharding import PartitionSpec as P

HEADS = 16
EPSILON = 1e-05
NEG_LARGE = -1e30
F32 = jnp.float32
BF16 = jnp.bfloat16
PLANE = ("expert", "dp")
VMEM_LIMIT = 48 * 1024 * 1024


def dot(left, right, dims=((1,), (0,)), out=F32):
    return lax.dot_general(left, right, (dims, ((), ())), preferred_element_type=out)


NT = ((1,), (1,))
TN = ((0,), (0,))


def post_kernel(count, *refs):
    parts, (gain_ref, cos_ref, sin_ref, raw_ref, low_ref) = refs[:count], refs[count:]
    raw = parts[0][...]
    for part in parts[1:]:
        raw = raw + part[...].astype(F32)
    raw_ref[...] = raw
    inverse = lax.rsqrt(jnp.mean(raw * raw, axis=-1, keepdims=True) + EPSILON)
    scaled = raw * inverse * gain_ref[...]
    cosine, sine = cos_ref[...], sin_ref[...]
    head = cosine.shape[1]
    for h in range(raw.shape[1] // head):
        piece = scaled[:, h * head : (h + 1) * head]
        turned = piece * cosine + pltpu.roll(piece, head // 2, 1) * sine
        low_ref[:, h * head : (h + 1) * head] = turned.astype(BF16)


def qk_post(parts, gain, cosine, sine):
    rows, width = parts[0].shape
    head = cosine.shape[1]
    step = 64
    row = lambda w: pl.BlockSpec((step, w), lambda i: (i, 0))
    return pl.pallas_call(
        functools.partial(post_kernel, len(parts)),
        grid=(rows // step,),
        in_specs=[row(width)] * len(parts)
        + [pl.BlockSpec((1, width), lambda i: (0, 0)), row(head), row(head)],
        out_specs=[row(width), row(width)],
        out_shape=[
            jax.ShapeDtypeStruct((rows, width), F32),
            jax.ShapeDtypeStruct((rows, width), BF16),
        ],
        compiler_params=pltpu.CompilerParams(vmem_limit_bytes=VMEM_LIMIT),
        name="qk_post",
    )(*parts, gain, cosine, sine)


def post_back_kernel(grad_ref, raw_ref, gain_ref, cos_ref, sin_ref, low_ref, gain_grad_ref):
    raw = raw_ref[...]
    inverse = lax.rsqrt(jnp.mean(raw * raw, axis=-1, keepdims=True) + EPSILON)
    cosine, sine = cos_ref[...], sin_ref[...]
    head = cosine.shape[1]
    pieces = []
    for h in range(raw.shape[1] // head):
        piece = grad_ref[:, h * head : (h + 1) * head]
        pieces.append(piece * cosine - pltpu.roll(piece, head // 2, 1) * sine)
    grad = jnp.concatenate(pieces, axis=1)
    scaled = grad * gain_ref[...]
    centre = jnp.mean(scaled * raw, axis=-1, keepdims=True)
    low_ref[...] = (inverse * scaled - raw * (inverse * inverse * inverse * centre)).astype(BF16)
    total = jnp.sum(grad * raw * inverse, axis=0, keepdims=True)

    @pl.when(pl.program_id(0) == 0)
    def _():
        gain_grad_ref[...] = total

    @pl.when(pl.program_id(0) > 0)
    def _():
        gain_grad_ref[...] += total


def qk_post_back(grad, raw, gain, cosine, sine):
    rows, width = raw.shape
    head = cosine.shape[1]
    step = 64
    row = lambda w: pl.BlockSpec((step, w), lambda i: (i, 0))
    whole = pl.BlockSpec((1, width), lambda i: (0, 0))
    return pl.pallas_call(
        post_back_kernel,
        grid=(rows // step,),
        in_specs=[row(width), row(width), whole, row(head), row(head)],
        out_specs=[row(width), whole],
        out_shape=[
            jax.ShapeDtypeStruct((rows, width), BF16),
            jax.ShapeDtypeStruct((1, width), F32),
        ],
        compiler_params=pltpu.CompilerParams(vmem_limit_bytes=VMEM_LIMIT),
        name="qk_post_back",
    )(grad, raw, gain, cosine, sine)


def read_mask(meta_ref, rows, keys, prompt_dev, prompt_total):
    row = lax.broadcasted_iota(jnp.int32, (rows, keys), 0)
    key = lax.broadcasted_iota(jnp.int32, (rows, keys), 1)
    is_prompt_row = row < prompt_dev
    is_prompt_key = key < prompt_total
    prompt_limit = jnp.where(is_prompt_row, meta_ref[0] + row + 1, meta_ref[1])
    own_limit = jnp.where(is_prompt_row, 0, row - prompt_dev + 1)
    limit = jnp.where(is_prompt_key, prompt_limit, own_limit + prompt_total)
    return key < limit


def head_probs(query, key, mask):
    scores = jnp.where(mask, dot(query, key, NT) * (query.shape[1] ** -0.5), NEG_LARGE)
    exponent = jnp.exp(scores - jnp.max(scores, axis=-1, keepdims=True))
    return exponent / jnp.sum(exponent, axis=-1, keepdims=True)


def attend_kernel(heads, prompt_dev, prompt_total, meta_ref, q_ref, k_ref, v_ref, out_ref):
    mask = read_mask(meta_ref, q_ref.shape[0], k_ref.shape[0], prompt_dev, prompt_total)
    head = q_ref.shape[1] // heads
    for h in range(heads):
        at = slice(h * head, (h + 1) * head)
        weights = head_probs(q_ref[:, at], k_ref[:, at], mask).astype(BF16)
        out_ref[:, at] = dot(weights, v_ref[:, at]).astype(BF16)


def attend_back_kernel(
    heads, prompt_dev, prompt_total, meta_ref, q_ref, k_ref, v_ref, d_ref, dq_ref, dk_ref, dv_ref
):
    mask = read_mask(meta_ref, q_ref.shape[0], k_ref.shape[0], prompt_dev, prompt_total)
    head = q_ref.shape[1] // heads
    for h in range(heads):
        at = slice(h * head, (h + 1) * head)
        query, key, grad = q_ref[:, at], k_ref[:, at], d_ref[:, at]
        probs = head_probs(query, key, mask)
        d_probs = dot(grad, v_ref[:, at], NT)
        centre = jnp.sum(probs * d_probs, axis=-1, keepdims=True)
        d_scores = (probs * (d_probs - centre) * head**-0.5).astype(BF16)
        dq_ref[:, at] = dot(d_scores, key)
        dk_ref[:, at] = dot(d_scores, query, TN)
        dv_ref[:, at] = dot(probs.astype(BF16), grad, TN)


def attention_call(kernel, name, arrays, outs, meta, prompt_dev, prompt_total):
    width = arrays[0].shape[1]
    heads = 4
    spec = lambda a: pl.BlockSpec((a.shape[0], width * heads // HEADS), lambda i, m: (0, i))
    return pl.pallas_call(
        functools.partial(kernel, heads, prompt_dev, prompt_total),
        grid_spec=pltpu.PrefetchScalarGridSpec(
            num_scalar_prefetch=1,
            grid=(HEADS // heads,),
            in_specs=[spec(a) for a in arrays],
            out_specs=[spec(a) for a in outs],
        ),
        out_shape=outs,
        compiler_params=pltpu.CompilerParams(vmem_limit_bytes=VMEM_LIMIT),
        name=name,
    )(meta, *arrays)


def shards(
    prompt_in,
    cont_in,
    prompt_cot,
    cont_cot,
    prompt_routes,
    cont_routes,
    prefix,
    attn_gain,
    query_gain,
    key_gain,
    ffn_gain,
    w_query,
    w_key,
    w_value,
    w_output,
    w_router,
    expert_gate,
    expert_up,
    expert_down,
):
    prompt_dev, width = prompt_in.shape[1:]
    cont_len = cont_in.shape[2]
    tokens = prompt_dev + cont_len
    head_dim = width // HEADS
    top_count = prompt_routes.shape[2]
    expert_count = w_router.shape[1]
    hidden = expert_gate.shape[1]
    planes = lax.axis_size("context")
    me = lax.axis_index("context")
    rows_e, rows_d = lax.axis_size("expert"), lax.axis_size("dp")
    owners = rows_e * rows_d
    my_expert = lax.axis_index("expert") * rows_d + lax.axis_index("dp")
    prompt_total = prompt_dev * planes
    most_prompt = 9 * prompt_dev * top_count // (8 * expert_count)
    most_cont = 9 * cont_len * top_count // (8 * expert_count)
    slots = (most_prompt + most_cont + 15) // 16 * 16
    part = width // planes
    out_group = width // (rows_e * planes)

    def shift(value, r):
        return lax.ppermute(value, "context", [(i, (i + r) % planes) for i in range(planes)])

    def block(value, r):
        return lax.dynamic_slice_in_dim(value, ((me + r) % planes) * part, part, axis=1)

    def out_part(value, r):
        at = ((me + r) % planes) * out_group
        return jnp.concatenate(
            [
                lax.dynamic_slice_in_dim(value, e * planes * out_group + at, out_group, axis=1)
                for e in range(rows_e)
            ],
            axis=1,
        )

    def placed(blocks):
        full = jnp.zeros((tokens, width), blocks[0].dtype)
        for r, piece in enumerate(blocks):
            full = lax.dynamic_update_slice_in_dim(full, piece, ((me + r) % planes) * part, axis=1)
        return full

    others = range(1, planes)

    x_low = jnp.concatenate([prompt_in[0], cont_in[0, 0]], axis=0)
    x_rows = x_low.astype(F32)
    inverse = lax.rsqrt(jnp.mean(x_rows * x_rows, axis=-1) + EPSILON)
    x_blocks = [block(x_low, 0)] + [shift(block(x_low, r), r) for r in others]
    inverses = [inverse] + [shift(inverse, r) for r in others]
    gain_part = attn_gain.astype(F32)
    normed_blocks = [
        (piece.astype(F32) * inv[:, None] * gain_part).astype(BF16)
        for piece, inv in zip(x_blocks, inverses)
    ]

    small = jnp.concatenate(
        [jnp.stack([attn_gain, query_gain, key_gain, ffn_gain], axis=1), w_router], axis=1
    )
    small = lax.all_gather(small, "context", axis=0, tiled=True)
    gains = small[:, :4].T.astype(F32)
    gain_attn, gain_query, gain_key, gain_ffn = [gains[i : i + 1] for i in range(4)]
    full_router = small[:, 4:]

    d_out_low = jnp.concatenate([prompt_cot[0], cont_cot[0, 0]], axis=0)
    routes = jnp.concatenate([prompt_routes[0], cont_routes[0, 0]], axis=0)
    all_routes = lax.all_gather(routes, PLANE, axis=0, tiled=True)
    all_cot = lax.all_gather(d_out_low, PLANE, axis=0, tiled=True)

    start_len = prefix[0, 0]
    prompt_pos = me * prompt_dev + jnp.arange(prompt_dev, dtype=jnp.int32)
    positions = jnp.concatenate([prompt_pos, start_len + jnp.arange(cont_len, dtype=jnp.int32)])
    half_index = jnp.arange(head_dim // 2, dtype=F32)
    angles = positions.astype(F32)[:, None] * (10000.0 ** (-2.0 * half_index / head_dim))[None, :]
    cosine = jnp.cos(angles)
    sine = jnp.sin(angles)
    cosine = jnp.concatenate([cosine, cosine], axis=1)
    sine = jnp.concatenate([-sine, sine], axis=1)
    meta = jnp.stack([me * prompt_dev, start_len]).astype(jnp.int32)

    def project(pieces, weight):
        sent = [shift(dot(pieces[r], weight).astype(BF16), planes - r) for r in others]
        return [dot(pieces[0], weight)] + sent

    key_parts = project(normed_blocks, w_key)
    value_parts = project(normed_blocks, w_value)
    query_parts = project(normed_blocks, w_query)
    key_raw, key_low = qk_post(key_parts, gain_key, cosine, sine)
    value_low = sum(p.astype(F32) for p in value_parts).astype(BF16)
    query_raw, query_low = qk_post(query_parts, gain_query, cosine, sine)

    def with_prompt(rows):
        full = jnp.zeros((prompt_total + cont_len, width), BF16)
        full = lax.dynamic_update_slice_in_dim(full, rows[prompt_dev:], prompt_total, axis=0)
        for r in range(planes):
            piece = rows[:prompt_dev]
            if r:
                piece = shift(piece, planes - r)
            full = lax.dynamic_update_slice_in_dim(
                full, piece, ((me + r) % planes) * prompt_dev, axis=0
            )
        return full

    key_set = with_prompt(key_low)
    value_set = with_prompt(value_low)
    (attended,) = attention_call(
        attend_kernel,
        "attend",
        [query_low, key_set, value_set],
        [jax.ShapeDtypeStruct((tokens, width), BF16)],
        meta,
        prompt_dev,
        prompt_total,
    )

    attended_blocks = [block(attended, 0)] + [shift(block(attended, r), r) for r in others]
    mixed_rows = x_rows + sum(p.astype(F32) for p in project(attended_blocks, w_output))
    inverse2 = lax.rsqrt(jnp.mean(mixed_rows * mixed_rows, axis=-1, keepdims=True) + EPSILON)
    normed2_low = (mixed_rows * inverse2 * gain_ffn).astype(BF16)

    all_normed2 = lax.all_gather(normed2_low, PLANE, axis=0, tiled=True)

    normed_low = (x_rows * inverse[:, None] * gain_attn).astype(BF16)
    normed_out = jnp.concatenate(
        [out_part(normed_low, 0)] + [shift(out_part(normed_low, r), r) for r in others], axis=0
    )
    attended_out = jnp.concatenate(
        [out_part(attended, 0)] + [shift(out_part(attended, r), r) for r in others], axis=0
    )

    logits = dot(normed2_low, full_router)
    shifted = jnp.exp(logits - jnp.max(logits, axis=1, keepdims=True))
    router_probs = shifted / jnp.sum(shifted, axis=1, keepdims=True)

    member = jnp.sum((all_routes == my_expert).astype(F32), axis=1).reshape(owners, tokens)

    def ranks(m):
        count = m.shape[1]
        before = jnp.triu(jnp.ones((count, count), BF16), 1)
        return dot(m.astype(BF16), before)

    slot_of = jnp.concatenate(
        [ranks(member[:, :prompt_dev]), ranks(member[:, prompt_dev:]) + most_prompt], axis=1
    )
    slot_of = jnp.where(member > 0, slot_of, -1.0)
    pick = (
        slot_of[:, None, :] == jnp.arange(slots, dtype=F32)[None, :, None]
    ).astype(BF16)

    def gather_rows(values):
        picked = jnp.einsum(
            "sjt,std->sjd",
            pick,
            values.reshape(owners, tokens, width),
            preferred_element_type=BF16,
        )
        return picked.reshape(owners * slots, width)

    def spread_rows(values):
        return jnp.einsum(
            "sjt,sjd->std",
            pick,
            values.reshape(owners, slots, width),
            preferred_element_type=BF16,
        ).reshape(owners * tokens, width)

    gate_w, up_w, down_w = expert_gate[0], expert_up[0], expert_down[0]
    slot_cot = gather_rows(all_cot)
    d_act_plain = dot(slot_cot, down_w, NT)

    slot_in = gather_rows(all_normed2)
    slot_logits = dot(slot_in, full_router)
    slot_exp = jnp.exp(slot_logits - jnp.max(slot_logits, axis=1, keepdims=True))
    is_mine = jnp.arange(expert_count, dtype=jnp.int32) == my_expert
    slot_gate = jnp.sum(jnp.where(is_mine, slot_exp, 0.0), axis=1, keepdims=True) / jnp.sum(
        slot_exp, axis=1, keepdims=True
    )
    gate_pre = dot(slot_in, gate_w, NT)
    up_pre = dot(slot_in, up_w, NT)
    sigmoid = jax.nn.sigmoid(gate_pre)
    silu = gate_pre * sigmoid
    act_low = (silu * up_pre).astype(BF16)
    d_act = slot_gate * d_act_plain
    d_gate = (d_act * up_pre * (sigmoid * (1.0 + gate_pre * (1.0 - sigmoid)))).astype(BF16)
    d_up = (d_act * silu).astype(BF16)
    slot_dprob = jnp.sum(act_low.astype(F32) * d_act_plain, axis=1).reshape(owners, slots)
    token_dprob = jnp.sum(pick.astype(F32) * slot_dprob[:, :, None], axis=1)
    dprobs = lax.all_to_all(token_dprob, PLANE, split_axis=0, concat_axis=0, tiled=True).T
    d_input = (dot(d_gate, gate_w) + dot(d_up, up_w)).astype(BF16)
    d_normed2_moe = lax.psum_scatter(
        spread_rows(d_input), PLANE, scatter_dimension=0, tiled=True
    ).astype(F32)

    slot_dy = (slot_gate * slot_cot.astype(F32)).astype(BF16)
    piece = hidden // planes

    def expert_grad(left, right):
        def rows(r):
            cols = lax.dynamic_slice_in_dim(left, ((me + r) % planes) * piece, piece, axis=1)
            return dot(cols, right, TN)

        sent = [shift(rows(r).astype(BF16), r) for r in others]
        return rows(0) + sum(s.astype(F32) for s in sent)

    gate_grad = expert_grad(d_gate, slot_in)
    up_grad = expert_grad(d_up, slot_in)
    down_grad = expert_grad(act_low, slot_dy)

    slot_out = (slot_gate * dot(act_low, down_w)).astype(BF16)
    moe_out = lax.psum_scatter(
        spread_rows(slot_out), PLANE, scatter_dimension=0, tiled=True
    ).astype(F32)
    out_rows = mixed_rows + moe_out

    d_out = d_out_low.astype(F32)
    dlogit_low = (
        router_probs * (dprobs - jnp.sum(router_probs * dprobs, axis=1, keepdims=True))
    ).astype(BF16)
    router_grad = dot(normed2_low, dlogit_low, TN)
    d_normed2 = d_normed2_moe + dot(dlogit_low, full_router, NT)
    scaled2 = gain_ffn * d_normed2
    centre2 = jnp.mean(scaled2 * mixed_rows, axis=-1, keepdims=True)
    d_mixed = d_out + inverse2 * scaled2 - mixed_rows * (inverse2**3 * centre2)
    ffn_gain_grad = jnp.sum(d_normed2 * mixed_rows * inverse2, axis=0)

    branch_low = d_mixed.astype(BF16)
    branches = [branch_low] + [shift(branch_low, r) for r in others]

    def back_blocks(pairs_of):
        sent = [shift(pairs_of(r).astype(BF16), planes - r) for r in others]
        return [pairs_of(0)] + sent

    d_attended = placed(
        [p.astype(BF16) for p in back_blocks(lambda r: dot(branches[r], w_output, NT))]
    )
    output_grad = dot(attended_out, jnp.concatenate(branches, axis=0), TN).astype(BF16)

    key_total = prompt_total + cont_len
    d_queries, d_keys_all, d_values_all = attention_call(
        attend_back_kernel,
        "attend_back",
        [query_low, key_set, value_set, d_attended],
        [
            jax.ShapeDtypeStruct((tokens, width), F32),
            jax.ShapeDtypeStruct((key_total, width), F32),
            jax.ShapeDtypeStruct((key_total, width), F32),
        ],
        meta,
        prompt_dev,
        prompt_total,
    )

    def own_keys(rows):
        def prompt_rows(r):
            return lax.dynamic_slice_in_dim(
                rows, ((me + r) % planes) * prompt_dev, prompt_dev, axis=0
            )

        total = prompt_rows(0)
        for r in others:
            total = total + shift(prompt_rows(r).astype(BF16), r).astype(F32)
        return jnp.concatenate([total, rows[prompt_total:]], axis=0)

    d_value_low = own_keys(d_values_all).astype(BF16)
    d_query_low, query_gain_grad = qk_post_back(d_queries, query_raw, gain_query, cosine, sine)
    d_key_low, key_gain_grad = qk_post_back(
        own_keys(d_keys_all), key_raw, gain_key, cosine, sine
    )

    def spread(low):
        return [low] + [shift(low, r) for r in others]

    d_values, d_query_rows, d_key_rows = spread(d_value_low), spread(d_query_low), spread(d_key_low)
    d_normed = placed(
        [
            p.astype(F32)
            for p in back_blocks(
                lambda r: dot(d_values[r], w_value, NT)
                + dot(d_query_rows[r], w_query, NT)
                + dot(d_key_rows[r], w_key, NT)
            )
        ]
    )
    value_grad = dot(normed_out, jnp.concatenate(d_values, axis=0), TN).astype(BF16)
    query_grad = dot(normed_out, jnp.concatenate(d_query_rows, axis=0), TN).astype(BF16)
    key_grad = dot(normed_out, jnp.concatenate(d_key_rows, axis=0), TN).astype(BF16)

    scaled = gain_attn * d_normed
    centre = jnp.mean(scaled * x_rows, axis=-1, keepdims=True)
    inv = inverse[:, None]
    d_x = d_mixed + inv * scaled - x_rows * (inv**3 * centre)
    attn_gain_grad = jnp.sum(d_normed * x_rows * inv, axis=0)

    def scatter(value):
        return lax.psum_scatter(value, PLANE, scatter_dimension=0, tiled=True).astype(F32)

    everywhere = ("expert", "context", "dp")
    small_grads = jnp.concatenate(
        [
            jnp.stack([attn_gain_grad, query_gain_grad[0], key_gain_grad[0], ffn_gain_grad], axis=1),
            router_grad,
        ],
        axis=1,
    )
    small_grads = lax.psum_scatter(small_grads, everywhere, scatter_dimension=0, tiled=True)
    return (
        out_rows[:prompt_dev].astype(BF16)[None],
        out_rows[prompt_dev:].astype(BF16)[None, None],
        d_x[:prompt_dev][None],
        d_x[prompt_dev:][None, None],
        small_grads[:, 0],
        small_grads[:, 1],
        small_grads[:, 2],
        small_grads[:, 3],
        scatter(query_grad),
        scatter(key_grad),
        scatter(value_grad),
        scatter(output_grad),
        small_grads[:, 4:],
        gate_grad[None],
        up_grad[None],
        down_grad[None],
    )


def solution(mesh):
    rows = P(("expert", "dp"), "context", None)
    conts = P(("expert", "dp"), "context", None, None)
    experts = P(("expert", "dp"), None, None)
    everywhere = ("expert", "context", "dp")
    in_specs = (
        (rows, conts, rows, conts, rows, conts, P(("expert", "dp"), "context"))
        + (P("context"),) * 4
        + (P("context", None),) * 5
        + (experts,) * 3
    )
    out_specs = (
        (rows, conts, rows, conts)
        + (P(everywhere),) * 4
        + (P(everywhere, None),) * 5
        + (rows,) * 3
    )
    return jax.shard_map(shards, mesh=mesh, in_specs=in_specs, out_specs=out_specs, check_vma=False)
```

```python
import functools

import jax
import jax.numpy as jnp
from jax import lax
from jax.experimental import pallas as pl
from jax.experimental.pallas import tpu as pltpu
from jax.sharding import PartitionSpec as P

HEADS = 16
EPSILON = 1e-05
NEG_LARGE = -1e30
F32 = jnp.float32
BF16 = jnp.bfloat16
PLANE = ("expert", "dp")
VMEM_LIMIT = 48 * 1024 * 1024


def dot(left, right, dims=((1,), (0,)), out=F32):
    return lax.dot_general(left, right, (dims, ((), ())), preferred_element_type=out)


NT = ((1,), (1,))
TN = ((0,), (0,))


def post_kernel(count, *refs):
    parts, (gain_ref, cos_ref, sin_ref, raw_ref, low_ref) = refs[:count], refs[count:]
    raw = parts[0][...]
    for part in parts[1:]:
        raw = raw + part[...].astype(F32)
    raw_ref[...] = raw
    inverse = lax.rsqrt(jnp.mean(raw * raw, axis=-1, keepdims=True) + EPSILON)
    scaled = raw * inverse * gain_ref[...]
    cosine, sine = cos_ref[...], sin_ref[...]
    head = cosine.shape[1]
    for h in range(raw.shape[1] // head):
        piece = scaled[:, h * head : (h + 1) * head]
        turned = piece * cosine + pltpu.roll(piece, head // 2, 1) * sine
        low_ref[:, h * head : (h + 1) * head] = turned.astype(BF16)


def qk_post(parts, gain, cosine, sine):
    rows, width = parts[0].shape
    head = cosine.shape[1]
    step = 64
    row = lambda w: pl.BlockSpec((step, w), lambda i: (i, 0))
    return pl.pallas_call(
        functools.partial(post_kernel, len(parts)),
        grid=(rows // step,),
        in_specs=[row(width)] * len(parts)
        + [pl.BlockSpec((1, width), lambda i: (0, 0)), row(head), row(head)],
        out_specs=[row(width), row(width)],
        out_shape=[
            jax.ShapeDtypeStruct((rows, width), F32),
            jax.ShapeDtypeStruct((rows, width), BF16),
        ],
        compiler_params=pltpu.CompilerParams(vmem_limit_bytes=VMEM_LIMIT),
        name="qk_post",
    )(*parts, gain, cosine, sine)


def post_back_kernel(grad_ref, raw_ref, gain_ref, cos_ref, sin_ref, low_ref, gain_grad_ref):
    raw = raw_ref[...]
    inverse = lax.rsqrt(jnp.mean(raw * raw, axis=-1, keepdims=True) + EPSILON)
    cosine, sine = cos_ref[...], sin_ref[...]
    head = cosine.shape[1]
    pieces = []
    for h in range(raw.shape[1] // head):
        piece = grad_ref[:, h * head : (h + 1) * head]
        pieces.append(piece * cosine - pltpu.roll(piece, head // 2, 1) * sine)
    grad = jnp.concatenate(pieces, axis=1)
    scaled = grad * gain_ref[...]
    centre = jnp.mean(scaled * raw, axis=-1, keepdims=True)
    low_ref[...] = (inverse * scaled - raw * (inverse * inverse * inverse * centre)).astype(BF16)
    total = jnp.sum(grad * raw * inverse, axis=0, keepdims=True)

    @pl.when(pl.program_id(0) == 0)
    def _():
        gain_grad_ref[...] = total

    @pl.when(pl.program_id(0) > 0)
    def _():
        gain_grad_ref[...] += total


def qk_post_back(grad, raw, gain, cosine, sine):
    rows, width = raw.shape
    head = cosine.shape[1]
    step = 64
    row = lambda w: pl.BlockSpec((step, w), lambda i: (i, 0))
    whole = pl.BlockSpec((1, width), lambda i: (0, 0))
    return pl.pallas_call(
        post_back_kernel,
        grid=(rows // step,),
        in_specs=[row(width), row(width), whole, row(head), row(head)],
        out_specs=[row(width), whole],
        out_shape=[
            jax.ShapeDtypeStruct((rows, width), BF16),
            jax.ShapeDtypeStruct((1, width), F32),
        ],
        compiler_params=pltpu.CompilerParams(vmem_limit_bytes=VMEM_LIMIT),
        name="qk_post_back",
    )(grad, raw, gain, cosine, sine)


def read_mask(meta_ref, rows, keys, prompt_dev, prompt_total):
    row = lax.broadcasted_iota(jnp.int32, (rows, keys), 0)
    key = lax.broadcasted_iota(jnp.int32, (rows, keys), 1)
    is_prompt_row = row < prompt_dev
    is_prompt_key = key < prompt_total
    prompt_limit = jnp.where(is_prompt_row, meta_ref[0] + row + 1, meta_ref[1])
    own_limit = jnp.where(is_prompt_row, 0, row - prompt_dev + 1)
    limit = jnp.where(is_prompt_key, prompt_limit, own_limit + prompt_total)
    return key < limit


def head_probs(query, key, mask):
    scores = jnp.where(mask, dot(query, key, NT) * (query.shape[1] ** -0.5), NEG_LARGE)
    exponent = jnp.exp(scores - jnp.max(scores, axis=-1, keepdims=True))
    return exponent / jnp.sum(exponent, axis=-1, keepdims=True)


def attend_kernel(heads, prompt_dev, prompt_total, meta_ref, q_ref, k_ref, v_ref, out_ref):
    mask = read_mask(meta_ref, q_ref.shape[0], k_ref.shape[0], prompt_dev, prompt_total)
    head = q_ref.shape[1] // heads
    for h in range(heads):
        at = slice(h * head, (h + 1) * head)
        weights = head_probs(q_ref[:, at], k_ref[:, at], mask).astype(BF16)
        out_ref[:, at] = dot(weights, v_ref[:, at]).astype(BF16)


def attend_back_kernel(
    heads, prompt_dev, prompt_total, meta_ref, q_ref, k_ref, v_ref, d_ref, dq_ref, dk_ref, dv_ref
):
    mask = read_mask(meta_ref, q_ref.shape[0], k_ref.shape[0], prompt_dev, prompt_total)
    head = q_ref.shape[1] // heads
    for h in range(heads):
        at = slice(h * head, (h + 1) * head)
        query, key, grad = q_ref[:, at], k_ref[:, at], d_ref[:, at]
        probs = head_probs(query, key, mask)
        d_probs = dot(grad, v_ref[:, at], NT)
        centre = jnp.sum(probs * d_probs, axis=-1, keepdims=True)
        d_scores = (probs * (d_probs - centre) * head**-0.5).astype(BF16)
        dq_ref[:, at] = dot(d_scores, key)
        dk_ref[:, at] = dot(d_scores, query, TN)
        dv_ref[:, at] = dot(probs.astype(BF16), grad, TN)


def attention_call(kernel, name, arrays, outs, meta, prompt_dev, prompt_total):
    width = arrays[0].shape[1]
    heads = 4
    spec = lambda a: pl.BlockSpec((a.shape[0], width * heads // HEADS), lambda i, m: (0, i))
    return pl.pallas_call(
        functools.partial(kernel, heads, prompt_dev, prompt_total),
        grid_spec=pltpu.PrefetchScalarGridSpec(
            num_scalar_prefetch=1,
            grid=(HEADS // heads,),
            in_specs=[spec(a) for a in arrays],
            out_specs=[spec(a) for a in outs],
        ),
        out_shape=outs,
        compiler_params=pltpu.CompilerParams(vmem_limit_bytes=VMEM_LIMIT),
        name=name,
    )(meta, *arrays)


def expert_kernel(*refs):
    refs = refs[:10] + refs[-10:]
    (
        x0_ref, x1_ref, x2_ref, x3_ref, pick_ref, plain_ref, gate_w_ref, up_w_ref, router_ref, mine_ref,
        in_ref, act_ref, dg_ref, du_ref, prob_ref,
        keep_ref, send_ref, dprob_ref,
        total_ref, dp_ref,
    ) = refs
    step = pl.program_id(0)
    slots = pick_ref.shape[1]

    @pl.when(step == 0)
    def _():
        for s, x_ref in enumerate((x0_ref, x1_ref, x2_ref, x3_ref)):
            in_ref[s * slots : (s + 1) * slots, :] = dot(pick_ref[s], x_ref[...]).astype(BF16)
        logits = dot(in_ref[...], router_ref[...])
        exponent = jnp.exp(logits - jnp.max(logits, axis=1, keepdims=True))
        total = jnp.sum(exponent, axis=1, keepdims=True)
        prob_ref[...] = jnp.sum(exponent * mine_ref[...], axis=1, keepdims=True) / total

    rows = in_ref[...]
    gate_w, up_w = gate_w_ref[...], up_w_ref[...]
    gate_pre = dot(rows, gate_w, NT)
    up_pre = dot(rows, up_w, NT)
    plain = plain_ref[...]
    sigmoid = 1.0 / (1.0 + jnp.exp(-gate_pre))
    silu = gate_pre * sigmoid
    act = (silu * up_pre).astype(BF16)
    act_ref[...] = act
    d_act = prob_ref[...] * plain
    d_gate = (d_act * up_pre * (sigmoid * (1.0 + gate_pre * (1.0 - sigmoid)))).astype(BF16)
    d_up = (d_act * silu).astype(BF16)
    dg_ref[...] = d_gate
    du_ref[...] = d_up
    d_prob = jnp.sum(act.astype(F32) * plain, axis=1, keepdims=True)
    d_in = dot(d_gate, gate_w) + dot(d_up, up_w)

    @pl.when(step == 0)
    def _():
        dp_ref[...] = d_prob
        total_ref[...] = d_in

    @pl.when(step > 0)
    def _():
        dp_ref[...] += d_prob
        total_ref[...] += d_in

    @pl.when(step == pl.num_programs(0) - 1)
    def _():
        values = total_ref[...].astype(BF16)
        for s in range(4):
            at = slice(s * slots, (s + 1) * slots)
            (keep_ref, send_ref)[s % 2][s // 2] = dot(pick_ref[s], values[at, :], TN).astype(BF16)
            dprob_ref[s : s + 1, :] = jnp.sum(
                pick_ref[s].astype(F32) * dp_ref[at, :], axis=0, keepdims=True
            )


def expert_quarter(quarter, blocks, pick, plain, gate_w, up_w, router, mine, kept):
    tokens, width = blocks[0].shape
    hidden = gate_w.shape[0]
    tile = 256
    slots = pick.shape[1]
    rows = 4 * slots
    whole = lambda *shape: pl.BlockSpec(shape, lambda f: (0,) * len(shape))
    any_spec = pl.BlockSpec(memory_space=pl.ANY)
    pair = jax.ShapeDtypeStruct((2, tokens, width), BF16)
    tiled = pl.BlockSpec((rows, tile), lambda f: (quarter, f))
    every = pick.shape[0] * slots
    return pl.pallas_call(
        expert_kernel,
        grid=(hidden // tile,),
        in_specs=[whole(tokens, width)] * 4
        + [
            pl.BlockSpec((4, slots, tokens), lambda f: (quarter, 0, 0)),
            tiled,
            pl.BlockSpec((tile, width), lambda f: (f, 0)),
            pl.BlockSpec((tile, width), lambda f: (f, 0)),
            whole(*router.shape),
            whole(*mine.shape),
        ]
        + [any_spec] * len(kept),
        out_specs=[
            pl.BlockSpec((rows, width), lambda f: (quarter, 0)),
            tiled,
            tiled,
            tiled,
            pl.BlockSpec((rows, 1), lambda f: (quarter, 0)),
        ]
        + [whole(2, tokens, width)] * 2
        + [whole(4, tokens)],
        out_shape=[
            jax.ShapeDtypeStruct((every, width), BF16),
            jax.ShapeDtypeStruct((every, hidden), BF16),
            jax.ShapeDtypeStruct((every, hidden), BF16),
            jax.ShapeDtypeStruct((every, hidden), BF16),
            jax.ShapeDtypeStruct((every, 1), F32),
            pair,
            pair,
            jax.ShapeDtypeStruct((4, tokens), F32),
        ],
        scratch_shapes=[pltpu.VMEM((rows, width), F32), pltpu.VMEM((rows, 1), F32)],
        input_output_aliases={10 + k: k for k in range(len(kept))},
        compiler_params=pltpu.CompilerParams(vmem_limit_bytes=VMEM_LIMIT),
        name="expert",
    )(*blocks, pick, plain, gate_w, up_w, router, mine, *kept)


def expert_out_kernel(source_ref, pick_ref, act_ref, down_ref, prob_ref, out_ref, values_ref):
    s = pl.program_id(1)

    @pl.when(s == 0)
    def _():
        values = (prob_ref[...] * dot(act_ref[...], down_ref[...])).astype(BF16)
        values_ref[...] = values.reshape(values_ref.shape)

    out_ref[0] = dot(pick_ref[0], values_ref[s], TN).astype(BF16)


def expert_out(source, pick, act, down_w, prob):
    hidden, width = down_w.shape
    owners, slots, tokens = pick.shape
    rows = 4 * slots
    return pl.pallas_call(
        expert_out_kernel,
        grid_spec=pltpu.PrefetchScalarGridSpec(
            num_scalar_prefetch=1,
            grid=(owners // 4, 4),
            in_specs=[
                pl.BlockSpec((1, slots, tokens), lambda q, s, m: (4 * q + s, 0, 0)),
                pl.BlockSpec((rows, hidden), lambda q, s, m: (q, 0)),
                pl.BlockSpec((hidden, width), lambda q, s, m: (0, 0)),
                pl.BlockSpec((rows, 1), lambda q, s, m: (q, 0)),
            ],
            out_specs=pl.BlockSpec((1, tokens, width), lambda q, s, m: (m[4 * q + s], 0, 0)),
            scratch_shapes=[pltpu.VMEM((4, slots, width), BF16)],
        ),
        out_shape=jax.ShapeDtypeStruct((owners, tokens, width), BF16),
        compiler_params=pltpu.CompilerParams(vmem_limit_bytes=VMEM_LIMIT),
        name="expert_out",
    )(source, pick, act, down_w, prob)


def swap(value, axis, bit):
    return lax.ppermute(value, axis, [(i, i ^ bit) for i in range(lax.axis_size(axis))])


def plus(*values):
    return sum(v.astype(F32) for v in values).astype(values[0].dtype)


ORDER = [
    (i, j) for x in (0, 2) for z in (0, 2) for i in (z, z + 1) for j in (x, x + 1)
]


def fence(*values):
    return lax.optimization_barrier(values)


def split(value, axis_name, bit, at):
    mine = (lax.axis_index(axis_name) // bit) % 2
    shape = value.shape
    pairs = value.reshape(shape[:at] + (shape[at] // 2, 2) + shape[at + 1 :])
    keep = lax.dynamic_index_in_dim(pairs, mine, at + 1, keepdims=False)
    send = lax.dynamic_index_in_dim(pairs, 1 - mine, at + 1, keepdims=False)
    return keep, send


STAGES = (("dp", 1, 1), ("dp", 2, 1), ("expert", 1, 0), ("expert", 2, 0))


class RowScatter:
    def __init__(self, value):
        rows_e, rows_d = lax.axis_size("expert"), lax.axis_size("dp")
        self.value = value.reshape((rows_e, rows_d, -1, value.shape[-1]))
        self.stage = 0

    def start(self):
        axis, bit, at = STAGES[self.stage]
        self.keep, send = split(self.value, axis, bit, at)
        self.stage += 1
        return swap(send, axis, bit)

    def finish(self, received):
        self.value = plus(self.keep, received)

    def result(self):
        return self.value.reshape(self.value.shape[-2:])


def shards(
    prompt_in,
    cont_in,
    prompt_cot,
    cont_cot,
    prompt_routes,
    cont_routes,
    prefix,
    attn_gain,
    query_gain,
    key_gain,
    ffn_gain,
    w_query,
    w_key,
    w_value,
    w_output,
    w_router,
    expert_gate,
    expert_up,
    expert_down,
):
    prompt_dev, width = prompt_in.shape[1:]
    cont_len = cont_in.shape[2]
    tokens = prompt_dev + cont_len
    head_dim = width // HEADS
    top_count = prompt_routes.shape[2]
    expert_count = w_router.shape[1]
    hidden = expert_gate.shape[1]
    planes = lax.axis_size("context")
    me = lax.axis_index("context")
    rows_e, rows_d = lax.axis_size("expert"), lax.axis_size("dp")
    owners = rows_e * rows_d
    my_expert = lax.axis_index("expert") * rows_d + lax.axis_index("dp")
    prompt_total = prompt_dev * planes
    most_prompt = 9 * prompt_dev * top_count // (8 * expert_count)
    most_cont = 9 * cont_len * top_count // (8 * expert_count)
    slots = (most_prompt + most_cont + 15) // 16 * 16
    part = width // planes
    out_group = width // (rows_e * planes)

    def shift(value, r):
        return lax.ppermute(value, "context", [(i, (i + r) % planes) for i in range(planes)])

    def block(value, r):
        return lax.dynamic_slice_in_dim(value, ((me + r) % planes) * part, part, axis=1)

    def out_part(value, r):
        at = ((me + r) % planes) * out_group
        return jnp.concatenate(
            [
                lax.dynamic_slice_in_dim(value, e * planes * out_group + at, out_group, axis=1)
                for e in range(rows_e)
            ],
            axis=1,
        )

    def placed(blocks):
        full = jnp.zeros((tokens, width), blocks[0].dtype)
        for r, piece in enumerate(blocks):
            full = lax.dynamic_update_slice_in_dim(full, piece, ((me + r) % planes) * part, axis=1)
        return full

    others = range(1, planes)

    x_low = jnp.concatenate([prompt_in[0], cont_in[0, 0]], axis=0)
    x_rows = x_low.astype(F32)
    inverse = lax.rsqrt(jnp.mean(x_rows * x_rows, axis=-1) + EPSILON)
    x_blocks = [block(x_low, 0)] + [shift(block(x_low, r), r) for r in others]
    inverses = [inverse] + [shift(inverse, r) for r in others]
    gain_part = attn_gain.astype(F32)
    normed_blocks = [
        (piece.astype(F32) * inv[:, None] * gain_part).astype(BF16)
        for piece, inv in zip(x_blocks, inverses)
    ]

    def gathered(value, axis):
        shape = list(value.shape)
        shape[axis] = shape[axis] * planes
        full = jnp.zeros(shape, value.dtype)
        for r in range(planes):
            piece = shift(value, r) if r else value
            at = ((me - r) % planes) * value.shape[axis]
            full = lax.dynamic_update_slice_in_dim(full, piece, at, axis=axis)
        return full

    gains = gathered(jnp.stack([attn_gain, query_gain, key_gain, ffn_gain]), 1).astype(F32)
    gain_attn, gain_query, gain_key, gain_ffn = [gains[i : i + 1] for i in range(4)]
    full_router = gathered(w_router, 0)

    d_out_low = jnp.concatenate([prompt_cot[0], cont_cot[0, 0]], axis=0)
    routes = jnp.concatenate([prompt_routes[0], cont_routes[0, 0]], axis=0)
    named = sum(
        (routes[:, k : k + 1] == jnp.arange(expert_count, dtype=jnp.int32)[None, :]).astype(F32)
        for k in range(top_count)
    )
    member = lax.all_to_all(named.T, PLANE, split_axis=0, concat_axis=0, tiled=True)
    all_cot = lax.all_gather(d_out_low, PLANE, axis=0, tiled=True)

    start_len = prefix[0, 0]
    prompt_pos = me * prompt_dev + jnp.arange(prompt_dev, dtype=jnp.int32)
    positions = jnp.concatenate([prompt_pos, start_len + jnp.arange(cont_len, dtype=jnp.int32)])
    half_index = jnp.arange(head_dim // 2, dtype=F32)
    angles = positions.astype(F32)[:, None] * (10000.0 ** (-2.0 * half_index / head_dim))[None, :]
    cosine = jnp.cos(angles)
    sine = jnp.sin(angles)
    cosine = jnp.concatenate([cosine, cosine], axis=1)
    sine = jnp.concatenate([-sine, sine], axis=1)
    meta = jnp.stack([me * prompt_dev, start_len]).astype(jnp.int32)

    def project(pieces, weight):
        products = [dot(pieces[r], weight).astype(BF16) for r in others]
        products = fence(pieces[0], *products)
        sent = [shift(product, planes - r) for r, product in zip(others, products[1:])]
        return [dot(products[0], weight)] + sent

    key_parts = project(normed_blocks, w_key)
    value_parts = project(normed_blocks, w_value)
    query_parts = project(normed_blocks, w_query)
    key_raw, key_low = qk_post(key_parts, gain_key, cosine, sine)
    value_low = sum(p.astype(F32) for p in value_parts).astype(BF16)
    query_raw, query_low = qk_post(query_parts, gain_query, cosine, sine)

    def with_prompt(rows):
        full = jnp.zeros((prompt_total + cont_len, width), BF16)
        full = lax.dynamic_update_slice_in_dim(full, rows[prompt_dev:], prompt_total, axis=0)
        for r in range(planes):
            piece = rows[:prompt_dev]
            if r:
                piece = shift(piece, planes - r)
            full = lax.dynamic_update_slice_in_dim(
                full, piece, ((me + r) % planes) * prompt_dev, axis=0
            )
        return full

    key_set = with_prompt(key_low)
    value_set = with_prompt(value_low)
    (attended,) = attention_call(
        attend_kernel,
        "attend",
        [query_low, key_set, value_set],
        [jax.ShapeDtypeStruct((tokens, width), BF16)],
        meta,
        prompt_dev,
        prompt_total,
    )

    attended_blocks = [block(attended, 0)] + [shift(block(attended, r), r) for r in others]
    mixed_rows = x_rows + sum(p.astype(F32) for p in project(attended_blocks, w_output))
    inverse2 = lax.rsqrt(jnp.mean(mixed_rows * mixed_rows, axis=-1, keepdims=True) + EPSILON)
    normed2_low = (mixed_rows * inverse2 * gain_ffn).astype(BF16)

    normed_low = (x_rows * inverse[:, None] * gain_attn).astype(BF16)

    logits = dot(normed2_low, full_router)
    shifted = jnp.exp(logits - jnp.max(logits, axis=1, keepdims=True))
    router_probs = shifted / jnp.sum(shifted, axis=1, keepdims=True)

    my_e, my_d = lax.axis_index("expert"), lax.axis_index("dp")
    source = jnp.stack([(my_e ^ i) * rows_d + (my_d ^ j) for i, j in ORDER]).astype(jnp.int32)
    member = jnp.take(member, source, axis=0)

    def ranks(m):
        count = m.shape[1]
        before = jnp.triu(jnp.ones((count, count), BF16), 1)
        return dot(m.astype(BF16), before)

    slot_of = jnp.concatenate(
        [ranks(member[:, :prompt_dev]), ranks(member[:, prompt_dev:]) + most_prompt], axis=1
    )
    slot_of = jnp.where(member > 0, slot_of, -1.0)
    pick = (
        slot_of[:, None, :] == jnp.arange(slots, dtype=F32)[None, :, None]
    ).astype(BF16)
    gate_w, up_w, down_w = expert_gate[0], expert_up[0], expert_down[0]
    mine = (jnp.arange(expert_count, dtype=jnp.int32) == my_expert).astype(F32)[None, :]

    def z1(v):
        return swap(v, "expert", 1)

    def z2(v):
        return swap(v, "expert", 2)

    def core(v):
        return swap(v, "dp", 1)

    def across(v):
        return swap(v, "dp", 2)

    b0, all_cot, normed_low = fence(normed2_low, all_cot, normed_low)
    b1, b2, x0, c0 = z1(b0), z2(b0), across(b0), core(b0)
    normed_sent = [shift(out_part(normed_low, r), r) for r in others]
    all_cot = all_cot.reshape(owners, tokens, width)
    slot_cot = jnp.concatenate(
        [
            dot(pick[b], lax.dynamic_index_in_dim(all_cot, source[b], 0, False), out=BF16)
            for b in range(owners)
        ],
        axis=0,
    )
    d_act_plain = dot(slot_cot, down_w, NT)
    b1, b2, x0, c0, d_act_plain, attended, *normed_sent = fence(
        b1, b2, x0, c0, d_act_plain, attended, *normed_sent
    )
    normed_out = jnp.concatenate([out_part(normed_low, 0)] + normed_sent, axis=0)
    b3, x1, c1, x0c = z1(b2), across(b1), core(b1), core(x0)
    attended_sent = [shift(out_part(attended, r), r) for r in others]
    b3, x1, c1, x0c, *attended_sent = fence(b3, x1, c1, x0c, *attended_sent)
    attended_out = jnp.concatenate([out_part(attended, 0)] + attended_sent, axis=0)

    def quarter(q, blocks, kept):
        outs = expert_quarter(q, blocks, pick, d_act_plain, gate_w, up_w, full_router, mine, kept)
        return outs[:5], outs[5], outs[6], outs[7]

    x2, c2, c3, x1c = across(b2), core(b2), core(b3), core(x1)
    kept, keep0, send0, dprob0 = quarter(0, (b0, c0, b1, c1), ())
    x2, c2, c3, x1c, *kept = fence(x2, c2, c3, x1c, *kept)
    x3, x2c = across(b3), core(x2)
    kept, keep2, send2, dprob2 = quarter(2, (x0, x0c, x1, x1c), kept)
    x3, x2c, send2, *kept = fence(x3, x2c, send2, *kept)
    x3c, near2 = core(x3), core(send2)
    x3c, near2, *kept = fence(x3c, near2, *kept)
    got2 = across(plus(keep2, near2))
    kept, keep1, send1, dprob1 = quarter(1, (b2, c2, b3, c3), kept)
    kept, keep3, send3, dprob3 = quarter(3, (x2, x2c, x3, x3c), kept)
    got2, send0, send1, send3, *kept = fence(got2, send0, send1, send3, *kept)
    slot_in, act_low, d_gate, d_up, slot_gate = kept

    piece = hidden // planes

    def grad_rows(left, right, r):
        cols = lax.dynamic_slice_in_dim(left, ((me + r) % planes) * piece, piece, axis=1)
        return dot(cols, right, TN)

    def grad_low(left, right):
        return [grad_rows(left, right, r).astype(BF16) for r in others]

    def send_rows(values, low, high):
        at = slice(piece * low // 4, piece * high // 4)
        return [shift(v[at], r) for r, v in zip(others, values)]

    near0, near1, near3 = core(send0), core(send1), core(send3)
    gate_low = grad_low(d_gate, slot_in)
    near0, near1, near3, *gate_low = fence(near0, near1, near3, *gate_low)
    first = plus(keep0, near0, got2)
    got3, first_got = across(plus(keep3, near3)), z1(first[1])
    gate_a = send_rows(gate_low, 0, 3)
    up_low = grad_low(d_up, slot_in)
    place = jnp.zeros((owners,), jnp.int32).at[source].set(jnp.arange(owners, dtype=jnp.int32))
    token_dprob = jnp.take(
        jnp.concatenate([dprob0, dprob1, dprob2, dprob3], axis=0), place, axis=0
    )
    dprobs = lax.all_to_all(token_dprob, PLANE, split_axis=0, concat_axis=0, tiled=True).T
    got3, first_got, dprobs, *rest = fence(got3, first_got, dprobs, *gate_a, *up_low)
    gate_a, up_low = rest[: planes - 1], rest[planes - 1 :]
    second = plus(keep1, near1, got3)
    second_got = z1(second[1])
    gate_b = send_rows(gate_low, 3, 4)
    up_a = send_rows(up_low, 0, 1)
    slot_dy = (slot_gate * slot_cot.astype(F32)).astype(BF16)
    down_low = grad_low(act_low, slot_dy)
    second_got, *rest = fence(second_got, *gate_b, *up_a, *down_low)
    gate_b, up_a, down_low = (rest[k * (planes - 1) : (k + 1) * (planes - 1)] for k in range(3))
    far_got = z2(plus(second[0], second_got))
    up_b = send_rows(up_low, 1, 4)
    slot_out = expert_out(source, pick, act_low, down_w, slot_gate)
    far_got, slot_out, *up_b = fence(far_got, slot_out, *up_b)
    d_normed2_moe = first[0].astype(F32) + first_got.astype(F32) + far_got.astype(F32)

    d_out = d_out_low.astype(F32)
    dlogit_low = (
        router_probs * (dprobs - jnp.sum(router_probs * dprobs, axis=1, keepdims=True))
    ).astype(BF16)
    router_grad = dot(normed2_low, dlogit_low, TN)
    d_normed2 = d_normed2_moe + dot(dlogit_low, full_router, NT)
    scaled2 = gain_ffn * d_normed2
    centre2 = jnp.mean(scaled2 * mixed_rows, axis=-1, keepdims=True)
    d_mixed = d_out + inverse2 * scaled2 - mixed_rows * (inverse2**3 * centre2)
    ffn_gain_grad = jnp.sum(d_normed2 * mixed_rows * inverse2, axis=0)

    branch_low = d_mixed.astype(BF16)
    branch_low, slot_out = fence(branch_low, slot_out)
    moe_out = lax.psum_scatter(
        slot_out.reshape(owners * tokens, width), PLANE, scatter_dimension=0, tiled=True
    ).astype(F32)
    out_rows = mixed_rows + moe_out
    branches = [branch_low] + [shift(branch_low, r) for r in others]
    gate_own = grad_rows(d_gate, slot_in, 0)
    up_own = grad_rows(d_up, slot_in, 0)
    *branches, gate_own, up_own = fence(*branches, gate_own, up_own)
    blocks_low = [dot(branches[r], w_output, NT).astype(BF16) for r in others]
    blocks_low = fence(*blocks_low)
    d_att_blocks = [dot(branches[0], w_output, NT).astype(BF16)] + [
        shift(v, planes - r) for r, v in zip(others, blocks_low)
    ]
    output_rows = RowScatter(dot(attended_out, jnp.concatenate(branches, axis=0), TN).astype(BF16))
    output_got = output_rows.start()
    output_got, *d_att_blocks = fence(output_got, *d_att_blocks)
    output_rows.finish(output_got)
    d_attended = placed(d_att_blocks)

    key_total = prompt_total + cont_len
    output_got = output_rows.start()
    d_queries, d_keys_all, d_values_all = attention_call(
        attend_back_kernel,
        "attend_back",
        [query_low, key_set, value_set, d_attended],
        [
            jax.ShapeDtypeStruct((tokens, width), F32),
            jax.ShapeDtypeStruct((key_total, width), F32),
            jax.ShapeDtypeStruct((key_total, width), F32),
        ],
        meta,
        prompt_dev,
        prompt_total,
    )

    def own_keys(rows):
        def prompt_rows(r):
            return lax.dynamic_slice_in_dim(
                rows, ((me + r) % planes) * prompt_dev, prompt_dev, axis=0
            )

        total = prompt_rows(0)
        for r in others:
            total = total + shift(prompt_rows(r).astype(BF16), r).astype(F32)
        return jnp.concatenate([total, rows[prompt_total:]], axis=0)

    d_value_low = own_keys(d_values_all).astype(BF16)
    d_query_low, query_gain_grad = qk_post_back(d_queries, query_raw, gain_query, cosine, sine)
    d_key_low, key_gain_grad = qk_post_back(
        own_keys(d_keys_all), key_raw, gain_key, cosine, sine
    )
    output_got, d_value_low, d_query_low, d_key_low = fence(
        output_got, d_value_low, d_query_low, d_key_low
    )
    output_rows.finish(output_got)

    def spread(low):
        return [shift(low, r) for r in others]

    def weight_rows(own, got):
        return RowScatter(dot(normed_out, jnp.concatenate([own, *got], axis=0), TN).astype(BF16))

    got, output_got = spread(d_value_low), output_rows.start()
    output_got, *d_values = fence(output_got, *got)
    output_rows.finish(output_got)

    value_rows = weight_rows(d_value_low, d_values)
    got, output_got, value_got = spread(d_query_low), output_rows.start(), value_rows.start()
    output_got, value_got, *d_query_got = fence(output_got, value_got, *got)
    output_rows.finish(output_got)
    value_rows.finish(value_got)

    query_rows = weight_rows(d_query_low, d_query_got)
    got, value_got, query_got = spread(d_key_low), value_rows.start(), query_rows.start()
    partial = [
        dot(d_values[k], w_value, NT) + dot(d_query_got[k], w_query, NT) for k in range(planes - 1)
    ]
    rest = fence(value_got, query_got, *got, *partial)
    value_got, query_got = rest[:2]
    d_key_got, partial = rest[2 : planes + 1], rest[planes + 1 :]
    value_rows.finish(value_got)
    query_rows.finish(query_got)

    blocks_low = [
        (partial[k] + dot(d_key_got[k], w_key, NT)).astype(BF16) for k in range(planes - 1)
    ]
    query_got, value_got = query_rows.start(), value_rows.start()
    d_normed_got = [shift(v, planes - r) for r, v in zip(others, blocks_low)]
    down_a = send_rows(down_low, 0, 1)
    key_rows = weight_rows(d_key_low, d_key_got)
    key_got = key_rows.start()
    d_normed_own = (
        dot(d_value_low, w_value, NT) + dot(d_query_low, w_query, NT) + dot(d_key_low, w_key, NT)
    )
    query_got, value_got, key_got, d_normed_own, *rest = fence(
        query_got, value_got, key_got, d_normed_own, *d_normed_got, *down_a
    )
    d_normed_got, down_a = rest[: planes - 1], rest[planes - 1 :]
    query_rows.finish(query_got)
    value_rows.finish(value_got)
    key_rows.finish(key_got)

    d_normed = placed([d_normed_own] + [p.astype(F32) for p in d_normed_got])
    key_got, query_got, value_got = key_rows.start(), query_rows.start(), value_rows.start()
    down_b = send_rows(down_low, 1, 3)
    scaled = gain_attn * d_normed
    centre = jnp.mean(scaled * x_rows, axis=-1, keepdims=True)
    inv = inverse[:, None]
    d_x = d_mixed + inv * scaled - x_rows * (inv**3 * centre)
    attn_gain_grad = jnp.sum(d_normed * x_rows * inv, axis=0)
    small_grads = jnp.concatenate(
        [
            jnp.stack([attn_gain_grad, query_gain_grad[0], key_gain_grad[0], ffn_gain_grad], axis=1),
            router_grad,
        ],
        axis=1,
    )
    by_plane = small_grads.reshape(rows_e, planes, out_group, small_grads.shape[1])

    def plane_rows(r):
        return lax.dynamic_index_in_dim(by_plane, (me + r) % planes, 1, False)

    small_rows = RowScatter(plus(plane_rows(0), *[shift(plane_rows(r), r) for r in others]))
    small_rows.finish(small_rows.start())
    key_got, query_got, value_got, small_rows.value, *down_b = fence(
        key_got, query_got, value_got, small_rows.value, *down_b
    )
    key_rows.finish(key_got)
    query_rows.finish(query_got)
    value_rows.finish(value_got)

    key_got, query_got = key_rows.start(), query_rows.start()
    small_rows.finish(small_rows.start())
    down_c = send_rows(down_low, 3, 4)
    down_own = grad_rows(act_low, slot_dy, 0)
    key_got, query_got, small_rows.value, down_own, *down_c = fence(
        key_got, query_got, small_rows.value, down_own, *down_c
    )
    key_rows.finish(key_got)
    query_rows.finish(query_got)
    key_rows.finish(key_rows.start())
    small_rows.finish(small_rows.start())
    small_rows.finish(small_rows.start())
    small_grads = small_rows.result()

    def total(own, *parts):
        cuts = [jnp.concatenate([p[k] for p in parts], axis=0) for k in range(planes - 1)]
        return own + sum(c.astype(F32) for c in cuts)

    gate_grad = total(gate_own, gate_a, gate_b)
    up_grad = total(up_own, up_a, up_b)
    down_grad = total(down_own, down_a, down_b, down_c)
    return (
        out_rows[:prompt_dev].astype(BF16)[None],
        out_rows[prompt_dev:].astype(BF16)[None, None],
        d_x[:prompt_dev][None],
        d_x[prompt_dev:][None, None],
        small_grads[:, 0],
        small_grads[:, 1],
        small_grads[:, 2],
        small_grads[:, 3],
        query_rows.result().astype(F32),
        key_rows.result().astype(F32),
        value_rows.result().astype(F32),
        output_rows.result().astype(F32),
        small_grads[:, 4:],
        gate_grad[None],
        up_grad[None],
        down_grad[None],
    )


def solution(mesh):
    rows = P(("expert", "dp"), "context", None)
    conts = P(("expert", "dp"), "context", None, None)
    experts = P(("expert", "dp"), None, None)
    everywhere = ("expert", "context", "dp")
    in_specs = (
        (rows, conts, rows, conts, rows, conts, P(("expert", "dp"), "context"))
        + (P("context"),) * 4
        + (P("context", None),) * 5
        + (experts,) * 3
    )
    out_specs = (
        (rows, conts, rows, conts)
        + (P(everywhere),) * 4
        + (P(everywhere, None),) * 5
        + (rows,) * 3
    )
    return jax.shard_map(shards, mesh=mesh, in_specs=in_specs, out_specs=out_specs, check_vma=False)
```

```python
import functools
import math

import jax
import jax.numpy as jnp
from jax import lax
from jax.experimental import pallas as pl
from jax.experimental.pallas import tpu as pltpu
from jax.sharding import PartitionSpec as P

HEADS = 16
EPSILON = 1e-05
NEG_LARGE = -1e30
F32 = jnp.float32
BF16 = jnp.bfloat16
PLANE = ("expert", "dp")
VMEM_LIMIT = 48 * 1024 * 1024


def dot(left, right, dims=((1,), (0,)), out=F32):
    return lax.dot_general(left, right, (dims, ((), ())), preferred_element_type=out)


NT = ((1,), (1,))
TN = ((0,), (0,))


def post_kernel(count, *refs):
    parts, (gain_ref, cos_ref, sin_ref, raw_ref, low_ref) = refs[:count], refs[count:]
    raw = parts[0][...]
    for part in parts[1:]:
        raw = raw + part[...].astype(F32)
    raw_ref[...] = raw
    inverse = lax.rsqrt(jnp.mean(raw * raw, axis=-1, keepdims=True) + EPSILON)
    scaled = raw * inverse * gain_ref[...]
    cosine, sine = cos_ref[...], sin_ref[...]
    head = cosine.shape[1]
    for h in range(raw.shape[1] // head):
        piece = scaled[:, h * head : (h + 1) * head]
        turned = piece * cosine + pltpu.roll(piece, head // 2, 1) * sine
        low_ref[:, h * head : (h + 1) * head] = turned.astype(BF16)


def qk_post(parts, gain, cosine, sine):
    rows, width = parts[0].shape
    head = cosine.shape[1]
    step = 64
    row = lambda w: pl.BlockSpec((step, w), lambda i: (i, 0))
    return pl.pallas_call(
        functools.partial(post_kernel, len(parts)),
        grid=(rows // step,),
        in_specs=[row(width)] * len(parts)
        + [pl.BlockSpec((1, width), lambda i: (0, 0)), row(head), row(head)],
        out_specs=[row(width), row(width)],
        out_shape=[
            jax.ShapeDtypeStruct((rows, width), F32),
            jax.ShapeDtypeStruct((rows, width), BF16),
        ],
        compiler_params=pltpu.CompilerParams(vmem_limit_bytes=VMEM_LIMIT),
        name="qk_post",
    )(*parts, gain, cosine, sine)


def post_back_kernel(grad_ref, raw_ref, gain_ref, cos_ref, sin_ref, low_ref, gain_grad_ref):
    raw = raw_ref[...]
    inverse = lax.rsqrt(jnp.mean(raw * raw, axis=-1, keepdims=True) + EPSILON)
    cosine, sine = cos_ref[...], sin_ref[...]
    head = cosine.shape[1]
    pieces = []
    for h in range(raw.shape[1] // head):
        piece = grad_ref[:, h * head : (h + 1) * head]
        pieces.append(piece * cosine - pltpu.roll(piece, head // 2, 1) * sine)
    grad = jnp.concatenate(pieces, axis=1)
    scaled = grad * gain_ref[...]
    centre = jnp.mean(scaled * raw, axis=-1, keepdims=True)
    low_ref[...] = (inverse * scaled - raw * (inverse * inverse * inverse * centre)).astype(BF16)
    total = jnp.sum(grad * raw * inverse, axis=0, keepdims=True)

    @pl.when(pl.program_id(0) == 0)
    def _():
        gain_grad_ref[...] = total

    @pl.when(pl.program_id(0) > 0)
    def _():
        gain_grad_ref[...] += total


def qk_post_back(grad, raw, gain, cosine, sine):
    rows, width = raw.shape
    head = cosine.shape[1]
    step = 64
    row = lambda w: pl.BlockSpec((step, w), lambda i: (i, 0))
    whole = pl.BlockSpec((1, width), lambda i: (0, 0))
    return pl.pallas_call(
        post_back_kernel,
        grid=(rows // step,),
        in_specs=[row(width), row(width), whole, row(head), row(head)],
        out_specs=[row(width), whole],
        out_shape=[
            jax.ShapeDtypeStruct((rows, width), BF16),
            jax.ShapeDtypeStruct((1, width), F32),
        ],
        compiler_params=pltpu.CompilerParams(vmem_limit_bytes=VMEM_LIMIT),
        name="qk_post_back",
    )(grad, raw, gain, cosine, sine)


def read_mask(meta_ref, rows, keys, prompt_dev, prompt_total):
    row = lax.broadcasted_iota(jnp.int32, (rows, keys), 0)
    key = lax.broadcasted_iota(jnp.int32, (rows, keys), 1)
    is_prompt_row = row < prompt_dev
    is_prompt_key = key < prompt_total
    prompt_limit = jnp.where(is_prompt_row, meta_ref[0] + row + 1, meta_ref[1])
    own_limit = jnp.where(is_prompt_row, 0, row - prompt_dev + 1)
    limit = jnp.where(is_prompt_key, prompt_limit, own_limit + prompt_total)
    return key < limit


def head_probs(query, key, mask):
    scores = jnp.where(mask, dot(query, key, NT) * (query.shape[1] ** -0.5), NEG_LARGE)
    exponent = jnp.exp(scores - jnp.max(scores, axis=-1, keepdims=True))
    return exponent / jnp.sum(exponent, axis=-1, keepdims=True)


def attend_kernel(heads, prompt_dev, prompt_total, meta_ref, q_ref, k_ref, v_ref, out_ref):
    mask = read_mask(meta_ref, q_ref.shape[0], k_ref.shape[0], prompt_dev, prompt_total)
    head = q_ref.shape[1] // heads
    for h in range(heads):
        at = slice(h * head, (h + 1) * head)
        weights = head_probs(q_ref[:, at], k_ref[:, at], mask).astype(BF16)
        out_ref[:, at] = dot(weights, v_ref[:, at]).astype(BF16)


def attend_back_kernel(
    heads, prompt_dev, prompt_total, meta_ref, q_ref, k_ref, v_ref, d_ref, dq_ref, dk_ref, dv_ref
):
    mask = read_mask(meta_ref, q_ref.shape[0], k_ref.shape[0], prompt_dev, prompt_total)
    head = q_ref.shape[1] // heads
    for h in range(heads):
        at = slice(h * head, (h + 1) * head)
        query, key, grad = q_ref[:, at], k_ref[:, at], d_ref[:, at]
        probs = head_probs(query, key, mask)
        d_probs = dot(grad, v_ref[:, at], NT)
        centre = jnp.sum(probs * d_probs, axis=-1, keepdims=True)
        d_scores = (probs * (d_probs - centre) * head**-0.5).astype(BF16)
        dq_ref[:, at] = dot(d_scores, key)
        dk_ref[:, at] = dot(d_scores, query, TN)
        dv_ref[:, at] = dot(probs.astype(BF16), grad, TN)


def attention_call(kernel, name, arrays, outs, meta, prompt_dev, prompt_total):
    width = arrays[0].shape[1]
    heads = 4
    spec = lambda a: pl.BlockSpec((a.shape[0], width * heads // HEADS), lambda i, m: (0, i))
    return pl.pallas_call(
        functools.partial(kernel, heads, prompt_dev, prompt_total),
        grid_spec=pltpu.PrefetchScalarGridSpec(
            num_scalar_prefetch=1,
            grid=(HEADS // heads,),
            in_specs=[spec(a) for a in arrays],
            out_specs=[spec(a) for a in outs],
        ),
        out_shape=outs,
        compiler_params=pltpu.CompilerParams(vmem_limit_bytes=VMEM_LIMIT),
        name=name,
    )(meta, *arrays)


def expert_kernel(*refs):
    refs = refs[:10] + refs[-10:]
    (
        x0_ref, x1_ref, x2_ref, x3_ref, pick_ref, plain_ref, gate_w_ref, up_w_ref, router_ref, mine_ref,
        in_ref, act_ref, dg_ref, du_ref,
        keep_ref, send_ref, dprob_ref,
        total_ref, dp_ref, prob_ref,
    ) = refs
    step = pl.program_id(0)
    slots = pick_ref.shape[1]

    @pl.when(step == 0)
    def _():
        for s, x_ref in enumerate((x0_ref, x1_ref, x2_ref, x3_ref)):
            in_ref[s * slots : (s + 1) * slots, :] = dot(pick_ref[s], x_ref[...]).astype(BF16)
        logits = dot(in_ref[...], router_ref[...])
        exponent = jnp.exp(logits - jnp.max(logits, axis=1, keepdims=True))
        total = jnp.sum(exponent, axis=1, keepdims=True)
        prob_ref[...] = jnp.sum(exponent * mine_ref[...], axis=1, keepdims=True) / total

    rows = in_ref[...]
    gate_w, up_w = gate_w_ref[...], up_w_ref[...]
    gate_pre = dot(rows, gate_w, NT)
    up_pre = dot(rows, up_w, NT)
    plain = plain_ref[...]
    sigmoid = 1.0 / (1.0 + jnp.exp(-gate_pre))
    silu = gate_pre * sigmoid
    act = silu * up_pre
    prob = prob_ref[...]
    act_ref[...] = (prob * act).astype(BF16)
    d_act = prob * plain
    d_gate = (d_act * up_pre * (sigmoid * (1.0 + gate_pre * (1.0 - sigmoid)))).astype(BF16)
    d_up = (d_act * silu).astype(BF16)
    dg_ref[...] = d_gate
    du_ref[...] = d_up
    d_prob = jnp.sum(act * plain, axis=1, keepdims=True)
    d_in = dot(d_gate, gate_w) + dot(d_up, up_w)

    @pl.when(step == 0)
    def _():
        dp_ref[...] = d_prob
        total_ref[...] = d_in

    @pl.when(step > 0)
    def _():
        dp_ref[...] += d_prob
        total_ref[...] += d_in

    @pl.when(step == pl.num_programs(0) - 1)
    def _():
        values = total_ref[...].astype(BF16)
        for s in range(4):
            at = slice(s * slots, (s + 1) * slots)
            (keep_ref, send_ref)[s % 2][s // 2] = dot(pick_ref[s], values[at, :], TN).astype(BF16)
            dprob_ref[s : s + 1, :] = jnp.sum(
                pick_ref[s].astype(F32) * dp_ref[at, :], axis=0, keepdims=True
            )


def expert_quarter(quarter, blocks, pick, plain, gate_w, up_w, router, mine, kept):
    tokens, width = blocks[0].shape
    hidden = gate_w.shape[0]
    tile = 256
    slots = pick.shape[1]
    rows = 4 * slots
    whole = lambda *shape: pl.BlockSpec(shape, lambda f: (0,) * len(shape))
    any_spec = pl.BlockSpec(memory_space=pl.ANY)
    pair = jax.ShapeDtypeStruct((2, tokens, width), BF16)
    tiled = pl.BlockSpec((rows, tile), lambda f: (quarter, f))
    every = pick.shape[0] * slots
    return pl.pallas_call(
        expert_kernel,
        grid=(hidden // tile,),
        in_specs=[whole(tokens, width)] * 4
        + [
            pl.BlockSpec((4, slots, tokens), lambda f: (quarter, 0, 0)),
            tiled,
            pl.BlockSpec((tile, width), lambda f: (f, 0)),
            pl.BlockSpec((tile, width), lambda f: (f, 0)),
            whole(*router.shape),
            whole(*mine.shape),
        ]
        + [any_spec] * len(kept),
        out_specs=[
            pl.BlockSpec((rows, width), lambda f: (quarter, 0)),
            tiled,
            tiled,
            tiled,
        ]
        + [whole(2, tokens, width)] * 2
        + [whole(4, tokens)],
        out_shape=[
            jax.ShapeDtypeStruct((every, width), BF16),
            jax.ShapeDtypeStruct((every, hidden), BF16),
            jax.ShapeDtypeStruct((every, hidden), BF16),
            jax.ShapeDtypeStruct((every, hidden), BF16),
            pair,
            pair,
            jax.ShapeDtypeStruct((4, tokens), F32),
        ],
        scratch_shapes=[
            pltpu.VMEM((rows, width), F32),
            pltpu.VMEM((rows, 1), F32),
            pltpu.VMEM((rows, 1), F32),
        ],
        input_output_aliases={10 + k: k for k in range(len(kept))},
        compiler_params=pltpu.CompilerParams(vmem_limit_bytes=VMEM_LIMIT),
        name="expert",
    )(*blocks, pick, plain, gate_w, up_w, router, mine, *kept)


def expert_out_kernel(pick_ref, act_ref, down_ref, keep_ref, send_ref, values_ref):
    s = pl.program_id(1)

    @pl.when(s == 0)
    def _():
        values = dot(act_ref[...], down_ref[...]).astype(BF16)
        values_ref[...] = values.reshape(values_ref.shape)

    rows = dot(pick_ref[0], values_ref[s], TN).astype(BF16)

    @pl.when(s % 2 == 0)
    def _():
        keep_ref[0, 0] = rows

    @pl.when(s % 2 == 1)
    def _():
        send_ref[0, 0] = rows


def expert_out(pick, act, down_w):
    hidden, width = down_w.shape
    owners, slots, tokens = pick.shape
    rows = 4 * slots
    block = pl.BlockSpec((1, 1, tokens, width), lambda q, s: (q, s // 2, 0, 0))
    return pl.pallas_call(
        expert_out_kernel,
        grid=(owners // 4, 4),
        in_specs=[
            pl.BlockSpec((1, slots, tokens), lambda q, s: (4 * q + s, 0, 0)),
            pl.BlockSpec((rows, hidden), lambda q, s: (q, 0)),
            pl.BlockSpec((hidden, width), lambda q, s: (0, 0)),
        ],
        out_specs=[block, block],
        out_shape=[jax.ShapeDtypeStruct((owners // 4, 2, tokens, width), BF16)] * 2,
        scratch_shapes=[pltpu.VMEM((4, slots, width), BF16)],
        compiler_params=pltpu.CompilerParams(vmem_limit_bytes=VMEM_LIMIT),
        name="expert_out",
    )(pick, act, down_w)


def cot_kernel(source_ref, c0_ref, c1_ref, c2_ref, c3_ref, pick_ref, down_ref, slot_ref, plain_ref):
    slots = pick_ref.shape[1]

    @pl.when(pl.program_id(1) == 0)
    def _():
        for s, cot_ref in enumerate((c0_ref, c1_ref, c2_ref, c3_ref)):
            slot_ref[s * slots : (s + 1) * slots, :] = dot(pick_ref[s], cot_ref[0]).astype(BF16)

    plain_ref[...] = dot(slot_ref[...], down_ref[...], NT)


def gather_cot(source, all_cot, pick, down_w):
    hidden, width = down_w.shape
    owners, slots, tokens = pick.shape
    rows = 4 * slots
    tile = hidden // 2

    def block(s):
        return pl.BlockSpec((1, tokens, width), lambda q, f, m: (m[4 * q + s], 0, 0))

    return pl.pallas_call(
        cot_kernel,
        grid_spec=pltpu.PrefetchScalarGridSpec(
            num_scalar_prefetch=1,
            grid=(owners // 4, hidden // tile),
            in_specs=[block(s) for s in range(4)]
            + [
                pl.BlockSpec((4, slots, tokens), lambda q, f, m: (q, 0, 0)),
                pl.BlockSpec((tile, width), lambda q, f, m: (f, 0)),
            ],
            out_specs=[
                pl.BlockSpec((rows, width), lambda q, f, m: (q, 0)),
                pl.BlockSpec((rows, tile), lambda q, f, m: (q, f)),
            ],
        ),
        out_shape=[
            jax.ShapeDtypeStruct((owners * slots, width), BF16),
            jax.ShapeDtypeStruct((owners * slots, hidden), F32),
        ],
        compiler_params=pltpu.CompilerParams(vmem_limit_bytes=VMEM_LIMIT),
        name="gather_cot",
    )(source, all_cot, all_cot, all_cot, all_cot, pick, down_w)


def row_grads_kernel(cuts, me_ref, left_ref, right_ref, *outs):
    pieces, own_ref = outs[:-1], outs[-1]
    product = dot(left_ref[...], right_ref[...], TN)
    mine = pl.program_id(1) == me_ref[0]

    @pl.when(mine)
    def _():
        own_ref[...] = product

    @pl.when(jnp.logical_not(mine))
    def _():
        low = product.astype(BF16)
        for k, piece_ref in enumerate(pieces):
            piece_ref[0] = low[cuts[k] : cuts[k + 1], :]


def row_grads(me, planes, left, right, shares):
    count, hidden = left.shape
    width = right.shape[1]
    piece = hidden // planes
    tile = width // 2
    cuts = [piece * sum(shares[:k]) // sum(shares) for k in range(len(shares) + 1)]
    sizes = [high - low for low, high in zip(cuts, cuts[1:])]

    def place(n, p, m):
        ahead = (p - m[0] + planes) % planes
        idle = jnp.where(m[0] == planes - 1, planes - 2, 0)
        return (jnp.where(ahead == 0, idle, ahead - 1), 0, n)

    return pl.pallas_call(
        functools.partial(row_grads_kernel, cuts),
        grid_spec=pltpu.PrefetchScalarGridSpec(
            num_scalar_prefetch=1,
            grid=(width // tile, planes),
            in_specs=[
                pl.BlockSpec((count, piece), lambda n, p, m: (0, p)),
                pl.BlockSpec((count, tile), lambda n, p, m: (0, n)),
            ],
            out_specs=[pl.BlockSpec((1, size, tile), place) for size in sizes]
            + [pl.BlockSpec((piece, tile), lambda n, p, m: (0, n))],
        ),
        out_shape=[jax.ShapeDtypeStruct((planes - 1, size, width), BF16) for size in sizes]
        + [jax.ShapeDtypeStruct((piece, width), F32)],
        compiler_params=pltpu.CompilerParams(vmem_limit_bytes=VMEM_LIMIT),
        name="row_grads",
    )(me.reshape(1).astype(jnp.int32), left, right)


def weight_grad_kernel(planes, core_ref, left_ref, *refs):
    rights, (keep_ref, send_ref) = refs[:-2], refs[-2:]
    rows_e, pairs, size, tile = keep_ref.shape
    tokens = left_ref.shape[0] // planes
    count = len(rights) // planes
    size = size // count
    for k in range(count):
        product = sum(
            dot(left_ref[r * tokens : (r + 1) * tokens, :], rights[k * planes + r][...], TN)
            for r in range(planes)
        )
        split_rows = product.astype(BF16).reshape(rows_e, pairs, 2, size, tile)
        at = slice(k * size, (k + 1) * size)

        @pl.when(core_ref[0] == 0)
        def _():
            keep_ref[:, :, at, :] = split_rows[:, :, 0]
            send_ref[:, :, at, :] = split_rows[:, :, 1]

        @pl.when(core_ref[0] != 0)
        def _():
            keep_ref[:, :, at, :] = split_rows[:, :, 1]
            send_ref[:, :, at, :] = split_rows[:, :, 0]


def weight_grads(left, *rights):
    rows_e, rows_d = lax.axis_size("expert"), lax.axis_size("dp")
    planes = len(rights[0])
    total, part = left.shape
    width = rights[0][0].shape[1]
    tile = width // 4
    size = part // (rows_e * rows_d) * len(rights)
    core = (lax.axis_index("dp") % 2).reshape(1).astype(jnp.int32)
    block = pl.BlockSpec((rows_e, rows_d // 2, size, tile), lambda n, m: (0, 0, 0, n))
    return pl.pallas_call(
        functools.partial(weight_grad_kernel, planes),
        grid_spec=pltpu.PrefetchScalarGridSpec(
            num_scalar_prefetch=1,
            grid=(width // tile,),
            in_specs=[pl.BlockSpec((total, part), lambda n, m: (0, 0))]
            + [pl.BlockSpec((total // planes, tile), lambda n, m: (0, n))] * (planes * len(rights)),
            out_specs=[block, block],
        ),
        out_shape=[jax.ShapeDtypeStruct((rows_e, rows_d // 2, size, width), BF16)] * 2,
        compiler_params=pltpu.CompilerParams(vmem_limit_bytes=VMEM_LIMIT),
        name="weight_grads",
    )(core, left, *[array for right in rights for array in right])


def add_rows_kernel(counts, *refs):
    own_ref, parts, out_ref = refs[0], refs[1:-1], refs[-1]
    step = pl.program_id(0)
    at = 0
    for count, ref in zip(counts, parts):

        @pl.when((step >= at) & (step < at + count))
        def _():
            out_ref[...] = own_ref[...] + ref[...].astype(F32)

        at += count


def add_rows(own, parts):
    width = own.shape[1]
    step = math.gcd(*(p.shape[0] for p in parts))
    counts = [p.shape[0] // step for p in parts]
    starts = [sum(counts[:k]) for k in range(len(counts))]

    def spec(start, count):
        return pl.BlockSpec((step, width), lambda i: (jnp.clip(i - start, 0, count - 1), 0))

    rows = pl.BlockSpec((step, width), lambda i: (i, 0))
    return pl.pallas_call(
        functools.partial(add_rows_kernel, counts),
        grid=(own.shape[0] // step,),
        in_specs=[rows] + [spec(a, c) for a, c in zip(starts, counts)],
        out_specs=rows,
        out_shape=jax.ShapeDtypeStruct(own.shape, F32),
        compiler_params=pltpu.CompilerParams(vmem_limit_bytes=VMEM_LIMIT),
        name="add_rows",
    )(own, *parts)


def swap(value, axis, bit):
    return lax.ppermute(value, axis, [(i, i ^ bit) for i in range(lax.axis_size(axis))])


def plus(*values):
    return sum(v.astype(F32) for v in values).astype(values[0].dtype)


ORDER = [
    (i, j) for x in (0, 2) for z in (0, 2) for i in (z, z + 1) for j in (x, x + 1)
]


def fence(*values):
    return lax.optimization_barrier(values)


def split(values, axis_name, bit, at):
    mine = (lax.axis_index(axis_name) // bit) % 2

    def half(index):
        parts = []
        for value in values:
            shape = value.shape
            pairs = value.reshape(shape[:at] + (shape[at] // 2, 2) + shape[at + 1 :])
            parts.append(lax.dynamic_index_in_dim(pairs, index, at + 1, keepdims=False))
        return plus(*parts)

    return half(mine), half(1 - mine)


STAGES = (("dp", 1, 1), ("dp", 2, 1), ("expert", 1, 0), ("expert", 2, 0))


class RowScatter:
    def __init__(self, keep, send):
        self.keep, self.send = keep, send
        self.stage = 0

    def start(self):
        axis, bit, at = STAGES[self.stage]
        if self.stage:
            self.keep, self.send = split(self.parts, axis, bit, at)
        self.stage += 1
        return swap(self.send, axis, bit)

    def finish(self, received):
        self.parts = (self.keep, received)

    def result(self):
        value = plus(*self.parts)
        return value.reshape(value.shape[-2:])


def shards(
    prompt_in,
    cont_in,
    prompt_cot,
    cont_cot,
    prompt_routes,
    cont_routes,
    prefix,
    attn_gain,
    query_gain,
    key_gain,
    ffn_gain,
    w_query,
    w_key,
    w_value,
    w_output,
    w_router,
    expert_gate,
    expert_up,
    expert_down,
):
    prompt_dev, width = prompt_in.shape[1:]
    cont_len = cont_in.shape[2]
    tokens = prompt_dev + cont_len
    head_dim = width // HEADS
    top_count = prompt_routes.shape[2]
    expert_count = w_router.shape[1]
    hidden = expert_gate.shape[1]
    planes = lax.axis_size("context")
    me = lax.axis_index("context")
    rows_e, rows_d = lax.axis_size("expert"), lax.axis_size("dp")
    owners = rows_e * rows_d
    my_expert = lax.axis_index("expert") * rows_d + lax.axis_index("dp")
    prompt_total = prompt_dev * planes
    most_prompt = 9 * prompt_dev * top_count // (8 * expert_count)
    most_cont = 9 * cont_len * top_count // (8 * expert_count)
    slots = (most_prompt + most_cont + 15) // 16 * 16
    part = width // planes
    out_group = width // (rows_e * planes)

    def shift(value, r):
        return lax.ppermute(value, "context", [(i, (i + r) % planes) for i in range(planes)])

    def block(value, r):
        return lax.dynamic_slice_in_dim(value, ((me + r) % planes) * part, part, axis=1)

    def out_part(value, r):
        at = ((me + r) % planes) * out_group
        return jnp.concatenate(
            [
                lax.dynamic_slice_in_dim(value, e * planes * out_group + at, out_group, axis=1)
                for e in range(rows_e)
            ],
            axis=1,
        )

    def placed(blocks):
        full = jnp.zeros((tokens, width), blocks[0].dtype)
        for r, piece in enumerate(blocks):
            full = lax.dynamic_update_slice_in_dim(full, piece, ((me + r) % planes) * part, axis=1)
        return full

    others = range(1, planes)

    x_low = jnp.concatenate([prompt_in[0], cont_in[0, 0]], axis=0)
    x_rows = x_low.astype(F32)
    inverse = lax.rsqrt(jnp.mean(x_rows * x_rows, axis=-1) + EPSILON)
    x_blocks = [block(x_low, 0)] + [shift(block(x_low, r), r) for r in others]
    inverses = [inverse] + [shift(inverse, r) for r in others]
    gain_part = attn_gain.astype(F32)
    normed_blocks = [
        (piece.astype(F32) * inv[:, None] * gain_part).astype(BF16)
        for piece, inv in zip(x_blocks, inverses)
    ]

    def gathered(value, axis):
        shape = list(value.shape)
        shape[axis] = shape[axis] * planes
        full = jnp.zeros(shape, value.dtype)
        for r in range(planes):
            piece = shift(value, r) if r else value
            at = ((me - r) % planes) * value.shape[axis]
            full = lax.dynamic_update_slice_in_dim(full, piece, at, axis=axis)
        return full

    gains_in = jnp.stack([attn_gain, query_gain, key_gain, ffn_gain])

    d_out_low = jnp.concatenate([prompt_cot[0], cont_cot[0, 0]], axis=0)
    routes = jnp.concatenate([prompt_routes[0], cont_routes[0, 0]], axis=0)
    named = sum(
        (routes[:, k : k + 1] == jnp.arange(expert_count, dtype=jnp.int32)[None, :]).astype(F32)
        for k in range(top_count)
    )
    all_cot = lax.all_gather(d_out_low, PLANE, axis=0, tiled=True)

    start_len = prefix[0, 0]
    prompt_pos = me * prompt_dev + jnp.arange(prompt_dev, dtype=jnp.int32)
    positions = jnp.concatenate([prompt_pos, start_len + jnp.arange(cont_len, dtype=jnp.int32)])
    half_index = jnp.arange(head_dim // 2, dtype=F32)
    angles = positions.astype(F32)[:, None] * (10000.0 ** (-2.0 * half_index / head_dim))[None, :]
    cosine = jnp.cos(angles)
    sine = jnp.sin(angles)
    cosine = jnp.concatenate([cosine, cosine], axis=1)
    sine = jnp.concatenate([-sine, sine], axis=1)
    meta = jnp.stack([me * prompt_dev, start_len]).astype(jnp.int32)

    def project(pieces, weight):
        products = [dot(pieces[r], weight).astype(BF16) for r in others]
        products = fence(pieces[0], *products)
        sent = [shift(product, planes - r) for r, product in zip(others, products[1:])]
        return [dot(products[0], weight)] + sent

    key_parts = project(normed_blocks, w_key)
    key_parts[0], named, gains_in, w_router = fence(key_parts[0], named, gains_in, w_router)
    gains = gathered(gains_in, 1).astype(F32)
    gain_attn, gain_query, gain_key, gain_ffn = [gains[i : i + 1] for i in range(4)]
    full_router = gathered(w_router, 0)
    member = lax.all_to_all(named.T, PLANE, split_axis=0, concat_axis=0, tiled=True)
    value_parts = project(normed_blocks, w_value)
    query_parts = project(normed_blocks, w_query)
    key_raw, key_low = qk_post(key_parts, gain_key, cosine, sine)
    value_low = sum(p.astype(F32) for p in value_parts).astype(BF16)
    query_parts[0], full_router, member = fence(query_parts[0], full_router, member)
    query_raw, query_low = qk_post(query_parts, gain_query, cosine, sine)

    def with_prompt(rows):
        full = jnp.zeros((prompt_total + cont_len, width), BF16)
        full = lax.dynamic_update_slice_in_dim(full, rows[prompt_dev:], prompt_total, axis=0)
        for r in range(planes):
            piece = rows[:prompt_dev]
            if r:
                piece = shift(piece, planes - r)
            full = lax.dynamic_update_slice_in_dim(
                full, piece, ((me + r) % planes) * prompt_dev, axis=0
            )
        return full

    key_set = with_prompt(key_low)
    value_set = with_prompt(value_low)
    (attended,) = attention_call(
        attend_kernel,
        "attend",
        [query_low, key_set, value_set],
        [jax.ShapeDtypeStruct((tokens, width), BF16)],
        meta,
        prompt_dev,
        prompt_total,
    )

    attended_blocks = [block(attended, 0)] + [shift(block(attended, r), r) for r in others]
    mixed_rows = x_rows + sum(p.astype(F32) for p in project(attended_blocks, w_output))
    inverse2 = lax.rsqrt(jnp.mean(mixed_rows * mixed_rows, axis=-1, keepdims=True) + EPSILON)
    normed2_low = (mixed_rows * inverse2 * gain_ffn).astype(BF16)

    normed_low = (x_rows * inverse[:, None] * gain_attn).astype(BF16)

    logits = dot(normed2_low, full_router)
    shifted = jnp.exp(logits - jnp.max(logits, axis=1, keepdims=True))
    router_probs = shifted / jnp.sum(shifted, axis=1, keepdims=True)

    my_e, my_d = lax.axis_index("expert"), lax.axis_index("dp")
    source = jnp.stack([(my_e ^ i) * rows_d + (my_d ^ j) for i, j in ORDER]).astype(jnp.int32)
    member = jnp.take(member, source, axis=0)

    def ranks(m):
        count = m.shape[1]
        before = jnp.triu(jnp.ones((count, count), BF16), 1)
        return dot(m.astype(BF16), before)

    slot_of = jnp.concatenate(
        [ranks(member[:, :prompt_dev]), ranks(member[:, prompt_dev:]) + most_prompt], axis=1
    )
    slot_of = jnp.where(member > 0, slot_of, -1.0)
    pick = (
        slot_of[:, None, :] == jnp.arange(slots, dtype=F32)[None, :, None]
    ).astype(BF16)
    gate_w, up_w, down_w = expert_gate[0], expert_up[0], expert_down[0]
    mine = (jnp.arange(expert_count, dtype=jnp.int32) == my_expert).astype(F32)[None, :]

    def z1(v):
        return swap(v, "expert", 1)

    def z2(v):
        return swap(v, "expert", 2)

    def core(v):
        return swap(v, "dp", 1)

    def across(v):
        return swap(v, "dp", 2)

    b0, all_cot, normed_low = fence(normed2_low, all_cot, normed_low)
    b1, b2, x0, c0 = z1(b0), z2(b0), across(b0), core(b0)
    normed_sent = [shift(out_part(normed_low, r), r) for r in others]
    attended_sent = [shift(out_part(attended, r), r) for r in others]
    all_cot = all_cot.reshape(owners, tokens, width)
    slot_cot, d_act_plain = gather_cot(source, all_cot, pick, down_w)
    b1, b2, x0, c0, d_act_plain, *rest = fence(
        b1, b2, x0, c0, d_act_plain, *normed_sent, *attended_sent
    )
    normed_out = jnp.concatenate([out_part(normed_low, 0), *rest[: planes - 1]], axis=0)
    attended_out = jnp.concatenate([out_part(attended, 0), *rest[planes - 1 :]], axis=0)
    b3, x1, c1, x0c = z1(b2), across(b1), core(b1), core(x0)
    b3, x1, c1, x0c = fence(b3, x1, c1, x0c)

    def quarter(q, blocks, kept):
        outs = expert_quarter(q, blocks, pick, d_act_plain, gate_w, up_w, full_router, mine, kept)
        return outs[:4], outs[4], outs[5], outs[6]

    x2, c2, c3, x1c = across(b2), core(b2), core(b3), core(x1)
    kept, keep0, send0, dprob0 = quarter(0, (b0, c0, b1, c1), ())
    x2, c2, c3, x1c, *kept = fence(x2, c2, c3, x1c, *kept)
    x3, x2c = across(b3), core(x2)
    kept, keep2, send2, dprob2 = quarter(2, (x0, x0c, x1, x1c), kept)
    x3, x2c, send2, *kept = fence(x3, x2c, send2, *kept)
    x3c, near2, near0 = core(x3), core(send2), core(send0)
    x3c, near2, near0, *kept = fence(x3c, near2, near0, *kept)
    pair2 = plus(keep2, near2)
    got21 = across(pair2[1])
    kept, keep3, send3, dprob3 = quarter(3, (x2, x2c, x3, x3c), kept)
    got21, pair20, send3, *kept = fence(got21, pair2[0], send3, *kept)
    got20, near3 = across(pair20), core(send3)
    kept, keep1, send1, dprob1 = quarter(1, (b2, c2, b3, c3), kept)
    got20, near3, send1, *kept = fence(got20, near3, send1, *kept)
    slot_in, act_low, d_gate, d_up = kept

    piece = hidden // planes

    def send_rows(values):
        return [shift(values[r - 1], r) for r in others]

    pair3 = plus(keep3, near3)
    first_got, got31, near1 = z1(plus(keep0[1], near0[1], got21)), across(pair3[1]), core(send1)
    *gate_low, gate_own = row_grads(me, planes, d_gate, slot_in, (1, 1))
    first_got, got31, near1, gate_own, pair30, d_up, slot_in, *gate_low = fence(
        first_got, got31, near1, gate_own, pair3[0], d_up, slot_in, *gate_low
    )
    second_got, got30 = z1(plus(keep1[1], near1[1], got31)), across(pair30)
    gate_a = send_rows(gate_low[0])
    *up_low, up_own = row_grads(me, planes, d_up, slot_in, (1, 2, 1))
    place = jnp.zeros((owners,), jnp.int32).at[source].set(jnp.arange(owners, dtype=jnp.int32))
    token_dprob = jnp.take(
        jnp.concatenate([dprob0, dprob1, dprob2, dprob3], axis=0), place, axis=0
    )
    second_got, got30, token_dprob, act_low, up_own, gate_b, up_0, up_1, up_2, *gate_a = fence(
        second_got, got30, token_dprob, act_low, up_own, gate_low[1], *up_low, *gate_a
    )
    far_got = z2(plus(keep1[0], near1[0], got30, second_got))
    gate_b, up_a = send_rows(gate_b), send_rows(up_0)
    out_keep, out_send = expert_out(pick, act_low, down_w)
    dprobs = lax.all_to_all(token_dprob, PLANE, split_axis=0, concat_axis=0, tiled=True).T
    out_near = core(out_send)
    far_got, dprobs, act_low, out_keep, out_near, *rest = fence(
        far_got, dprobs, act_low, out_keep, out_near, *gate_b, *up_a
    )
    gate_b, up_a = rest[: planes - 1], rest[planes - 1 :]
    d_normed2_moe = (
        keep0[0].astype(F32)
        + near0[0].astype(F32)
        + got20.astype(F32)
        + first_got.astype(F32)
        + far_got.astype(F32)
    )

    d_out = d_out_low.astype(F32)
    dlogit_low = (
        router_probs * (dprobs - jnp.sum(router_probs * dprobs, axis=1, keepdims=True))
    ).astype(BF16)
    router_grad = dot(normed2_low, dlogit_low, TN)
    d_normed2 = d_normed2_moe + dot(dlogit_low, full_router, NT)
    scaled2 = gain_ffn * d_normed2
    centre2 = jnp.mean(scaled2 * mixed_rows, axis=-1, keepdims=True)
    d_mixed = d_out + inverse2 * scaled2 - mixed_rows * (inverse2**3 * centre2)
    ffn_gain_grad = jnp.sum(d_normed2 * mixed_rows * inverse2, axis=0)

    branch_low = d_mixed.astype(BF16)
    def out_sum(q, i):
        return plus(out_keep[q, i], out_near[q, i])

    branch_low, out31, act_low = fence(branch_low, out_sum(3, 1), act_low)
    sent = [shift(branch_low, r) for r in others]
    out_got31 = across(out31)
    *down_low, down_own = row_grads(me, planes, act_low, slot_cot, (1, 1))
    out30 = out_sum(3, 0)
    out_got31, out30, out_keep, out_near, down_own, down_0, down_1, branch_low, *sent = fence(
        out_got31, out30, out_keep, out_near, down_own, *down_low, branch_low, *sent
    )
    branches = [branch_low, *sent]
    blocks_low = [dot(branches[r], w_output, NT).astype(BF16) for r in others]
    d_att_blocks = [shift(v, planes - r) for r, v in zip(others, blocks_low)]
    d_att_own = dot(branches[0], w_output, NT).astype(BF16)
    out_second = plus(out_keep[1, 1], out_near[1, 1], out_got31)
    d_att_own, up_1, out_second, gate_own, branch_low, *d_att_blocks = fence(
        d_att_own, up_1, out_second, gate_own, branch_low, *d_att_blocks
    )
    branches[0] = branch_low
    d_attended = placed([d_att_own, *d_att_blocks])

    key_total = prompt_total + cont_len
    out_got30, out_second = across(out30), z1(out_second)
    up_b = send_rows(up_1)
    output_keep, output_send = weight_grads(attended_out, branches)
    d_queries, d_keys_all, d_values_all = attention_call(
        attend_back_kernel,
        "attend_back",
        [query_low, key_set, value_set, d_attended],
        [
            jax.ShapeDtypeStruct((tokens, width), F32),
            jax.ShapeDtypeStruct((key_total, width), F32),
            jax.ShapeDtypeStruct((key_total, width), F32),
        ],
        meta,
        prompt_dev,
        prompt_total,
    )
    out21 = out_sum(2, 1)
    out_got30, out_second, output_keep, output_send, out21, d_queries, d_keys_all, d_values_all, *up_b = fence(
        out_got30, out_second, output_keep, output_send, out21, d_queries, d_keys_all, d_values_all, *up_b
    )
    output_rows = RowScatter(output_keep, output_send)

    def prompt_sent(rows):
        return [
            shift(
                lax.dynamic_slice_in_dim(
                    rows, ((me + r) % planes) * prompt_dev, prompt_dev, axis=0
                ).astype(BF16),
                r,
            )
            for r in others
        ]

    def own_keys(rows, got):
        total = lax.dynamic_slice_in_dim(rows, me * prompt_dev, prompt_dev, axis=0)
        for part in got:
            total = total + part.astype(F32)
        return jnp.concatenate([total, rows[prompt_total:]], axis=0)

    value_prompt, key_prompt = prompt_sent(d_values_all), prompt_sent(d_keys_all)
    out_got21, output_got = across(out21), output_rows.start()
    d_query_low, query_gain_grad = qk_post_back(d_queries, query_raw, gain_query, cosine, sine)
    out20, out_far = out_sum(2, 0), plus(out_keep[1, 0], out_near[1, 0], out_got30, out_second)
    out_got21, output_got, out20, out_far, d_query_low, gate_own, *rest = fence(
        out_got21, output_got, out20, out_far, d_query_low, gate_own, *value_prompt, *key_prompt
    )
    output_rows.finish(output_got)
    d_value_low = own_keys(d_values_all, rest[: planes - 1]).astype(BF16)
    d_keys = own_keys(d_keys_all, rest[planes - 1 :])

    def spread(low):
        return [shift(low, r) for r in others]

    def total(own, *parts):
        for k in range(planes - 1):
            own = add_rows(own, [p[k] for p in parts])
        return own

    d_value_low, d_keys = fence(d_value_low, d_keys)
    got = spread(d_value_low) + spread(d_query_low)
    out_got20, out_far = across(out20), z2(out_far)
    d_key_low, key_gain_grad = qk_post_back(d_keys, key_raw, gain_key, cosine, sine)
    gate_grad = total(gate_own, gate_a, gate_b)
    out_first = plus(out_keep[0, 1], out_near[0, 1], out_got21)
    out_got20, out_far, out_first, d_key_low, gate_grad, *rest = fence(
        out_got20, out_far, out_first, d_key_low, gate_grad, *got
    )
    d_values, d_query_got = rest[: planes - 1], rest[planes - 1 :]

    got, output_got, out_first = spread(d_key_low), output_rows.start(), z1(out_first)
    early_keep, early_send = weight_grads(
        normed_out, [d_value_low, *d_values], [d_query_low, *d_query_got]
    )
    partial = [
        dot(d_values[k], w_value, NT) + dot(d_query_got[k], w_query, NT) for k in range(planes - 1)
    ]
    output_got, out_first, early_keep, early_send, *rest = fence(
        output_got, out_first, early_keep, early_send, *got, *partial
    )
    d_key_got, partial = rest[: planes - 1], rest[planes - 1 :]
    output_rows.finish(output_got)
    early_rows = RowScatter(early_keep, early_send)
    out_rows = (
        mixed_rows
        + plus(out_keep[0, 0].astype(F32), out_near[0, 0])
        + out_got20.astype(F32)
        + out_first.astype(F32)
        + out_far.astype(F32)
    )

    early_got = early_rows.start()
    key_keep, key_send = weight_grads(normed_out, [d_key_low, *d_key_got])
    blocks_low = [
        (partial[k] + dot(d_key_got[k], w_key, NT)).astype(BF16) for k in range(planes - 1)
    ]
    early_got, key_keep, key_send, up_2, down_0, *blocks_low = fence(
        early_got, key_keep, key_send, up_2, down_0, *blocks_low
    )
    early_rows.finish(early_got)
    key_rows = RowScatter(key_keep, key_send)

    d_normed_got = [shift(v, planes - r) for r, v in zip(others, blocks_low)]
    early_got, key_got, output_got = early_rows.start(), key_rows.start(), output_rows.start()
    up_c, down_a = send_rows(up_2), send_rows(down_0)
    d_normed_own = (
        dot(d_value_low, w_value, NT) + dot(d_query_low, w_query, NT) + dot(d_key_low, w_key, NT)
    )
    d_normed = placed([d_normed_own] + [p.astype(F32) for p in d_normed_got])
    scaled = gain_attn * d_normed
    centre = jnp.mean(scaled * x_rows, axis=-1, keepdims=True)
    inv = inverse[:, None]
    d_x = d_mixed + inv * scaled - x_rows * (inv**3 * centre)
    attn_gain_grad = jnp.sum(d_normed * x_rows * inv, axis=0)
    small_grads = jnp.concatenate(
        [
            jnp.stack([attn_gain_grad, query_gain_grad[0], key_gain_grad[0], ffn_gain_grad], axis=1),
            router_grad,
        ],
        axis=1,
    )
    early_got, key_got, output_got, d_x, small_grads, down_1, *rest = fence(
        early_got, key_got, output_got, d_x, small_grads, down_1, *up_c, *down_a
    )
    up_c, down_a = rest[: planes - 1], rest[planes - 1 :]
    early_rows.finish(early_got)
    key_rows.finish(key_got)
    output_rows.finish(output_got)

    key_got, early_got, output_got = key_rows.start(), early_rows.start(), output_rows.start()
    down_b = send_rows(down_1)
    by_plane = small_grads.reshape(rows_e, planes, out_group, small_grads.shape[1])

    def plane_rows(r):
        return lax.dynamic_index_in_dim(by_plane, (me + r) % planes, 1, False)

    small_sum = plus(plane_rows(0), *[shift(plane_rows(r), r) for r in others])
    small_rows = RowScatter(
        *split([small_sum.reshape(rows_e, rows_d, -1, small_sum.shape[-1])], *STAGES[0])
    )
    small_rows.finish(small_rows.start())
    up_grad = total(up_own, up_a, up_b, up_c)
    key_got, early_got, output_got, small_rows.parts, up_grad, *down_b = fence(
        key_got, early_got, output_got, small_rows.parts, up_grad, *down_b
    )
    key_rows.finish(key_got)
    early_rows.finish(early_got)
    output_rows.finish(output_got)

    key_got, early_got = key_rows.start(), early_rows.start()
    small_rows.finish(small_rows.start())
    small_rows.finish(small_rows.start())
    down_grad = total(down_own, down_a, down_b)
    key_got, early_got, small_rows.parts, down_grad = fence(
        key_got, early_got, small_rows.parts, down_grad
    )
    key_rows.finish(key_got)
    early_rows.finish(early_got)
    key_rows.finish(key_rows.start())
    small_rows.finish(small_rows.start())
    small_grads = small_rows.result()
    early_grads = early_rows.result().astype(F32)
    size = early_grads.shape[0] // 2
    return (
        out_rows[:prompt_dev].astype(BF16)[None],
        out_rows[prompt_dev:].astype(BF16)[None, None],
        d_x[:prompt_dev][None],
        d_x[prompt_dev:][None, None],
        small_grads[:, 0],
        small_grads[:, 1],
        small_grads[:, 2],
        small_grads[:, 3],
        early_grads[size:],
        key_rows.result().astype(F32),
        early_grads[:size],
        output_rows.result().astype(F32),
        small_grads[:, 4:],
        gate_grad[None],
        up_grad[None],
        down_grad[None],
    )


def solution(mesh):
    rows = P(("expert", "dp"), "context", None)
    conts = P(("expert", "dp"), "context", None, None)
    experts = P(("expert", "dp"), None, None)
    everywhere = ("expert", "context", "dp")
    in_specs = (
        (rows, conts, rows, conts, rows, conts, P(("expert", "dp"), "context"))
        + (P("context"),) * 4
        + (P("context", None),) * 5
        + (experts,) * 3
    )
    out_specs = (
        (rows, conts, rows, conts)
        + (P(everywhere),) * 4
        + (P(everywhere, None),) * 5
        + (rows,) * 3
    )
    return jax.shard_map(shards, mesh=mesh, in_specs=in_specs, out_specs=out_specs, check_vma=False)
```

```python
import functools
import math

import jax
import jax.numpy as jnp
from jax import lax
from jax.experimental import pallas as pl
from jax.experimental.pallas import tpu as pltpu
from jax.sharding import PartitionSpec as P

HEADS = 16
EPSILON = 1e-05
NEG_LARGE = -1e30
F32 = jnp.float32
BF16 = jnp.bfloat16
PLANE = ("expert", "dp")
VMEM_LIMIT = 48 * 1024 * 1024


def dot(left, right, dims=((1,), (0,)), out=F32):
    return lax.dot_general(left, right, (dims, ((), ())), preferred_element_type=out)


NT = ((1,), (1,))
TN = ((0,), (0,))


def post_kernel(count, *refs):
    parts, (gain_ref, cos_ref, sin_ref, raw_ref, low_ref) = refs[:count], refs[count:]
    raw = parts[0][...]
    for part in parts[1:]:
        raw = raw + part[...].astype(F32)
    raw_ref[...] = raw
    inverse = lax.rsqrt(jnp.mean(raw * raw, axis=-1, keepdims=True) + EPSILON)
    scaled = raw * inverse * gain_ref[...]
    cosine, sine = cos_ref[...], sin_ref[...]
    head = cosine.shape[1]
    for h in range(raw.shape[1] // head):
        piece = scaled[:, h * head : (h + 1) * head]
        turned = piece * cosine + pltpu.roll(piece, head // 2, 1) * sine
        low_ref[:, h * head : (h + 1) * head] = turned.astype(BF16)


def qk_post(parts, gain, cosine, sine):
    rows, width = parts[0].shape
    head = cosine.shape[1]
    step = 64
    row = lambda w: pl.BlockSpec((step, w), lambda i: (i, 0))
    return pl.pallas_call(
        functools.partial(post_kernel, len(parts)),
        grid=(rows // step,),
        in_specs=[row(width)] * len(parts)
        + [pl.BlockSpec((1, width), lambda i: (0, 0)), row(head), row(head)],
        out_specs=[row(width), row(width)],
        out_shape=[
            jax.ShapeDtypeStruct((rows, width), F32),
            jax.ShapeDtypeStruct((rows, width), BF16),
        ],
        compiler_params=pltpu.CompilerParams(vmem_limit_bytes=VMEM_LIMIT),
        name="qk_post",
    )(*parts, gain, cosine, sine)


def post_back_kernel(grad_ref, raw_ref, gain_ref, cos_ref, sin_ref, *refs):
    got, (low_ref, gain_grad_ref, sum_ref) = refs[:-3], refs[-3:]
    sum_ref[...] = grad_ref[...]
    if got:

        @pl.when(pl.program_id(0) == 0)
        def _():
            for ref in got:
                sum_ref[...] += ref[...].astype(F32)

    raw = raw_ref[...]
    inverse = lax.rsqrt(jnp.mean(raw * raw, axis=-1, keepdims=True) + EPSILON)
    cosine, sine = cos_ref[...], sin_ref[...]
    head = cosine.shape[1]
    pieces = []
    for h in range(raw.shape[1] // head):
        piece = sum_ref[:, h * head : (h + 1) * head]
        pieces.append(piece * cosine - pltpu.roll(piece, head // 2, 1) * sine)
    grad = jnp.concatenate(pieces, axis=1)
    scaled = grad * gain_ref[...]
    centre = jnp.mean(scaled * raw, axis=-1, keepdims=True)
    low_ref[...] = (inverse * scaled - raw * (inverse * inverse * inverse * centre)).astype(BF16)
    total = jnp.sum(grad * raw * inverse, axis=0, keepdims=True)

    @pl.when(pl.program_id(0) == 0)
    def _():
        gain_grad_ref[...] = total

    @pl.when(pl.program_id(0) > 0)
    def _():
        gain_grad_ref[...] += total


def qk_post_back(grad, raw, gain, cosine, sine, got=()):
    rows, width = raw.shape
    head = cosine.shape[1]
    step = got[0].shape[0] if got else 64
    row = lambda w: pl.BlockSpec((step, w), lambda i: (i, 0))
    whole = pl.BlockSpec((1, width), lambda i: (0, 0))
    return pl.pallas_call(
        post_back_kernel,
        grid=(rows // step,),
        in_specs=[row(width), row(width), whole, row(head), row(head)]
        + [pl.BlockSpec((step, width), lambda i: (0, 0))] * len(got),
        out_specs=[row(width), whole],
        out_shape=[
            jax.ShapeDtypeStruct((rows, width), BF16),
            jax.ShapeDtypeStruct((1, width), F32),
        ],
        scratch_shapes=[pltpu.VMEM((step, width), F32)],
        compiler_params=pltpu.CompilerParams(vmem_limit_bytes=VMEM_LIMIT),
        name="qk_post_back",
    )(grad, raw, gain, cosine, sine, *got)


def row_specs(items, step):
    pairs = [item if isinstance(item, tuple) else (item,) for item in items]

    def spec(array, at):
        width = array.shape[-1]
        return pl.BlockSpec((None,) * len(at) + (step, width), lambda i: at + (i, 0))

    return [p[0] for p in pairs], [spec(p[0], p[1:]) for p in pairs]


def add_blocks(*items):
    return plus(*[item[0][item[1:]] if isinstance(item, tuple) else item for item in items])


def norm_back_kernel(count, *refs):
    parts = refs[:count]
    (
        d_out_ref, mixed_ref, gain_ref, probs_ref, d_probs_ref, router_ref,
        d_mixed_ref, branch_ref, d_logit_ref, gain_grad_ref,
    ) = refs[count:]
    probs, d_probs = probs_ref[...], d_probs_ref[...]
    centre = jnp.sum(probs * d_probs, axis=1, keepdims=True)
    d_logit = (probs * (d_probs - centre)).astype(BF16)
    d_logit_ref[...] = d_logit
    grad = dot(d_logit, router_ref[...], NT)
    for part in parts:
        grad = grad + part[...].astype(F32)
    mixed = mixed_ref[...]
    inverse = lax.rsqrt(jnp.mean(mixed * mixed, axis=-1, keepdims=True) + EPSILON)
    scaled = grad * gain_ref[...]
    centre = jnp.mean(scaled * mixed, axis=-1, keepdims=True)
    d_mixed = (
        d_out_ref[...].astype(F32)
        + inverse * scaled
        - mixed * (inverse * inverse * inverse * centre)
    )
    d_mixed_ref[...] = d_mixed
    branch_ref[...] = d_mixed.astype(BF16)
    total = jnp.sum(grad * mixed * inverse, axis=0, keepdims=True)

    @pl.when(pl.program_id(0) == 0)
    def _():
        gain_grad_ref[...] = total

    @pl.when(pl.program_id(0) > 0)
    def _():
        gain_grad_ref[...] += total


def norm_back(parts, d_out, mixed, gain, probs, d_probs, router):
    rows, width = mixed.shape
    experts = probs.shape[1]
    step = 64
    row = lambda w: pl.BlockSpec((step, w), lambda i: (i, 0))
    whole = lambda *shape: pl.BlockSpec(shape, lambda i: (0, 0))
    parts, specs = row_specs(parts, step)
    return pl.pallas_call(
        functools.partial(norm_back_kernel, len(parts)),
        grid=(rows // step,),
        in_specs=specs
        + [row(width)] * 2
        + [whole(1, width), row(experts), row(experts), whole(width, experts)],
        out_specs=[row(width), row(width), row(experts), whole(1, width)],
        out_shape=[
            jax.ShapeDtypeStruct((rows, width), F32),
            jax.ShapeDtypeStruct((rows, width), BF16),
            jax.ShapeDtypeStruct((rows, experts), BF16),
            jax.ShapeDtypeStruct((1, width), F32),
        ],
        compiler_params=pltpu.CompilerParams(vmem_limit_bytes=VMEM_LIMIT),
        name="norm_back",
    )(*parts, d_out, mixed, gain, probs, d_probs, router)


def read_mask(meta_ref, rows, keys, prompt_dev, prompt_total):
    row = lax.broadcasted_iota(jnp.int32, (rows, keys), 0)
    key = lax.broadcasted_iota(jnp.int32, (rows, keys), 1)
    is_prompt_row = row < prompt_dev
    is_prompt_key = key < prompt_total
    prompt_limit = jnp.where(is_prompt_row, meta_ref[0] + row + 1, meta_ref[1])
    own_limit = jnp.where(is_prompt_row, 0, row - prompt_dev + 1)
    limit = jnp.where(is_prompt_key, prompt_limit, own_limit + prompt_total)
    return key < limit


def head_probs(query, key, mask):
    scores = jnp.where(mask, dot(query, key, NT) * (query.shape[1] ** -0.5), NEG_LARGE)
    exponent = jnp.exp(scores - jnp.max(scores, axis=-1, keepdims=True))
    return exponent / jnp.sum(exponent, axis=-1, keepdims=True)


def attend_kernel(heads, prompt_dev, prompt_total, meta_ref, q_ref, k_ref, v_ref, out_ref):
    mask = read_mask(meta_ref, q_ref.shape[0], k_ref.shape[0], prompt_dev, prompt_total)
    head = q_ref.shape[1] // heads
    for h in range(heads):
        at = slice(h * head, (h + 1) * head)
        weights = head_probs(q_ref[:, at], k_ref[:, at], mask).astype(BF16)
        out_ref[:, at] = dot(weights, v_ref[:, at]).astype(BF16)


def attend_back_kernel(
    heads, prompt_dev, prompt_total, meta_ref, q_ref, k_ref, v_ref, d_ref,
    dq_ref, dk_ref, dv_ref, dk_low_ref, dv_low_ref, rows_ref,
):
    mask = read_mask(meta_ref, q_ref.shape[0], k_ref.shape[0], prompt_dev, prompt_total)
    head = q_ref.shape[1] // heads
    mine = pl.ds(pl.multiple_of(meta_ref[0], prompt_dev), prompt_dev)

    def store(rows, own_ref, low_ref, at):
        low_ref[:, at] = rows[:prompt_total].astype(BF16)
        rows_ref[...] = rows[:prompt_total]
        own_ref[:prompt_dev, at] = rows_ref[mine, :]
        own_ref[prompt_dev:, at] = rows[prompt_total:]

    for h in range(heads):
        at = slice(h * head, (h + 1) * head)
        query, key, grad = q_ref[:, at], k_ref[:, at], d_ref[:, at]
        probs = head_probs(query, key, mask)
        d_probs = dot(grad, v_ref[:, at], NT)
        centre = jnp.sum(probs * d_probs, axis=-1, keepdims=True)
        d_scores = (probs * (d_probs - centre) * head**-0.5).astype(BF16)
        dq_ref[:, at] = dot(d_scores, key)
        store(dot(d_scores, query, TN), dk_ref, dk_low_ref, at)
        store(dot(probs.astype(BF16), grad, TN), dv_ref, dv_low_ref, at)


def value_kernel(own_ref, *refs):
    got, low_ref = refs[:-1], refs[-1]

    @pl.when(pl.program_id(0) == 0)
    def _():
        total = own_ref[...]
        for ref in got:
            total = total + ref[...].astype(F32)
        low_ref[...] = total.astype(BF16)

    @pl.when(pl.program_id(0) > 0)
    def _():
        low_ref[...] = own_ref[...].astype(BF16)


def value_rows_low(own, got):
    rows, width = own.shape
    step = got[0].shape[0] if got else 64
    row = pl.BlockSpec((step, width), lambda i: (i, 0))
    first = pl.BlockSpec((step, width), lambda i: (0, 0))
    return pl.pallas_call(
        value_kernel,
        grid=(rows // step,),
        in_specs=[row] + [first] * len(got),
        out_specs=row,
        out_shape=jax.ShapeDtypeStruct((rows, width), BF16),
        compiler_params=pltpu.CompilerParams(vmem_limit_bytes=VMEM_LIMIT),
        name="value_rows",
    )(own, *got)


def attention_call(kernel, name, arrays, outs, meta, prompt_dev, prompt_total, scratch=()):
    width = arrays[0].shape[1]
    heads = 4
    spec = lambda a: pl.BlockSpec((a.shape[0], width * heads // HEADS), lambda i, m: (0, i))
    return pl.pallas_call(
        functools.partial(kernel, heads, prompt_dev, prompt_total),
        grid_spec=pltpu.PrefetchScalarGridSpec(
            num_scalar_prefetch=1,
            grid=(HEADS // heads,),
            in_specs=[spec(a) for a in arrays],
            out_specs=[spec(a) for a in outs],
            scratch_shapes=scratch,
        ),
        out_shape=outs,
        compiler_params=pltpu.CompilerParams(vmem_limit_bytes=VMEM_LIMIT),
        name=name,
    )(meta, *arrays)


def expert_kernel(*refs):
    refs = refs[:10] + refs[-10:]
    (
        x0_ref, x1_ref, x2_ref, x3_ref, pick_ref, plain_ref, gate_w_ref, up_w_ref, router_ref, mine_ref,
        in_ref, act_ref, dg_ref, du_ref,
        keep_ref, send_ref, dprob_ref,
        total_ref, dp_ref, prob_ref,
    ) = refs
    step = pl.program_id(0)
    slots = pick_ref.shape[1]

    @pl.when(step == 0)
    def _():
        for s, x_ref in enumerate((x0_ref, x1_ref, x2_ref, x3_ref)):
            in_ref[s * slots : (s + 1) * slots, :] = dot(pick_ref[s], x_ref[...]).astype(BF16)
        logits = dot(in_ref[...], router_ref[...])
        exponent = jnp.exp(logits - jnp.max(logits, axis=1, keepdims=True))
        total = jnp.sum(exponent, axis=1, keepdims=True)
        prob_ref[...] = jnp.sum(exponent * mine_ref[...], axis=1, keepdims=True) / total

    rows = in_ref[...]
    gate_w, up_w = gate_w_ref[...], up_w_ref[...]
    gate_pre = dot(rows, gate_w, NT)
    up_pre = dot(rows, up_w, NT)
    plain = plain_ref[...]
    sigmoid = 1.0 / (1.0 + jnp.exp(-gate_pre))
    silu = gate_pre * sigmoid
    act = silu * up_pre
    prob = prob_ref[...]
    act_ref[...] = (prob * act).astype(BF16)
    d_act = prob * plain
    d_gate = (d_act * up_pre * (sigmoid * (1.0 + gate_pre * (1.0 - sigmoid)))).astype(BF16)
    d_up = (d_act * silu).astype(BF16)
    dg_ref[...] = d_gate
    du_ref[...] = d_up
    d_prob = jnp.sum(act * plain, axis=1, keepdims=True)
    d_in = dot(d_gate, gate_w) + dot(d_up, up_w)

    @pl.when(step == 0)
    def _():
        dp_ref[...] = d_prob
        total_ref[...] = d_in

    @pl.when(step > 0)
    def _():
        dp_ref[...] += d_prob
        total_ref[...] += d_in

    @pl.when(step == pl.num_programs(0) - 1)
    def _():
        values = total_ref[...].astype(BF16)
        for s in range(4):
            at = slice(s * slots, (s + 1) * slots)
            (keep_ref, send_ref)[s % 2][s // 2] = dot(pick_ref[s], values[at, :], TN).astype(BF16)
            dprob_ref[s : s + 1, :] = jnp.sum(
                pick_ref[s].astype(F32) * dp_ref[at, :], axis=0, keepdims=True
            )


def expert_quarter(quarter, blocks, pick, plain, gate_w, up_w, router, mine, kept):
    tokens, width = blocks[0].shape
    hidden = gate_w.shape[0]
    tile = 256
    slots = pick.shape[1]
    rows = 4 * slots
    whole = lambda *shape: pl.BlockSpec(shape, lambda f: (0,) * len(shape))
    any_spec = pl.BlockSpec(memory_space=pl.ANY)
    pair = jax.ShapeDtypeStruct((2, tokens, width), BF16)
    tiled = pl.BlockSpec((rows, tile), lambda f: (quarter, f))
    every = pick.shape[0] * slots
    return pl.pallas_call(
        expert_kernel,
        grid=(hidden // tile,),
        in_specs=[whole(tokens, width)] * 4
        + [
            pl.BlockSpec((4, slots, tokens), lambda f: (quarter, 0, 0)),
            tiled,
            pl.BlockSpec((tile, width), lambda f: (f, 0)),
            pl.BlockSpec((tile, width), lambda f: (f, 0)),
            whole(*router.shape),
            whole(*mine.shape),
        ]
        + [any_spec] * len(kept),
        out_specs=[
            pl.BlockSpec((rows, width), lambda f: (quarter, 0)),
            tiled,
            tiled,
            tiled,
        ]
        + [whole(2, tokens, width)] * 2
        + [whole(4, tokens)],
        out_shape=[
            jax.ShapeDtypeStruct((every, width), BF16),
            jax.ShapeDtypeStruct((every, hidden), BF16),
            jax.ShapeDtypeStruct((every, hidden), BF16),
            jax.ShapeDtypeStruct((every, hidden), BF16),
            pair,
            pair,
            jax.ShapeDtypeStruct((4, tokens), F32),
        ],
        scratch_shapes=[
            pltpu.VMEM((rows, width), F32),
            pltpu.VMEM((rows, 1), F32),
            pltpu.VMEM((rows, 1), F32),
        ],
        input_output_aliases={10 + k: k for k in range(len(kept))},
        compiler_params=pltpu.CompilerParams(vmem_limit_bytes=VMEM_LIMIT),
        name="expert",
    )(*blocks, pick, plain, gate_w, up_w, router, mine, *kept)


def expert_out_kernel(pick_ref, act_ref, down_ref, keep_ref, send_ref, values_ref):
    s = pl.program_id(1)

    @pl.when(s == 0)
    def _():
        values = dot(act_ref[...], down_ref[...]).astype(BF16)
        values_ref[...] = values.reshape(values_ref.shape)

    rows = dot(pick_ref[0], values_ref[s], TN).astype(BF16)

    @pl.when(s % 2 == 0)
    def _():
        keep_ref[0, 0] = rows

    @pl.when(s % 2 == 1)
    def _():
        send_ref[0, 0] = rows


def expert_out(pick, act, down_w):
    hidden, width = down_w.shape
    owners, slots, tokens = pick.shape
    rows = 4 * slots
    block = pl.BlockSpec((1, 1, tokens, width), lambda q, s: (q, s // 2, 0, 0))
    return pl.pallas_call(
        expert_out_kernel,
        grid=(owners // 4, 4),
        in_specs=[
            pl.BlockSpec((1, slots, tokens), lambda q, s: (4 * q + s, 0, 0)),
            pl.BlockSpec((rows, hidden), lambda q, s: (q, 0)),
            pl.BlockSpec((hidden, width), lambda q, s: (0, 0)),
        ],
        out_specs=[block, block],
        out_shape=[jax.ShapeDtypeStruct((owners // 4, 2, tokens, width), BF16)] * 2,
        scratch_shapes=[pltpu.VMEM((4, slots, width), BF16)],
        compiler_params=pltpu.CompilerParams(vmem_limit_bytes=VMEM_LIMIT),
        name="expert_out",
    )(pick, act, down_w)


def cot_kernel(source_ref, c0_ref, c1_ref, c2_ref, c3_ref, pick_ref, down_ref, slot_ref, plain_ref):
    slots = pick_ref.shape[1]

    @pl.when(pl.program_id(1) == 0)
    def _():
        for s, cot_ref in enumerate((c0_ref, c1_ref, c2_ref, c3_ref)):
            slot_ref[s * slots : (s + 1) * slots, :] = dot(pick_ref[s], cot_ref[0]).astype(BF16)

    plain_ref[...] = dot(slot_ref[...], down_ref[...], NT)


def gather_cot(source, all_cot, pick, down_w):
    hidden, width = down_w.shape
    owners, slots, tokens = pick.shape
    rows = 4 * slots
    tile = hidden // 2

    def block(s):
        return pl.BlockSpec((1, tokens, width), lambda q, f, m: (m[4 * q + s], 0, 0))

    return pl.pallas_call(
        cot_kernel,
        grid_spec=pltpu.PrefetchScalarGridSpec(
            num_scalar_prefetch=1,
            grid=(owners // 4, hidden // tile),
            in_specs=[block(s) for s in range(4)]
            + [
                pl.BlockSpec((4, slots, tokens), lambda q, f, m: (q, 0, 0)),
                pl.BlockSpec((tile, width), lambda q, f, m: (f, 0)),
            ],
            out_specs=[
                pl.BlockSpec((rows, width), lambda q, f, m: (q, 0)),
                pl.BlockSpec((rows, tile), lambda q, f, m: (q, f)),
            ],
        ),
        out_shape=[
            jax.ShapeDtypeStruct((owners * slots, width), BF16),
            jax.ShapeDtypeStruct((owners * slots, hidden), F32),
        ],
        compiler_params=pltpu.CompilerParams(vmem_limit_bytes=VMEM_LIMIT),
        name="gather_cot",
    )(source, all_cot, all_cot, all_cot, all_cot, pick, down_w)


def row_grads_kernel(cuts, me_ref, left_ref, right_ref, *outs):
    pieces, own_ref = outs[:-1], outs[-1]
    product = dot(left_ref[...], right_ref[...], TN)
    mine = pl.program_id(1) == me_ref[0]

    @pl.when(mine)
    def _():
        own_ref[...] = product

    @pl.when(jnp.logical_not(mine))
    def _():
        low = product.astype(BF16)
        for k, piece_ref in enumerate(pieces):
            piece_ref[0] = low[cuts[k] : cuts[k + 1], :]


def row_grads(me, planes, left, right, shares):
    count, hidden = left.shape
    width = right.shape[1]
    piece = hidden // planes
    tile = width // 2
    cuts = [piece * sum(shares[:k]) // sum(shares) for k in range(len(shares) + 1)]
    sizes = [high - low for low, high in zip(cuts, cuts[1:])]

    def place(n, p, m):
        ahead = (p - m[0] + planes) % planes
        idle = jnp.where(m[0] == planes - 1, planes - 2, 0)
        return (jnp.where(ahead == 0, idle, ahead - 1), 0, n)

    return pl.pallas_call(
        functools.partial(row_grads_kernel, cuts),
        grid_spec=pltpu.PrefetchScalarGridSpec(
            num_scalar_prefetch=1,
            grid=(width // tile, planes),
            in_specs=[
                pl.BlockSpec((count, piece), lambda n, p, m: (0, p)),
                pl.BlockSpec((count, tile), lambda n, p, m: (0, n)),
            ],
            out_specs=[pl.BlockSpec((1, size, tile), place) for size in sizes]
            + [pl.BlockSpec((piece, tile), lambda n, p, m: (0, n))],
        ),
        out_shape=[jax.ShapeDtypeStruct((planes - 1, size, width), BF16) for size in sizes]
        + [jax.ShapeDtypeStruct((piece, width), F32)],
        compiler_params=pltpu.CompilerParams(vmem_limit_bytes=VMEM_LIMIT),
        name="row_grads",
    )(me.reshape(1).astype(jnp.int32), left, right)


def weight_grad_kernel(planes, core_ref, left_ref, *refs):
    rights, (keep_ref, send_ref) = refs[:-2], refs[-2:]
    rows_e, pairs, size, tile = keep_ref.shape
    tokens = left_ref.shape[0] // planes
    count = len(rights) // planes
    size = size // count
    for k in range(count):
        product = sum(
            dot(left_ref[r * tokens : (r + 1) * tokens, :], rights[k * planes + r][...], TN)
            for r in range(planes)
        )
        split_rows = product.astype(BF16).reshape(rows_e, pairs, 2, size, tile)
        at = slice(k * size, (k + 1) * size)

        @pl.when(core_ref[0] == 0)
        def _():
            keep_ref[:, :, at, :] = split_rows[:, :, 0]
            send_ref[:, :, at, :] = split_rows[:, :, 1]

        @pl.when(core_ref[0] != 0)
        def _():
            keep_ref[:, :, at, :] = split_rows[:, :, 1]
            send_ref[:, :, at, :] = split_rows[:, :, 0]


def weight_grads(left, *rights):
    rows_e, rows_d = lax.axis_size("expert"), lax.axis_size("dp")
    planes = len(rights[0])
    total, part = left.shape
    width = rights[0][0].shape[1]
    tile = width // 4
    size = part // (rows_e * rows_d) * len(rights)
    core = (lax.axis_index("dp") % 2).reshape(1).astype(jnp.int32)
    block = pl.BlockSpec((rows_e, rows_d // 2, size, tile), lambda n, m: (0, 0, 0, n))
    return pl.pallas_call(
        functools.partial(weight_grad_kernel, planes),
        grid_spec=pltpu.PrefetchScalarGridSpec(
            num_scalar_prefetch=1,
            grid=(width // tile,),
            in_specs=[pl.BlockSpec((total, part), lambda n, m: (0, 0))]
            + [pl.BlockSpec((total // planes, tile), lambda n, m: (0, n))] * (planes * len(rights)),
            out_specs=[block, block],
        ),
        out_shape=[jax.ShapeDtypeStruct((rows_e, rows_d // 2, size, width), BF16)] * 2,
        compiler_params=pltpu.CompilerParams(vmem_limit_bytes=VMEM_LIMIT),
        name="weight_grads",
    )(core, left, *[array for right in rights for array in right])


def add_rows_kernel(counts, *refs):
    own_ref, parts, out_ref = refs[0], refs[1:-1], refs[-1]
    step = pl.program_id(0)
    at = 0
    for count, ref in zip(counts, parts):

        @pl.when((step >= at) & (step < at + count))
        def _():
            out_ref[...] = own_ref[...] + ref[...].astype(F32)

        at += count


def add_rows(own, parts):
    width = own.shape[1]
    step = math.gcd(*(p.shape[0] for p in parts))
    counts = [p.shape[0] // step for p in parts]
    starts = [sum(counts[:k]) for k in range(len(counts))]

    def spec(start, count):
        return pl.BlockSpec((step, width), lambda i: (jnp.clip(i - start, 0, count - 1), 0))

    rows = pl.BlockSpec((step, width), lambda i: (i, 0))
    return pl.pallas_call(
        functools.partial(add_rows_kernel, counts),
        grid=(own.shape[0] // step,),
        in_specs=[rows] + [spec(a, c) for a, c in zip(starts, counts)],
        out_specs=rows,
        out_shape=jax.ShapeDtypeStruct(own.shape, F32),
        compiler_params=pltpu.CompilerParams(vmem_limit_bytes=VMEM_LIMIT),
        name="add_rows",
    )(own, *parts)


def swap(value, axis, bit):
    return lax.ppermute(value, axis, [(i, i ^ bit) for i in range(lax.axis_size(axis))])


def plus(*values):
    return sum(v.astype(F32) for v in values).astype(values[0].dtype)


ORDER = [
    (i, j) for x in (0, 2) for z in (0, 2) for i in (z, z + 1) for j in (x, x + 1)
]


def fence(*values):
    return lax.optimization_barrier(values)


def split(values, axis_name, bit, at):
    mine = (lax.axis_index(axis_name) // bit) % 2

    def half(index):
        parts = []
        for value in values:
            shape = value.shape
            pairs = value.reshape(shape[:at] + (shape[at] // 2, 2) + shape[at + 1 :])
            parts.append(lax.dynamic_index_in_dim(pairs, index, at + 1, keepdims=False))
        return plus(*parts)

    return half(mine), half(1 - mine)


STAGES = (("dp", 1, 1), ("dp", 2, 1), ("expert", 1, 0), ("expert", 2, 0))


class RowScatter:
    def __init__(self, keep, send):
        self.keep, self.send = keep, send
        self.stage = 0

    def start(self):
        axis, bit, at = STAGES[self.stage]
        if self.stage:
            self.keep, self.send = split(self.parts, axis, bit, at)
        self.stage += 1
        return swap(self.send, axis, bit)

    def finish(self, received):
        self.parts = (self.keep, received)

    def result(self):
        value = plus(*self.parts)
        return value.reshape(value.shape[-2:])


def shards(
    prompt_in,
    cont_in,
    prompt_cot,
    cont_cot,
    prompt_routes,
    cont_routes,
    prefix,
    attn_gain,
    query_gain,
    key_gain,
    ffn_gain,
    w_query,
    w_key,
    w_value,
    w_output,
    w_router,
    expert_gate,
    expert_up,
    expert_down,
):
    prompt_dev, width = prompt_in.shape[1:]
    cont_len = cont_in.shape[2]
    tokens = prompt_dev + cont_len
    head_dim = width // HEADS
    top_count = prompt_routes.shape[2]
    expert_count = w_router.shape[1]
    hidden = expert_gate.shape[1]
    planes = lax.axis_size("context")
    me = lax.axis_index("context")
    rows_e, rows_d = lax.axis_size("expert"), lax.axis_size("dp")
    owners = rows_e * rows_d
    my_expert = lax.axis_index("expert") * rows_d + lax.axis_index("dp")
    prompt_total = prompt_dev * planes
    most_prompt = 9 * prompt_dev * top_count // (8 * expert_count)
    most_cont = 9 * cont_len * top_count // (8 * expert_count)
    slots = (most_prompt + most_cont + 15) // 16 * 16
    part = width // planes
    out_group = width // (rows_e * planes)

    def shift(value, r):
        return lax.ppermute(value, "context", [(i, (i + r) % planes) for i in range(planes)])

    def block(value, r):
        return lax.dynamic_slice_in_dim(value, ((me + r) % planes) * part, part, axis=1)

    def out_part(value, r):
        at = ((me + r) % planes) * out_group
        return jnp.concatenate(
            [
                lax.dynamic_slice_in_dim(value, e * planes * out_group + at, out_group, axis=1)
                for e in range(rows_e)
            ],
            axis=1,
        )

    def placed(blocks):
        full = jnp.zeros((tokens, width), blocks[0].dtype)
        for r, piece in enumerate(blocks):
            full = lax.dynamic_update_slice_in_dim(full, piece, ((me + r) % planes) * part, axis=1)
        return full

    others = range(1, planes)

    x_low = jnp.concatenate([prompt_in[0], cont_in[0, 0]], axis=0)
    x_rows = x_low.astype(F32)
    inverse = lax.rsqrt(jnp.mean(x_rows * x_rows, axis=-1) + EPSILON)
    x_blocks = [block(x_low, 0)] + [shift(block(x_low, r), r) for r in others]
    inverses = [inverse] + [shift(inverse, r) for r in others]
    gain_part = attn_gain.astype(F32)
    normed_blocks = [
        (piece.astype(F32) * inv[:, None] * gain_part).astype(BF16)
        for piece, inv in zip(x_blocks, inverses)
    ]

    def gathered(value, axis):
        shape = list(value.shape)
        shape[axis] = shape[axis] * planes
        full = jnp.zeros(shape, value.dtype)
        for r in range(planes):
            piece = shift(value, r) if r else value
            at = ((me - r) % planes) * value.shape[axis]
            full = lax.dynamic_update_slice_in_dim(full, piece, at, axis=axis)
        return full

    gains_in = jnp.stack([attn_gain, query_gain, key_gain, ffn_gain])

    d_out_low = jnp.concatenate([prompt_cot[0], cont_cot[0, 0]], axis=0)
    routes = jnp.concatenate([prompt_routes[0], cont_routes[0, 0]], axis=0)
    named = sum(
        (routes[:, k : k + 1] == jnp.arange(expert_count, dtype=jnp.int32)[None, :]).astype(F32)
        for k in range(top_count)
    )
    all_cot = lax.all_gather(d_out_low, PLANE, axis=0, tiled=True)

    start_len = prefix[0, 0]
    prompt_pos = me * prompt_dev + jnp.arange(prompt_dev, dtype=jnp.int32)
    positions = jnp.concatenate([prompt_pos, start_len + jnp.arange(cont_len, dtype=jnp.int32)])
    half_index = jnp.arange(head_dim // 2, dtype=F32)
    angles = positions.astype(F32)[:, None] * (10000.0 ** (-2.0 * half_index / head_dim))[None, :]
    cosine = jnp.cos(angles)
    sine = jnp.sin(angles)
    cosine = jnp.concatenate([cosine, cosine], axis=1)
    sine = jnp.concatenate([-sine, sine], axis=1)
    meta = jnp.stack([me * prompt_dev, start_len]).astype(jnp.int32)

    def project(pieces, weight):
        products = [dot(pieces[r], weight).astype(BF16) for r in others]
        fenced = fence(*pieces, *products)
        pieces, products = fenced[:planes], fenced[planes:]
        sent = [shift(product, planes - r) for r, product in zip(others, products)]
        return [dot(pieces[0], weight)] + sent, pieces

    def products(weight):
        return [dot(normed_blocks[r], weight).astype(BF16) for r in others]

    def shift_back(values):
        return [shift(v, planes - r) for r, v in zip(others, values)]

    key_low, value_low, named, gains_in, w_router, d_out_low, *normed_blocks = fence(
        products(w_key), products(w_value), named, gains_in, w_router, d_out_low, *normed_blocks
    )
    key_got, value_got = shift_back(key_low), shift_back(value_low)
    query_low = products(w_query)
    key_own, value_own = dot(normed_blocks[0], w_key), dot(normed_blocks[0], w_value)
    member = lax.all_to_all(named.T, PLANE, split_axis=0, concat_axis=0, tiled=True)
    gains = gathered(gains_in, 1)
    full_router = gathered(w_router, 0)
    key_got, value_got, query_low, key_own, value_own, member, gains, full_router, *normed_blocks = fence(
        key_got, value_got, query_low, key_own, value_own, member, gains, full_router, *normed_blocks
    )
    gains = gains.astype(F32)
    gain_attn, gain_query, gain_key, gain_ffn = [gains[i : i + 1] for i in range(4)]
    query_parts = [dot(normed_blocks[0], w_query)] + shift_back(query_low)
    key_raw, key_low = qk_post([key_own, *key_got], gain_key, cosine, sine)
    value_low = plus(value_own, *value_got).astype(BF16)
    query_raw, query_low = qk_post(query_parts, gain_query, cosine, sine)

    def with_prompt(rows):
        full = jnp.zeros((prompt_total + cont_len, width), BF16)
        full = lax.dynamic_update_slice_in_dim(full, rows[prompt_dev:], prompt_total, axis=0)
        for r in range(planes):
            piece = rows[:prompt_dev]
            if r:
                piece = shift(piece, planes - r)
            full = lax.dynamic_update_slice_in_dim(
                full, piece, ((me + r) % planes) * prompt_dev, axis=0
            )
        return full

    key_set = with_prompt(key_low)
    value_set = with_prompt(value_low)
    (attended,) = attention_call(
        attend_kernel,
        "attend",
        [query_low, key_set, value_set],
        [jax.ShapeDtypeStruct((tokens, width), BF16)],
        meta,
        prompt_dev,
        prompt_total,
    )

    attended_blocks = [block(attended, 0)] + [shift(block(attended, r), r) for r in others]
    mixed_rows = x_rows + sum(p.astype(F32) for p in project(attended_blocks, w_output)[0])
    inverse2 = lax.rsqrt(jnp.mean(mixed_rows * mixed_rows, axis=-1, keepdims=True) + EPSILON)
    normed2_low = (mixed_rows * inverse2 * gain_ffn).astype(BF16)

    normed_low = (x_rows * inverse[:, None] * gain_attn).astype(BF16)

    logits = dot(normed2_low, full_router)
    shifted = jnp.exp(logits - jnp.max(logits, axis=1, keepdims=True))
    router_probs = shifted / jnp.sum(shifted, axis=1, keepdims=True)

    my_e, my_d = lax.axis_index("expert"), lax.axis_index("dp")
    source = jnp.stack([(my_e ^ i) * rows_d + (my_d ^ j) for i, j in ORDER]).astype(jnp.int32)
    member = jnp.take(member, source, axis=0)

    def ranks(m):
        count = m.shape[1]
        before = jnp.triu(jnp.ones((count, count), BF16), 1)
        return dot(m.astype(BF16), before)

    slot_of = jnp.concatenate(
        [ranks(member[:, :prompt_dev]), ranks(member[:, prompt_dev:]) + most_prompt], axis=1
    )
    slot_of = jnp.where(member > 0, slot_of, -1.0)
    pick = (
        slot_of[:, None, :] == jnp.arange(slots, dtype=F32)[None, :, None]
    ).astype(BF16)
    gate_w, up_w, down_w = expert_gate[0], expert_up[0], expert_down[0]
    mine = (jnp.arange(expert_count, dtype=jnp.int32) == my_expert).astype(F32)[None, :]

    def z1(v):
        return swap(v, "expert", 1)

    def z2(v):
        return swap(v, "expert", 2)

    def core(v):
        return swap(v, "dp", 1)

    def across(v):
        return swap(v, "dp", 2)

    b0, all_cot, normed_low = fence(normed2_low, all_cot, normed_low)
    b1, b2, x0, c0 = z1(b0), z2(b0), across(b0), core(b0)
    normed_sent = [shift(out_part(normed_low, r), r) for r in others]
    attended_sent = [shift(out_part(attended, r), r) for r in others]
    all_cot = all_cot.reshape(owners, tokens, width)
    slot_cot, d_act_plain = gather_cot(source, all_cot, pick, down_w)
    b1, b2, x0, c0, d_act_plain, *rest = fence(
        b1, b2, x0, c0, d_act_plain, *normed_sent, *attended_sent
    )
    normed_out = jnp.concatenate([out_part(normed_low, 0), *rest[: planes - 1]], axis=0)
    attended_out = jnp.concatenate([out_part(attended, 0), *rest[planes - 1 :]], axis=0)
    b3, x1, c1, x0c = z1(b2), across(b1), core(b1), core(x0)
    b3, x1, c1, x0c = fence(b3, x1, c1, x0c)

    def quarter(q, blocks, kept):
        outs = expert_quarter(q, blocks, pick, d_act_plain, gate_w, up_w, full_router, mine, kept)
        return outs[:4], outs[4], outs[5], outs[6]

    x2, c2, c3, x1c = across(b2), core(b2), core(b3), core(x1)
    kept, keep0, send0, dprob0 = quarter(0, (b0, c0, b1, c1), ())
    x2, c2, c3, x1c, *kept = fence(x2, c2, c3, x1c, *kept)
    x3, x2c = across(b3), core(x2)
    kept, keep2, send2, dprob2 = quarter(2, (x0, x0c, x1, x1c), kept)
    x3, x2c, send2, *kept = fence(x3, x2c, send2, *kept)
    x3c, near2, near0 = core(x3), core(send2), core(send0)
    x3c, near2, near0, *kept = fence(x3c, near2, near0, *kept)
    got21 = across(add_blocks((keep2, 1), (near2, 1)))
    pair20 = add_blocks((keep2, 0), (near2, 0))
    kept, keep3, send3, dprob3 = quarter(3, (x2, x2c, x3, x3c), kept)
    got21, pair20, send3, *kept = fence(got21, pair20, send3, *kept)
    got20, near3 = across(pair20), core(send3)
    kept, keep1, send1, dprob1 = quarter(1, (b2, c2, b3, c3), kept)
    got20, near3, send1, *kept = fence(got20, near3, send1, *kept)
    slot_in, act_low, d_gate, d_up = kept

    piece = hidden // planes

    def send_rows(values):
        return [shift(values[r - 1], r) for r in others]

    first_got, near1 = z1(add_blocks((keep0, 1), (near0, 1), got21)), core(send1)
    got31 = across(add_blocks((keep3, 1), (near3, 1)))
    pair30 = add_blocks((keep3, 0), (near3, 0))
    *gate_low, gate_own = row_grads(me, planes, d_gate, slot_in, (1, 1))
    towards = jnp.arange(owners, dtype=jnp.int32)
    i_of, j_of = (towards // rows_d) ^ my_e, (towards % rows_d) ^ my_d
    place = (j_of // 2) * 8 + (i_of // 2) * 4 + (i_of % 2) * 2 + j_of % 2
    token_dprob = jnp.take(
        jnp.concatenate([dprob0, dprob1, dprob2, dprob3], axis=0), place, axis=0
    )
    first_got, got31, near1, gate_own, pair30, d_up, slot_in, token_dprob, *gate_low = fence(
        first_got, got31, near1, gate_own, pair30, d_up, slot_in, token_dprob, *gate_low
    )
    dprobs = lax.all_to_all(token_dprob, PLANE, split_axis=0, concat_axis=0, tiled=True).T
    second_got, got30 = z1(add_blocks((keep1, 1), (near1, 1), got31)), across(pair30)
    gate_a = send_rows(gate_low[0])
    *up_low, up_own = row_grads(me, planes, d_up, slot_in, (2, 4, 2))
    second_got, got30, dprobs, act_low, up_own, gate_b, up_0, up_1, up_2, *gate_a = fence(
        second_got, got30, dprobs, act_low, up_own, gate_low[1], *up_low, *gate_a
    )
    far_got = z2(add_blocks((keep1, 0), (near1, 0), got30, second_got))
    gate_b, up_a = send_rows(gate_b), send_rows(up_0)
    out_keep, out_send = expert_out(pick, act_low, down_w)
    far_got, act_low, out_keep, out_send, *rest = fence(
        far_got, act_low, out_keep, out_send, *gate_b, *up_a
    )
    gate_b, up_a = rest[: planes - 1], rest[planes - 1 :]

    out_near = core(out_send)
    d_mixed, branch_low, dlogit_low, ffn_gain_grad = norm_back(
        [(keep0, 0), (near0, 0), got20, first_got, far_got],
        d_out_low,
        mixed_rows,
        gain_ffn,
        router_probs,
        dprobs,
        full_router,
    )
    router_grad = dot(normed2_low, dlogit_low, TN)
    branch_low, act_low, out_near = fence(branch_low, act_low, out_near)

    def out_sum(q, i):
        return add_blocks((out_keep, q, i), (out_near, q, i))

    sent = [shift(branch_low, r) for r in others]
    out_got31, out_got30 = across(out_sum(3, 1)), across(out_sum(3, 0))
    *down_low, down_own = row_grads(me, planes, act_low, slot_cot, (1, 4, 3))
    out_got31, out_keep, out_near, down_own, down_0, down_1, down_2, branch_low, *sent = fence(
        out_got31, out_keep, out_near, down_own, *down_low, branch_low, *sent
    )
    branches = [branch_low, *sent]
    blocks_low = [dot(branches[r], w_output, NT).astype(BF16) for r in others]
    d_att_blocks = [shift(v, planes - r) for r, v in zip(others, blocks_low)]
    d_att_own = dot(branches[0], w_output, NT).astype(BF16)
    out_second = add_blocks((out_keep, 1, 1), (out_near, 1, 1), out_got31)
    out21 = out_sum(2, 1)
    d_att_own, up_1, out_second, out_got30, out21, gate_own, branch_low, *d_att_blocks = fence(
        d_att_own, up_1, out_second, out_got30, out21, gate_own, branch_low, *d_att_blocks
    )
    branches[0] = branch_low
    d_attended = placed([d_att_own, *d_att_blocks])

    out_got21, out_second = across(out21), z1(out_second)
    up_b = send_rows(up_1)
    output_keep, output_send = weight_grads(attended_out, branches)
    d_queries, d_keys, d_values_own, d_keys_low, d_values_low = attention_call(
        attend_back_kernel,
        "attend_back",
        [query_low, key_set, value_set, d_attended],
        [
            jax.ShapeDtypeStruct((tokens, width), F32),
            jax.ShapeDtypeStruct((tokens, width), F32),
            jax.ShapeDtypeStruct((tokens, width), F32),
            jax.ShapeDtypeStruct((prompt_total, width), BF16),
            jax.ShapeDtypeStruct((prompt_total, width), BF16),
        ],
        meta,
        prompt_dev,
        prompt_total,
        [pltpu.VMEM((prompt_total, head_dim), F32)],
    )
    out20 = out_sum(2, 0)
    (
        out_got21, out_second, output_keep, output_send, out20,
        d_queries, d_keys, d_values_own, d_keys_low, d_values_low, *up_b,
    ) = fence(
        out_got21, out_second, output_keep, output_send, out20,
        d_queries, d_keys, d_values_own, d_keys_low, d_values_low, *up_b,
    )
    output_rows = RowScatter(output_keep, output_send)

    def prompt_sent(rows):
        return [
            shift(
                lax.dynamic_slice_in_dim(
                    rows, ((me + r) % planes) * prompt_dev, prompt_dev, axis=0
                ),
                r,
            )
            for r in others
        ]

    value_prompt, key_prompt = prompt_sent(d_values_low), prompt_sent(d_keys_low)
    out_got20, output_got = across(out20), output_rows.start()
    d_query_low, query_gain_grad = qk_post_back(d_queries, query_raw, gain_query, cosine, sine)
    half = tokens // 2
    query_got_a = [shift(d_query_low[:half], r) for r in others]
    out_far = add_blocks((out_keep, 1, 0), (out_near, 1, 0), out_got30, out_second)
    out_first = z1(add_blocks((out_keep, 0, 1), (out_near, 0, 1), out_got21))
    out_got20, output_got, out_far, out_first, d_query_low, gate_own, *rest = fence(
        out_got20, output_got, out_far, out_first, d_query_low, gate_own,
        *value_prompt, *key_prompt, *query_got_a,
    )
    output_rows.finish(output_got)
    value_prompt, key_prompt, query_got_a = (
        rest[k * (planes - 1) : (k + 1) * (planes - 1)] for k in range(3)
    )
    d_value_low = value_rows_low(d_values_own, value_prompt)

    def spread(low):
        return [shift(low, r) for r in others]

    def total(own, *parts):
        for k in range(planes - 1):
            own = add_rows(own, [p[k] for p in parts])
        return own

    d_value_low, *key_prompt = fence(d_value_low, *key_prompt)
    got = spread(d_value_low) + [shift(d_query_low[half:], r) for r in others]
    out_far_a, output_got = z2(out_far[:half]), output_rows.start()
    d_key_low, key_gain_grad = qk_post_back(
        d_keys, key_raw, gain_key, cosine, sine, key_prompt
    )
    gate_grad = total(gate_own, gate_a, gate_b)
    out_far_a, out_far_b, output_got, d_key_low, gate_grad, *rest = fence(
        out_far_a, out_far[half:], output_got, d_key_low, gate_grad, *got
    )
    d_values = rest[: planes - 1]
    d_query_got = [
        jnp.concatenate([top, bottom], axis=0)
        for top, bottom in zip(query_got_a, rest[planes - 1 :])
    ]
    output_rows.finish(output_got)

    got, output_got, out_far_b = spread(d_key_low), output_rows.start(), z2(out_far_b)
    value_pair = weight_grads(normed_out, [d_value_low, *d_values])
    query_pair = weight_grads(normed_out, [d_query_low, *d_query_got])
    partial = [
        dot(d_values[k], w_value, NT) + dot(d_query_got[k], w_query, NT) for k in range(planes - 1)
    ]
    output_got, out_far_b, value_pair, query_pair, up_2, down_0, *rest = fence(
        output_got, out_far_b, value_pair, query_pair, up_2, down_0, *got, *partial
    )
    d_key_got, partial = rest[: planes - 1], rest[planes - 1 :]
    output_rows.finish(output_got)
    value_rows, query_rows = RowScatter(*value_pair), RowScatter(*query_pair)
    out_rows = (
        mixed_rows
        + plus(out_keep[0, 0].astype(F32), out_near[0, 0])
        + out_got20.astype(F32)
        + out_first.astype(F32)
        + jnp.concatenate([out_far_a, out_far_b], axis=0).astype(F32)
    )

    value_got, query_got = value_rows.start(), query_rows.start()
    key_pair = weight_grads(normed_out, [d_key_low, *d_key_got])
    blocks_low = [
        (partial[k] + dot(d_key_got[k], w_key, NT)).astype(BF16) for k in range(planes - 1)
    ]
    value_got, query_got, key_pair, d_key_low, *blocks_low = fence(
        value_got, query_got, key_pair, d_key_low, *blocks_low
    )
    value_rows.finish(value_got)
    query_rows.finish(query_got)
    key_rows = RowScatter(*key_pair)

    d_normed_got = [shift(v, planes - r) for r, v in zip(others, blocks_low)]
    value_got, output_got, key_got = value_rows.start(), output_rows.start(), key_rows.start()
    up_c, down_a = send_rows(up_2), send_rows(down_0)
    d_normed_own = (
        dot(d_value_low, w_value, NT) + dot(d_query_low, w_query, NT) + dot(d_key_low, w_key, NT)
    )
    value_got, output_got, key_got, d_normed_own, down_1, *rest = fence(
        value_got, output_got, key_got, d_normed_own, down_1, *d_normed_got, *up_c, *down_a
    )
    d_normed_got, up_c, down_a = (rest[k * (planes - 1) : (k + 1) * (planes - 1)] for k in range(3))
    value_rows.finish(value_got)
    output_rows.finish(output_got)
    key_rows.finish(key_got)

    query_got, value_got = query_rows.start(), value_rows.start()
    down_b = send_rows(down_1)
    d_normed = placed([d_normed_own] + [p.astype(F32) for p in d_normed_got])
    scaled = gain_attn * d_normed
    centre = jnp.mean(scaled * x_rows, axis=-1, keepdims=True)
    inv = inverse[:, None]
    d_x = d_mixed + inv * scaled - x_rows * (inv**3 * centre)
    attn_gain_grad = jnp.sum(d_normed * x_rows * inv, axis=0)
    small_grads = jnp.concatenate(
        [
            jnp.stack(
                [attn_gain_grad, query_gain_grad[0], key_gain_grad[0], ffn_gain_grad[0]], axis=1
            ),
            router_grad,
        ],
        axis=1,
    )
    query_got, value_got, d_x, small_grads, down_2, *down_b = fence(
        query_got, value_got, d_x, small_grads, down_2, *down_b
    )
    query_rows.finish(query_got)
    value_rows.finish(value_got)

    def laid(own, *parts):
        for k in range(planes - 1):
            own = own + jnp.concatenate([p[k] for p in parts], axis=0).astype(F32)
        return own

    key_got, query_got, value_got = key_rows.start(), query_rows.start(), value_rows.start()
    by_plane = small_grads.reshape(rows_e, planes, out_group, small_grads.shape[1])

    def plane_rows(r):
        return lax.dynamic_index_in_dim(by_plane, (me + r) % planes, 1, False)

    small_sum = plus(plane_rows(0), *[shift(plane_rows(r), r) for r in others])
    down_c = send_rows(down_2)
    up_grad = laid(up_own, up_a, up_b, up_c)
    key_got, query_got, value_got, small_sum, up_grad, *down_c = fence(
        key_got, query_got, value_got, small_sum, up_grad, *down_c
    )
    key_rows.finish(key_got)
    query_rows.finish(query_got)
    value_rows.finish(value_got)

    key_got, query_got = key_rows.start(), query_rows.start()
    small_rows = RowScatter(
        *split([small_sum.reshape(rows_e, rows_d, -1, small_sum.shape[-1])], *STAGES[0])
    )
    for _ in range(2):
        small_rows.finish(small_rows.start())
    down_grad = laid(down_own, down_a, down_b, down_c)
    key_got, query_got, small_rows.parts, down_grad = fence(
        key_got, query_got, small_rows.parts, down_grad
    )
    key_rows.finish(key_got)
    query_rows.finish(query_got)
    key_rows.finish(key_rows.start())
    for _ in range(2):
        small_rows.finish(small_rows.start())
    small_grads = small_rows.result()
    return (
        out_rows[:prompt_dev].astype(BF16)[None],
        out_rows[prompt_dev:].astype(BF16)[None, None],
        d_x[:prompt_dev][None],
        d_x[prompt_dev:][None, None],
        small_grads[:, 0],
        small_grads[:, 1],
        small_grads[:, 2],
        small_grads[:, 3],
        query_rows.result().astype(F32),
        key_rows.result().astype(F32),
        value_rows.result().astype(F32),
        output_rows.result().astype(F32),
        small_grads[:, 4:],
        gate_grad[None],
        up_grad[None],
        down_grad[None],
    )


def solution(mesh):
    rows = P(("expert", "dp"), "context", None)
    conts = P(("expert", "dp"), "context", None, None)
    experts = P(("expert", "dp"), None, None)
    everywhere = ("expert", "context", "dp")
    in_specs = (
        (rows, conts, rows, conts, rows, conts, P(("expert", "dp"), "context"))
        + (P("context"),) * 4
        + (P("context", None),) * 5
        + (experts,) * 3
    )
    out_specs = (
        (rows, conts, rows, conts)
        + (P(everywhere),) * 4
        + (P(everywhere, None),) * 5
        + (rows,) * 3
    )
    return jax.shard_map(shards, mesh=mesh, in_specs=in_specs, out_specs=out_specs, check_vma=False)
```

```python
import functools
import math

import jax
import jax.numpy as jnp
from jax import lax
from jax.experimental import pallas as pl
from jax.experimental.pallas import tpu as pltpu
from jax.sharding import PartitionSpec as P

HEADS = 16
EPSILON = 1e-05
NEG_LARGE = -1e30
F32 = jnp.float32
BF16 = jnp.bfloat16
PLANE = ("expert", "dp")
VMEM_LIMIT = 48 * 1024 * 1024


def dot(left, right, dims=((1,), (0,)), out=F32):
    return lax.dot_general(left, right, (dims, ((), ())), preferred_element_type=out)


NT = ((1,), (1,))
TN = ((0,), (0,))


def post_kernel(count, *refs):
    parts, (gain_ref, cos_ref, sin_ref, raw_ref, low_ref) = refs[:count], refs[count:]
    raw = parts[0][...]
    for part in parts[1:]:
        raw = raw + part[...].astype(F32)
    raw_ref[...] = raw
    inverse = lax.rsqrt(jnp.mean(raw * raw, axis=-1, keepdims=True) + EPSILON)
    scaled = raw * inverse * gain_ref[...]
    cosine, sine = cos_ref[...], sin_ref[...]
    head = cosine.shape[1]
    for h in range(raw.shape[1] // head):
        piece = scaled[:, h * head : (h + 1) * head]
        turned = piece * cosine + pltpu.roll(piece, head // 2, 1) * sine
        low_ref[:, h * head : (h + 1) * head] = turned.astype(BF16)


def qk_post(parts, gain, cosine, sine):
    rows, width = parts[0].shape
    head = cosine.shape[1]
    step = 64
    row = lambda w: pl.BlockSpec((step, w), lambda i: (i, 0))
    return pl.pallas_call(
        functools.partial(post_kernel, len(parts)),
        grid=(rows // step,),
        in_specs=[row(width)] * len(parts)
        + [pl.BlockSpec((1, width), lambda i: (0, 0)), row(head), row(head)],
        out_specs=[row(width), row(width)],
        out_shape=[
            jax.ShapeDtypeStruct((rows, width), F32),
            jax.ShapeDtypeStruct((rows, width), BF16),
        ],
        compiler_params=pltpu.CompilerParams(vmem_limit_bytes=VMEM_LIMIT),
        name="qk_post",
    )(*parts, gain, cosine, sine)


def post_back_kernel(grad_ref, raw_ref, gain_ref, cos_ref, sin_ref, *refs):
    got, (low_ref, gain_grad_ref, sum_ref) = refs[:-3], refs[-3:]
    sum_ref[...] = grad_ref[...]
    if got:

        @pl.when(pl.program_id(0) == 0)
        def _():
            for ref in got:
                sum_ref[...] += ref[...].astype(F32)

    raw = raw_ref[...]
    inverse = lax.rsqrt(jnp.mean(raw * raw, axis=-1, keepdims=True) + EPSILON)
    cosine, sine = cos_ref[...], sin_ref[...]
    head = cosine.shape[1]
    pieces = []
    for h in range(raw.shape[1] // head):
        piece = sum_ref[:, h * head : (h + 1) * head]
        pieces.append(piece * cosine - pltpu.roll(piece, head // 2, 1) * sine)
    grad = jnp.concatenate(pieces, axis=1)
    scaled = grad * gain_ref[...]
    centre = jnp.mean(scaled * raw, axis=-1, keepdims=True)
    low_ref[...] = (inverse * scaled - raw * (inverse * inverse * inverse * centre)).astype(BF16)
    total = jnp.sum(grad * raw * inverse, axis=0, keepdims=True)

    @pl.when(pl.program_id(0) == 0)
    def _():
        gain_grad_ref[...] = total

    @pl.when(pl.program_id(0) > 0)
    def _():
        gain_grad_ref[...] += total


def qk_post_back(grad, raw, gain, cosine, sine, got=()):
    rows, width = raw.shape
    head = cosine.shape[1]
    step = got[0].shape[0] if got else 64
    row = lambda w: pl.BlockSpec((step, w), lambda i: (i, 0))
    whole = pl.BlockSpec((1, width), lambda i: (0, 0))
    return pl.pallas_call(
        post_back_kernel,
        grid=(rows // step,),
        in_specs=[row(width), row(width), whole, row(head), row(head)]
        + [pl.BlockSpec((step, width), lambda i: (0, 0))] * len(got),
        out_specs=[row(width), whole],
        out_shape=[
            jax.ShapeDtypeStruct((rows, width), BF16),
            jax.ShapeDtypeStruct((1, width), F32),
        ],
        scratch_shapes=[pltpu.VMEM((step, width), F32)],
        compiler_params=pltpu.CompilerParams(vmem_limit_bytes=VMEM_LIMIT),
        name="qk_post_back",
    )(grad, raw, gain, cosine, sine, *got)


def row_specs(items, step):
    pairs = [item if isinstance(item, tuple) else (item,) for item in items]

    def spec(array, at):
        width = array.shape[-1]
        return pl.BlockSpec((None,) * len(at) + (step, width), lambda i: at + (i, 0))

    return [p[0] for p in pairs], [spec(p[0], p[1:]) for p in pairs]


def add_blocks(*items):
    return plus(*[item[0][item[1:]] if isinstance(item, tuple) else item for item in items])


def norm_back_kernel(count, *refs):
    parts = refs[:count]
    (
        d_out_ref, mixed_ref, gain_ref, probs_ref, d_probs_ref, router_ref,
        d_mixed_ref, branch_ref, d_logit_ref, gain_grad_ref,
    ) = refs[count:]
    probs, d_probs = probs_ref[...], d_probs_ref[...]
    centre = jnp.sum(probs * d_probs, axis=1, keepdims=True)
    d_logit = (probs * (d_probs - centre)).astype(BF16)
    d_logit_ref[...] = d_logit
    grad = dot(d_logit, router_ref[...], NT)
    for part in parts:
        grad = grad + part[...].astype(F32)
    mixed = mixed_ref[...]
    inverse = lax.rsqrt(jnp.mean(mixed * mixed, axis=-1, keepdims=True) + EPSILON)
    scaled = grad * gain_ref[...]
    centre = jnp.mean(scaled * mixed, axis=-1, keepdims=True)
    d_mixed = (
        d_out_ref[...].astype(F32)
        + inverse * scaled
        - mixed * (inverse * inverse * inverse * centre)
    )
    d_mixed_ref[...] = d_mixed
    branch_ref[...] = d_mixed.astype(BF16)
    total = jnp.sum(grad * mixed * inverse, axis=0, keepdims=True)

    @pl.when(pl.program_id(0) == 0)
    def _():
        gain_grad_ref[...] = total

    @pl.when(pl.program_id(0) > 0)
    def _():
        gain_grad_ref[...] += total


def norm_back(parts, d_out, mixed, gain, probs, d_probs, router):
    rows, width = mixed.shape
    experts = probs.shape[1]
    step = 64
    row = lambda w: pl.BlockSpec((step, w), lambda i: (i, 0))
    whole = lambda *shape: pl.BlockSpec(shape, lambda i: (0, 0))
    parts, specs = row_specs(parts, step)
    return pl.pallas_call(
        functools.partial(norm_back_kernel, len(parts)),
        grid=(rows // step,),
        in_specs=specs
        + [row(width)] * 2
        + [whole(1, width), row(experts), row(experts), whole(width, experts)],
        out_specs=[row(width), row(width), row(experts), whole(1, width)],
        out_shape=[
            jax.ShapeDtypeStruct((rows, width), F32),
            jax.ShapeDtypeStruct((rows, width), BF16),
            jax.ShapeDtypeStruct((rows, experts), BF16),
            jax.ShapeDtypeStruct((1, width), F32),
        ],
        compiler_params=pltpu.CompilerParams(vmem_limit_bytes=VMEM_LIMIT),
        name="norm_back",
    )(*parts, d_out, mixed, gain, probs, d_probs, router)


def read_mask(meta_ref, rows, keys, prompt_dev, prompt_total):
    row = lax.broadcasted_iota(jnp.int32, (rows, keys), 0)
    key = lax.broadcasted_iota(jnp.int32, (rows, keys), 1)
    is_prompt_row = row < prompt_dev
    is_prompt_key = key < prompt_total
    prompt_limit = jnp.where(is_prompt_row, meta_ref[0] + row + 1, meta_ref[1])
    own_limit = jnp.where(is_prompt_row, 0, row - prompt_dev + 1)
    limit = jnp.where(is_prompt_key, prompt_limit, own_limit + prompt_total)
    return key < limit


def head_probs(query, key, mask):
    scores = jnp.where(mask, dot(query, key, NT) * (query.shape[1] ** -0.5), NEG_LARGE)
    exponent = jnp.exp(scores - jnp.max(scores, axis=-1, keepdims=True))
    return exponent / jnp.sum(exponent, axis=-1, keepdims=True)


def attend_kernel(heads, prompt_dev, prompt_total, meta_ref, q_ref, k_ref, v_ref, out_ref):
    mask = read_mask(meta_ref, q_ref.shape[0], k_ref.shape[0], prompt_dev, prompt_total)
    head = q_ref.shape[1] // heads
    for h in range(heads):
        at = slice(h * head, (h + 1) * head)
        weights = head_probs(q_ref[:, at], k_ref[:, at], mask).astype(BF16)
        out_ref[:, at] = dot(weights, v_ref[:, at]).astype(BF16)


def attend_back_kernel(
    heads, prompt_dev, prompt_total, meta_ref, q_ref, k_ref, v_ref, d_ref,
    dq_ref, dk_ref, dv_ref, dk_low_ref, dv_low_ref, rows_ref,
):
    mask = read_mask(meta_ref, q_ref.shape[0], k_ref.shape[0], prompt_dev, prompt_total)
    head = q_ref.shape[1] // heads
    mine = pl.ds(pl.multiple_of(meta_ref[0], prompt_dev), prompt_dev)

    def store(rows, own_ref, low_ref, at):
        low_ref[:, at] = rows[:prompt_total].astype(BF16)
        rows_ref[...] = rows[:prompt_total]
        own_ref[:prompt_dev, at] = rows_ref[mine, :]
        own_ref[prompt_dev:, at] = rows[prompt_total:]

    for h in range(heads):
        at = slice(h * head, (h + 1) * head)
        query, key, grad = q_ref[:, at], k_ref[:, at], d_ref[:, at]
        probs = head_probs(query, key, mask)
        d_probs = dot(grad, v_ref[:, at], NT)
        centre = jnp.sum(probs * d_probs, axis=-1, keepdims=True)
        d_scores = (probs * (d_probs - centre) * head**-0.5).astype(BF16)
        dq_ref[:, at] = dot(d_scores, key)
        store(dot(d_scores, query, TN), dk_ref, dk_low_ref, at)
        store(dot(probs.astype(BF16), grad, TN), dv_ref, dv_low_ref, at)


def value_kernel(own_ref, *refs):
    got, low_ref = refs[:-1], refs[-1]

    @pl.when(pl.program_id(0) == 0)
    def _():
        total = own_ref[...]
        for ref in got:
            total = total + ref[...].astype(F32)
        low_ref[...] = total.astype(BF16)

    @pl.when(pl.program_id(0) > 0)
    def _():
        low_ref[...] = own_ref[...].astype(BF16)


def value_rows_low(own, got):
    rows, width = own.shape
    step = got[0].shape[0] if got else 64
    row = pl.BlockSpec((step, width), lambda i: (i, 0))
    first = pl.BlockSpec((step, width), lambda i: (0, 0))
    return pl.pallas_call(
        value_kernel,
        grid=(rows // step,),
        in_specs=[row] + [first] * len(got),
        out_specs=row,
        out_shape=jax.ShapeDtypeStruct((rows, width), BF16),
        compiler_params=pltpu.CompilerParams(vmem_limit_bytes=VMEM_LIMIT),
        name="value_rows",
    )(own, *got)


def attention_call(kernel, name, arrays, outs, meta, prompt_dev, prompt_total, scratch=()):
    width = arrays[0].shape[1]
    heads = 4
    spec = lambda a: pl.BlockSpec((a.shape[0], width * heads // HEADS), lambda i, m: (0, i))
    return pl.pallas_call(
        functools.partial(kernel, heads, prompt_dev, prompt_total),
        grid_spec=pltpu.PrefetchScalarGridSpec(
            num_scalar_prefetch=1,
            grid=(HEADS // heads,),
            in_specs=[spec(a) for a in arrays],
            out_specs=[spec(a) for a in outs],
            scratch_shapes=scratch,
        ),
        out_shape=outs,
        compiler_params=pltpu.CompilerParams(vmem_limit_bytes=VMEM_LIMIT),
        name=name,
    )(meta, *arrays)


def expert_kernel(*refs):
    refs = refs[:10] + refs[-10:]
    (
        x0_ref, x1_ref, x2_ref, x3_ref, pick_ref, plain_ref, gate_w_ref, up_w_ref, router_ref, mine_ref,
        in_ref, act_ref, dg_ref, du_ref,
        keep_ref, send_ref, dprob_ref,
        total_ref, dp_ref, prob_ref,
    ) = refs
    step = pl.program_id(0)
    slots = pick_ref.shape[1]

    @pl.when(step == 0)
    def _():
        for s, x_ref in enumerate((x0_ref, x1_ref, x2_ref, x3_ref)):
            in_ref[s * slots : (s + 1) * slots, :] = dot(pick_ref[s], x_ref[...]).astype(BF16)
        logits = dot(in_ref[...], router_ref[...])
        exponent = jnp.exp(logits - jnp.max(logits, axis=1, keepdims=True))
        total = jnp.sum(exponent, axis=1, keepdims=True)
        prob_ref[...] = jnp.sum(exponent * mine_ref[...], axis=1, keepdims=True) / total

    rows = in_ref[...]
    gate_w, up_w = gate_w_ref[...], up_w_ref[...]
    gate_pre = dot(rows, gate_w, NT)
    up_pre = dot(rows, up_w, NT)
    plain = plain_ref[...]
    sigmoid = 1.0 / (1.0 + jnp.exp(-gate_pre))
    silu = gate_pre * sigmoid
    act = silu * up_pre
    prob = prob_ref[...]
    act_ref[...] = (prob * act).astype(BF16)
    d_act = prob * plain
    d_gate = (d_act * up_pre * (sigmoid * (1.0 + gate_pre * (1.0 - sigmoid)))).astype(BF16)
    d_up = (d_act * silu).astype(BF16)
    dg_ref[...] = d_gate
    du_ref[...] = d_up
    d_prob = jnp.sum(act * plain, axis=1, keepdims=True)
    d_in = dot(d_gate, gate_w) + dot(d_up, up_w)

    @pl.when(step == 0)
    def _():
        dp_ref[...] = d_prob
        total_ref[...] = d_in

    @pl.when(step > 0)
    def _():
        dp_ref[...] += d_prob
        total_ref[...] += d_in

    @pl.when(step == pl.num_programs(0) - 1)
    def _():
        values = total_ref[...].astype(BF16)
        for s in range(4):
            at = slice(s * slots, (s + 1) * slots)
            (keep_ref, send_ref)[s % 2][s // 2] = dot(pick_ref[s], values[at, :], TN).astype(BF16)
            dprob_ref[s : s + 1, :] = jnp.sum(
                pick_ref[s].astype(F32) * dp_ref[at, :], axis=0, keepdims=True
            )


def expert_quarter(quarter, blocks, pick, plain, gate_w, up_w, router, mine, kept):
    tokens, width = blocks[0].shape
    hidden = gate_w.shape[0]
    tile = 256
    slots = pick.shape[1]
    rows = 4 * slots
    whole = lambda *shape: pl.BlockSpec(shape, lambda f: (0,) * len(shape))
    any_spec = pl.BlockSpec(memory_space=pl.ANY)
    pair = jax.ShapeDtypeStruct((2, tokens, width), BF16)
    tiled = pl.BlockSpec((rows, tile), lambda f: (quarter, f))
    every = pick.shape[0] * slots
    return pl.pallas_call(
        expert_kernel,
        grid=(hidden // tile,),
        in_specs=[whole(tokens, width)] * 4
        + [
            pl.BlockSpec((4, slots, tokens), lambda f: (quarter, 0, 0)),
            tiled,
            pl.BlockSpec((tile, width), lambda f: (f, 0)),
            pl.BlockSpec((tile, width), lambda f: (f, 0)),
            whole(*router.shape),
            whole(*mine.shape),
        ]
        + [any_spec] * len(kept),
        out_specs=[
            pl.BlockSpec((rows, width), lambda f: (quarter, 0)),
            tiled,
            tiled,
            tiled,
        ]
        + [whole(2, tokens, width)] * 2
        + [whole(4, tokens)],
        out_shape=[
            jax.ShapeDtypeStruct((every, width), BF16),
            jax.ShapeDtypeStruct((every, hidden), BF16),
            jax.ShapeDtypeStruct((every, hidden), BF16),
            jax.ShapeDtypeStruct((every, hidden), BF16),
            pair,
            pair,
            jax.ShapeDtypeStruct((4, tokens), F32),
        ],
        scratch_shapes=[
            pltpu.VMEM((rows, width), F32),
            pltpu.VMEM((rows, 1), F32),
            pltpu.VMEM((rows, 1), F32),
        ],
        input_output_aliases={10 + k: k for k in range(len(kept))},
        compiler_params=pltpu.CompilerParams(vmem_limit_bytes=VMEM_LIMIT),
        name="expert",
    )(*blocks, pick, plain, gate_w, up_w, router, mine, *kept)


def expert_out_kernel(pick_ref, act_ref, down_ref, keep_ref, send_ref, values_ref):
    s = pl.program_id(1)

    @pl.when(s == 0)
    def _():
        values = dot(act_ref[...], down_ref[...]).astype(BF16)
        values_ref[...] = values.reshape(values_ref.shape)

    rows = dot(pick_ref[0], values_ref[s], TN).astype(BF16)

    @pl.when(s % 2 == 0)
    def _():
        keep_ref[0, 0] = rows

    @pl.when(s % 2 == 1)
    def _():
        send_ref[0, 0] = rows


def expert_out(pick, act, down_w):
    hidden, width = down_w.shape
    owners, slots, tokens = pick.shape
    rows = 4 * slots
    block = pl.BlockSpec((1, 1, tokens, width), lambda q, s: (q, s // 2, 0, 0))
    return pl.pallas_call(
        expert_out_kernel,
        grid=(owners // 4, 4),
        in_specs=[
            pl.BlockSpec((1, slots, tokens), lambda q, s: (4 * q + s, 0, 0)),
            pl.BlockSpec((rows, hidden), lambda q, s: (q, 0)),
            pl.BlockSpec((hidden, width), lambda q, s: (0, 0)),
        ],
        out_specs=[block, block],
        out_shape=[jax.ShapeDtypeStruct((owners // 4, 2, tokens, width), BF16)] * 2,
        scratch_shapes=[pltpu.VMEM((4, slots, width), BF16)],
        compiler_params=pltpu.CompilerParams(vmem_limit_bytes=VMEM_LIMIT),
        name="expert_out",
    )(pick, act, down_w)


def cot_kernel(source_ref, c0_ref, c1_ref, c2_ref, c3_ref, pick_ref, down_ref, slot_ref, plain_ref):
    slots = pick_ref.shape[1]

    @pl.when(pl.program_id(1) == 0)
    def _():
        for s, cot_ref in enumerate((c0_ref, c1_ref, c2_ref, c3_ref)):
            slot_ref[s * slots : (s + 1) * slots, :] = dot(pick_ref[s], cot_ref[0]).astype(BF16)

    plain_ref[...] = dot(slot_ref[...], down_ref[...], NT)


def gather_cot(source, all_cot, pick, down_w):
    hidden, width = down_w.shape
    owners, slots, tokens = pick.shape
    rows = 4 * slots
    tile = hidden // 2

    def block(s):
        return pl.BlockSpec((1, tokens, width), lambda q, f, m: (m[4 * q + s], 0, 0))

    return pl.pallas_call(
        cot_kernel,
        grid_spec=pltpu.PrefetchScalarGridSpec(
            num_scalar_prefetch=1,
            grid=(owners // 4, hidden // tile),
            in_specs=[block(s) for s in range(4)]
            + [
                pl.BlockSpec((4, slots, tokens), lambda q, f, m: (q, 0, 0)),
                pl.BlockSpec((tile, width), lambda q, f, m: (f, 0)),
            ],
            out_specs=[
                pl.BlockSpec((rows, width), lambda q, f, m: (q, 0)),
                pl.BlockSpec((rows, tile), lambda q, f, m: (q, f)),
            ],
        ),
        out_shape=[
            jax.ShapeDtypeStruct((owners * slots, width), BF16),
            jax.ShapeDtypeStruct((owners * slots, hidden), F32),
        ],
        compiler_params=pltpu.CompilerParams(vmem_limit_bytes=VMEM_LIMIT),
        name="gather_cot",
    )(source, all_cot, all_cot, all_cot, all_cot, pick, down_w)


def row_grads_kernel(cuts, me_ref, left_ref, right_ref, *outs):
    pieces, own_ref = outs[:-1], outs[-1]
    product = dot(left_ref[...], right_ref[...], TN)
    mine = pl.program_id(1) == me_ref[0]

    @pl.when(mine)
    def _():
        own_ref[...] = product

    @pl.when(jnp.logical_not(mine))
    def _():
        low = product.astype(BF16)
        for k, piece_ref in enumerate(pieces):
            piece_ref[0] = low[cuts[k] : cuts[k + 1], :]


def row_grads(me, planes, left, right, shares):
    count, hidden = left.shape
    width = right.shape[1]
    piece = hidden // planes
    tile = width // 2
    cuts = [piece * sum(shares[:k]) // sum(shares) for k in range(len(shares) + 1)]
    sizes = [high - low for low, high in zip(cuts, cuts[1:])]

    def place(n, p, m):
        ahead = (p - m[0] + planes) % planes
        idle = jnp.where(m[0] == planes - 1, planes - 2, 0)
        return (jnp.where(ahead == 0, idle, ahead - 1), 0, n)

    return pl.pallas_call(
        functools.partial(row_grads_kernel, cuts),
        grid_spec=pltpu.PrefetchScalarGridSpec(
            num_scalar_prefetch=1,
            grid=(width // tile, planes),
            in_specs=[
                pl.BlockSpec((count, piece), lambda n, p, m: (0, p)),
                pl.BlockSpec((count, tile), lambda n, p, m: (0, n)),
            ],
            out_specs=[pl.BlockSpec((1, size, tile), place) for size in sizes]
            + [pl.BlockSpec((piece, tile), lambda n, p, m: (0, n))],
        ),
        out_shape=[jax.ShapeDtypeStruct((planes - 1, size, width), BF16) for size in sizes]
        + [jax.ShapeDtypeStruct((piece, width), F32)],
        compiler_params=pltpu.CompilerParams(vmem_limit_bytes=VMEM_LIMIT),
        name="row_grads",
    )(me.reshape(1).astype(jnp.int32), left, right)


def weight_grad_kernel(planes, core_ref, left_ref, *refs):
    rights, (keep_ref, send_ref) = refs[:-2], refs[-2:]
    rows_e, pairs, size, tile = keep_ref.shape
    tokens = left_ref.shape[0] // planes
    count = len(rights) // planes
    size = size // count
    for k in range(count):
        product = sum(
            dot(left_ref[r * tokens : (r + 1) * tokens, :], rights[k * planes + r][...], TN)
            for r in range(planes)
        )
        split_rows = product.astype(BF16).reshape(rows_e, pairs, 2, size, tile)
        at = slice(k * size, (k + 1) * size)

        @pl.when(core_ref[0] == 0)
        def _():
            keep_ref[:, :, at, :] = split_rows[:, :, 0]
            send_ref[:, :, at, :] = split_rows[:, :, 1]

        @pl.when(core_ref[0] != 0)
        def _():
            keep_ref[:, :, at, :] = split_rows[:, :, 1]
            send_ref[:, :, at, :] = split_rows[:, :, 0]


def weight_grads(left, *rights):
    rows_e, rows_d = lax.axis_size("expert"), lax.axis_size("dp")
    planes = len(rights[0])
    total, part = left.shape
    width = rights[0][0].shape[1]
    tile = width // 4
    size = part // (rows_e * rows_d) * len(rights)
    core = (lax.axis_index("dp") % 2).reshape(1).astype(jnp.int32)
    block = pl.BlockSpec((rows_e, rows_d // 2, size, tile), lambda n, m: (0, 0, 0, n))
    return pl.pallas_call(
        functools.partial(weight_grad_kernel, planes),
        grid_spec=pltpu.PrefetchScalarGridSpec(
            num_scalar_prefetch=1,
            grid=(width // tile,),
            in_specs=[pl.BlockSpec((total, part), lambda n, m: (0, 0))]
            + [pl.BlockSpec((total // planes, tile), lambda n, m: (0, n))] * (planes * len(rights)),
            out_specs=[block, block],
        ),
        out_shape=[jax.ShapeDtypeStruct((rows_e, rows_d // 2, size, width), BF16)] * 2,
        compiler_params=pltpu.CompilerParams(vmem_limit_bytes=VMEM_LIMIT),
        name="weight_grads",
    )(core, left, *[array for right in rights for array in right])


def add_rows_kernel(counts, *refs):
    own_ref, parts, out_ref = refs[0], refs[1:-1], refs[-1]
    step = pl.program_id(0)
    at = 0
    for count, ref in zip(counts, parts):

        @pl.when((step >= at) & (step < at + count))
        def _():
            out_ref[...] = own_ref[...] + ref[...].astype(F32)

        at += count


def add_rows(own, parts):
    width = own.shape[1]
    step = math.gcd(*(p.shape[0] for p in parts))
    counts = [p.shape[0] // step for p in parts]
    starts = [sum(counts[:k]) for k in range(len(counts))]

    def spec(start, count):
        return pl.BlockSpec((step, width), lambda i: (jnp.clip(i - start, 0, count - 1), 0))

    rows = pl.BlockSpec((step, width), lambda i: (i, 0))
    return pl.pallas_call(
        functools.partial(add_rows_kernel, counts),
        grid=(own.shape[0] // step,),
        in_specs=[rows] + [spec(a, c) for a, c in zip(starts, counts)],
        out_specs=rows,
        out_shape=jax.ShapeDtypeStruct(own.shape, F32),
        compiler_params=pltpu.CompilerParams(vmem_limit_bytes=VMEM_LIMIT),
        name="add_rows",
    )(own, *parts)


def swap(value, axis, bit):
    return lax.ppermute(value, axis, [(i, i ^ bit) for i in range(lax.axis_size(axis))])


def plus(*values):
    return sum(v.astype(F32) for v in values).astype(values[0].dtype)


ORDER = [
    (i, j) for x in (0, 2) for z in (0, 2) for i in (z, z + 1) for j in (x, x + 1)
]


def fence(*values):
    return lax.optimization_barrier(values)


def split(values, axis_name, bit, at):
    mine = (lax.axis_index(axis_name) // bit) % 2

    def half(index):
        parts = []
        for value in values:
            shape = value.shape
            pairs = value.reshape(shape[:at] + (shape[at] // 2, 2) + shape[at + 1 :])
            parts.append(lax.dynamic_index_in_dim(pairs, index, at + 1, keepdims=False))
        return plus(*parts)

    return half(mine), half(1 - mine)


STAGES = (("dp", 1, 1), ("dp", 2, 1), ("expert", 1, 0), ("expert", 2, 0))


class RowScatter:
    def __init__(self, keep, send):
        self.keep, self.send = keep, send
        self.stage = 0

    def start(self):
        axis, bit, at = STAGES[self.stage]
        if self.stage:
            self.keep, self.send = split(self.parts, axis, bit, at)
        self.stage += 1
        return swap(self.send, axis, bit)

    def finish(self, received):
        self.parts = (self.keep, received)

    def result(self):
        value = plus(*self.parts)
        return value.reshape(value.shape[-2:])


def shards(
    prompt_in,
    cont_in,
    prompt_cot,
    cont_cot,
    prompt_routes,
    cont_routes,
    prefix,
    attn_gain,
    query_gain,
    key_gain,
    ffn_gain,
    w_query,
    w_key,
    w_value,
    w_output,
    w_router,
    expert_gate,
    expert_up,
    expert_down,
):
    prompt_dev, width = prompt_in.shape[1:]
    cont_len = cont_in.shape[2]
    tokens = prompt_dev + cont_len
    head_dim = width // HEADS
    top_count = prompt_routes.shape[2]
    expert_count = w_router.shape[1]
    hidden = expert_gate.shape[1]
    planes = lax.axis_size("context")
    me = lax.axis_index("context")
    rows_e, rows_d = lax.axis_size("expert"), lax.axis_size("dp")
    owners = rows_e * rows_d
    my_expert = lax.axis_index("expert") * rows_d + lax.axis_index("dp")
    prompt_total = prompt_dev * planes
    most_prompt = 9 * prompt_dev * top_count // (8 * expert_count)
    most_cont = 9 * cont_len * top_count // (8 * expert_count)
    slots = (most_prompt + most_cont + 15) // 16 * 16
    part = width // planes
    out_group = width // (rows_e * planes)

    def shift(value, r):
        return lax.ppermute(value, "context", [(i, (i + r) % planes) for i in range(planes)])

    def block(value, r):
        return lax.dynamic_slice_in_dim(value, ((me + r) % planes) * part, part, axis=1)

    def out_part(value, r):
        at = ((me + r) % planes) * out_group
        return jnp.concatenate(
            [
                lax.dynamic_slice_in_dim(value, e * planes * out_group + at, out_group, axis=1)
                for e in range(rows_e)
            ],
            axis=1,
        )

    def placed(blocks):
        full = jnp.zeros((tokens, width), blocks[0].dtype)
        for r, piece in enumerate(blocks):
            full = lax.dynamic_update_slice_in_dim(full, piece, ((me + r) % planes) * part, axis=1)
        return full

    others = range(1, planes)

    x_low = jnp.concatenate([prompt_in[0], cont_in[0, 0]], axis=0)
    x_rows = x_low.astype(F32)
    inverse = lax.rsqrt(jnp.mean(x_rows * x_rows, axis=-1) + EPSILON)
    x_blocks = [block(x_low, 0)] + [shift(block(x_low, r), r) for r in others]
    inverses = [inverse] + [shift(inverse, r) for r in others]
    gain_part = attn_gain.astype(F32)
    normed_blocks = [
        (piece.astype(F32) * inv[:, None] * gain_part).astype(BF16)
        for piece, inv in zip(x_blocks, inverses)
    ]

    def gathered(value, axis):
        shape = list(value.shape)
        shape[axis] = shape[axis] * planes
        full = jnp.zeros(shape, value.dtype)
        for r in range(planes):
            piece = shift(value, r) if r else value
            at = ((me - r) % planes) * value.shape[axis]
            full = lax.dynamic_update_slice_in_dim(full, piece, at, axis=axis)
        return full

    gains_in = jnp.stack([attn_gain, query_gain, key_gain, ffn_gain])

    d_out_low = jnp.concatenate([prompt_cot[0], cont_cot[0, 0]], axis=0)
    routes = jnp.concatenate([prompt_routes[0], cont_routes[0, 0]], axis=0)
    named = sum(
        (routes[:, k : k + 1] == jnp.arange(expert_count, dtype=jnp.int32)[None, :]).astype(F32)
        for k in range(top_count)
    )
    all_cot = lax.all_gather(d_out_low, PLANE, axis=0, tiled=True)

    start_len = prefix[0, 0]
    prompt_pos = me * prompt_dev + jnp.arange(prompt_dev, dtype=jnp.int32)
    positions = jnp.concatenate([prompt_pos, start_len + jnp.arange(cont_len, dtype=jnp.int32)])
    half_index = jnp.arange(head_dim // 2, dtype=F32)
    angles = positions.astype(F32)[:, None] * (10000.0 ** (-2.0 * half_index / head_dim))[None, :]
    cosine = jnp.cos(angles)
    sine = jnp.sin(angles)
    cosine = jnp.concatenate([cosine, cosine], axis=1)
    sine = jnp.concatenate([-sine, sine], axis=1)
    meta = jnp.stack([me * prompt_dev, start_len]).astype(jnp.int32)

    def project(pieces, weight):
        products = [dot(pieces[r], weight).astype(BF16) for r in others]
        fenced = fence(*pieces, *products)
        pieces, products = fenced[:planes], fenced[planes:]
        sent = [shift(product, planes - r) for r, product in zip(others, products)]
        return [dot(pieces[0], weight)] + sent, pieces

    def products(weight):
        return [dot(normed_blocks[r], weight).astype(BF16) for r in others]

    def shift_back(values):
        return [shift(v, planes - r) for r, v in zip(others, values)]

    key_low, value_low, named, gains_in, w_router, d_out_low, *normed_blocks = fence(
        products(w_key), products(w_value), named, gains_in, w_router, d_out_low, *normed_blocks
    )
    key_got, value_got = shift_back(key_low), shift_back(value_low)
    query_low = products(w_query)
    key_own, value_own = dot(normed_blocks[0], w_key), dot(normed_blocks[0], w_value)
    member = lax.all_to_all(named.T, PLANE, split_axis=0, concat_axis=0, tiled=True)
    gains = gathered(gains_in, 1)
    full_router = gathered(w_router, 0)
    key_got, value_got, query_low, key_own, value_own, member, gains, full_router, *normed_blocks = fence(
        key_got, value_got, query_low, key_own, value_own, member, gains, full_router, *normed_blocks
    )
    gains = gains.astype(F32)
    gain_attn, gain_query, gain_key, gain_ffn = [gains[i : i + 1] for i in range(4)]
    query_parts = [dot(normed_blocks[0], w_query)] + shift_back(query_low)
    key_raw, key_low = qk_post([key_own, *key_got], gain_key, cosine, sine)
    value_low = plus(value_own, *value_got).astype(BF16)
    query_raw, query_low = qk_post(query_parts, gain_query, cosine, sine)

    def with_prompt(rows):
        full = jnp.zeros((prompt_total + cont_len, width), BF16)
        full = lax.dynamic_update_slice_in_dim(full, rows[prompt_dev:], prompt_total, axis=0)
        for r in range(planes):
            piece = rows[:prompt_dev]
            if r:
                piece = shift(piece, planes - r)
            full = lax.dynamic_update_slice_in_dim(
                full, piece, ((me + r) % planes) * prompt_dev, axis=0
            )
        return full

    key_set = with_prompt(key_low)
    value_set = with_prompt(value_low)
    (attended,) = attention_call(
        attend_kernel,
        "attend",
        [query_low, key_set, value_set],
        [jax.ShapeDtypeStruct((tokens, width), BF16)],
        meta,
        prompt_dev,
        prompt_total,
    )

    attended_blocks = [block(attended, 0)] + [shift(block(attended, r), r) for r in others]
    mixed_rows = x_rows + sum(p.astype(F32) for p in project(attended_blocks, w_output)[0])
    inverse2 = lax.rsqrt(jnp.mean(mixed_rows * mixed_rows, axis=-1, keepdims=True) + EPSILON)
    normed2_low = (mixed_rows * inverse2 * gain_ffn).astype(BF16)

    normed_low = (x_rows * inverse[:, None] * gain_attn).astype(BF16)

    logits = dot(normed2_low, full_router)
    shifted = jnp.exp(logits - jnp.max(logits, axis=1, keepdims=True))
    router_probs = shifted / jnp.sum(shifted, axis=1, keepdims=True)

    my_e, my_d = lax.axis_index("expert"), lax.axis_index("dp")
    source = jnp.stack([(my_e ^ i) * rows_d + (my_d ^ j) for i, j in ORDER]).astype(jnp.int32)
    member = jnp.take(member, source, axis=0)

    def ranks(m):
        count = m.shape[1]
        before = jnp.triu(jnp.ones((count, count), BF16), 1)
        return dot(m.astype(BF16), before)

    slot_of = jnp.concatenate(
        [ranks(member[:, :prompt_dev]), ranks(member[:, prompt_dev:]) + most_prompt], axis=1
    )
    slot_of = jnp.where(member > 0, slot_of, -1.0)
    pick = (
        slot_of[:, None, :] == jnp.arange(slots, dtype=F32)[None, :, None]
    ).astype(BF16)
    gate_w, up_w, down_w = expert_gate[0], expert_up[0], expert_down[0]
    mine = (jnp.arange(expert_count, dtype=jnp.int32) == my_expert).astype(F32)[None, :]

    def z1(v):
        return swap(v, "expert", 1)

    def z2(v):
        return swap(v, "expert", 2)

    def core(v):
        return swap(v, "dp", 1)

    def across(v):
        return swap(v, "dp", 2)

    b0, all_cot, normed_low, router_probs = fence(normed2_low, all_cot, normed_low, router_probs)
    b1, b2, x0, c0 = z1(b0), z2(b0), across(b0), core(b0)
    normed_sent = [shift(out_part(normed_low, r), r) for r in others]
    attended_sent = [shift(out_part(attended, r), r) for r in others]
    all_cot = all_cot.reshape(owners, tokens, width)
    slot_cot, d_act_plain = gather_cot(source, all_cot, pick, down_w)
    b1, b2, x0, c0, d_act_plain, *rest = fence(
        b1, b2, x0, c0, d_act_plain, *normed_sent, *attended_sent
    )
    normed_out = jnp.concatenate([out_part(normed_low, 0), *rest[: planes - 1]], axis=0)
    attended_out = jnp.concatenate([out_part(attended, 0), *rest[planes - 1 :]], axis=0)
    b3, x1, c1, x0c = z1(b2), across(b1), core(b1), core(x0)
    b3, x1, c1, x0c = fence(b3, x1, c1, x0c)

    def quarter(q, blocks, kept):
        outs = expert_quarter(q, blocks, pick, d_act_plain, gate_w, up_w, full_router, mine, kept)
        return outs[:4], outs[4], outs[5], outs[6]

    x2, c2, c3, x1c = across(b2), core(b2), core(b3), core(x1)
    kept, keep0, send0, dprob0 = quarter(0, (b0, c0, b1, c1), ())
    x2, c2, c3, x1c, *kept = fence(x2, c2, c3, x1c, *kept)
    x3, x2c = across(b3), core(x2)
    kept, keep2, send2, dprob2 = quarter(2, (x0, x0c, x1, x1c), kept)
    x3, x2c, send2, *kept = fence(x3, x2c, send2, *kept)
    x3c, near2, near0 = core(x3), core(send2), core(send0)
    x3c, near2, near0, *kept = fence(x3c, near2, near0, *kept)
    got21 = across(add_blocks((keep2, 1), (near2, 1)))
    pair20 = add_blocks((keep2, 0), (near2, 0))
    kept, keep3, send3, dprob3 = quarter(3, (x2, x2c, x3, x3c), kept)
    got21, pair20, send3, *kept = fence(got21, pair20, send3, *kept)
    got20, near3 = across(pair20), core(send3)
    kept, keep1, send1, dprob1 = quarter(1, (b2, c2, b3, c3), kept)
    got20, near3, send1, *kept = fence(got20, near3, send1, *kept)
    slot_in, act_low, d_gate, d_up = kept

    piece = hidden // planes

    def send_rows(values):
        return [shift(values[r - 1], r) for r in others]

    first_got, near1 = z1(add_blocks((keep0, 1), (near0, 1), got21)), core(send1)
    got31 = across(add_blocks((keep3, 1), (near3, 1)))
    pair30 = add_blocks((keep3, 0), (near3, 0))
    *gate_low, gate_own = row_grads(me, planes, d_gate, slot_in, (1, 1))
    towards = jnp.arange(owners, dtype=jnp.int32)
    i_of, j_of = (towards // rows_d) ^ my_e, (towards % rows_d) ^ my_d
    place = (j_of // 2) * 8 + (i_of // 2) * 4 + (i_of % 2) * 2 + j_of % 2
    token_dprob = jnp.take(
        jnp.concatenate([dprob0, dprob1, dprob2, dprob3], axis=0), place, axis=0
    )
    first_got, got31, near1, gate_own, pair30, d_up, slot_in, token_dprob, *gate_low = fence(
        first_got, got31, near1, gate_own, pair30, d_up, slot_in, token_dprob, *gate_low
    )
    dprobs = lax.all_to_all(token_dprob, PLANE, split_axis=0, concat_axis=0, tiled=True).T
    second_got, got30 = z1(add_blocks((keep1, 1), (near1, 1), got31)), across(pair30)
    gate_a = send_rows(gate_low[0])
    *up_low, up_own = row_grads(me, planes, d_up, slot_in, (2, 4, 2))
    second_got, got30, dprobs, act_low, up_own, gate_b, up_0, up_1, up_2, *gate_a = fence(
        second_got, got30, dprobs, act_low, up_own, gate_low[1], *up_low, *gate_a
    )
    far_got = z2(add_blocks((keep1, 0), (near1, 0), got30, second_got))
    gate_b, up_a = send_rows(gate_b), send_rows(up_0)
    out_keep, out_send = expert_out(pick, act_low, down_w)
    far_got, act_low, out_keep, out_send, *rest = fence(
        far_got, act_low, out_keep, out_send, *gate_b, *up_a
    )
    gate_b, up_a = rest[: planes - 1], rest[planes - 1 :]

    out_near = core(out_send)
    d_mixed, branch_low, dlogit_low, ffn_gain_grad = norm_back(
        [(keep0, 0), (near0, 0), got20, first_got, far_got],
        d_out_low,
        mixed_rows,
        gain_ffn,
        router_probs,
        dprobs,
        full_router,
    )
    router_grad = dot(normed2_low, dlogit_low, TN)
    branch_low, act_low, out_near = fence(branch_low, act_low, out_near)

    def out_sum(q, i):
        return add_blocks((out_keep, q, i), (out_near, q, i))

    sent = [shift(branch_low, r) for r in others]
    out_got31, out_got30 = across(out_sum(3, 1)), across(out_sum(3, 0))
    *down_low, down_own = row_grads(me, planes, act_low, slot_cot, (1, 4, 3))
    out_got31, out_keep, out_near, down_own, down_0, down_1, down_2, branch_low, *sent = fence(
        out_got31, out_keep, out_near, down_own, *down_low, branch_low, *sent
    )
    branches = [branch_low, *sent]
    blocks_low = [dot(branches[r], w_output, NT).astype(BF16) for r in others]
    d_att_blocks = [shift(v, planes - r) for r, v in zip(others, blocks_low)]
    d_att_own = dot(branches[0], w_output, NT).astype(BF16)
    out_second = add_blocks((out_keep, 1, 1), (out_near, 1, 1), out_got31)
    out21 = out_sum(2, 1)
    d_att_own, up_1, out_second, out_got30, out21, gate_own, branch_low, *d_att_blocks = fence(
        d_att_own, up_1, out_second, out_got30, out21, gate_own, branch_low, *d_att_blocks
    )
    branches[0] = branch_low
    d_attended = placed([d_att_own, *d_att_blocks])

    out_got21, out_second = across(out21), z1(out_second)
    up_b = send_rows(up_1)
    output_keep, output_send = weight_grads(attended_out, branches)
    d_queries, d_keys, d_values_own, d_keys_low, d_values_low = attention_call(
        attend_back_kernel,
        "attend_back",
        [query_low, key_set, value_set, d_attended],
        [
            jax.ShapeDtypeStruct((tokens, width), F32),
            jax.ShapeDtypeStruct((tokens, width), F32),
            jax.ShapeDtypeStruct((tokens, width), F32),
            jax.ShapeDtypeStruct((prompt_total, width), BF16),
            jax.ShapeDtypeStruct((prompt_total, width), BF16),
        ],
        meta,
        prompt_dev,
        prompt_total,
        [pltpu.VMEM((prompt_total, head_dim), F32)],
    )
    out20 = out_sum(2, 0)
    (
        out_got21, out_second, output_keep, output_send, out20,
        d_queries, d_keys, d_values_own, d_keys_low, d_values_low, *up_b,
    ) = fence(
        out_got21, out_second, output_keep, output_send, out20,
        d_queries, d_keys, d_values_own, d_keys_low, d_values_low, *up_b,
    )
    output_rows = RowScatter(output_keep, output_send)

    def prompt_sent(rows):
        return [
            shift(
                lax.dynamic_slice_in_dim(
                    rows, ((me + r) % planes) * prompt_dev, prompt_dev, axis=0
                ),
                r,
            )
            for r in others
        ]

    value_prompt, key_prompt = prompt_sent(d_values_low), prompt_sent(d_keys_low)
    out_got20, output_got = across(out20), output_rows.start()
    d_query_low, query_gain_grad = qk_post_back(d_queries, query_raw, gain_query, cosine, sine)
    half = tokens // 2
    query_got_a = [shift(d_query_low[:half], r) for r in others]
    out_far = add_blocks((out_keep, 1, 0), (out_near, 1, 0), out_got30, out_second)
    out_first = add_blocks((out_keep, 0, 1), (out_near, 0, 1), out_got21)
    out_got20, output_got, out_far, out_first, d_query_low, gate_own, *rest = fence(
        out_got20, output_got, out_far, out_first, d_query_low, gate_own,
        *value_prompt, *key_prompt, *query_got_a,
    )
    output_rows.finish(output_got)
    value_prompt, key_prompt, query_got_a = (
        rest[k * (planes - 1) : (k + 1) * (planes - 1)] for k in range(3)
    )
    d_value_low = value_rows_low(d_values_own, value_prompt)

    def spread(low):
        return [shift(low, r) for r in others]

    def total(own, *parts):
        for k in range(planes - 1):
            own = add_rows(own, [p[k] for p in parts])
        return own

    d_value_low, output_rows.parts, *key_prompt = fence(
        d_value_low, output_rows.parts, *key_prompt
    )
    got = spread(d_value_low) + [shift(d_query_low[half:], r) for r in others]
    out_far_a, out_first, output_got = z2(out_far[:half]), z1(out_first), output_rows.start()
    d_normed_own = dot(d_value_low, w_value, NT) + dot(d_query_low, w_query, NT)
    d_key_low, key_gain_grad = qk_post_back(
        d_keys, key_raw, gain_key, cosine, sine, key_prompt
    )
    gate_grad = total(gate_own, gate_a, gate_b)
    out_far_a, out_far_b, out_first, output_got, d_key_low, gate_grad, d_normed_own, *rest = fence(
        out_far_a, out_far[half:], out_first, output_got, d_key_low, gate_grad, d_normed_own, *got
    )
    d_values = rest[: planes - 1]
    d_query_got = [
        jnp.concatenate([top, bottom], axis=0)
        for top, bottom in zip(query_got_a, rest[planes - 1 :])
    ]
    output_rows.finish(output_got)

    got, output_got, out_far_b = spread(d_key_low), output_rows.start(), z2(out_far_b)
    value_pair = weight_grads(normed_out, [d_value_low, *d_values])
    query_pair = weight_grads(normed_out, [d_query_low, *d_query_got])
    partial = [
        dot(d_values[k], w_value, NT) + dot(d_query_got[k], w_query, NT) for k in range(planes - 1)
    ]
    output_got, out_far_b, value_pair, query_pair, up_2, down_0, *rest = fence(
        output_got, out_far_b, value_pair, query_pair, up_2, down_0, *got, *partial
    )
    d_key_got, partial = rest[: planes - 1], rest[planes - 1 :]
    output_rows.finish(output_got)
    value_rows, query_rows = RowScatter(*value_pair), RowScatter(*query_pair)
    value_got, query_got = value_rows.start(), query_rows.start()
    key_pair = weight_grads(normed_out, [d_key_low, *d_key_got])
    blocks_low = [
        (partial[k] + dot(d_key_got[k], w_key, NT)).astype(BF16) for k in range(planes - 1)
    ]
    value_got, query_got, key_pair, d_key_low, *blocks_low = fence(
        value_got, query_got, key_pair, d_key_low, *blocks_low
    )
    value_rows.finish(value_got)
    query_rows.finish(query_got)
    key_rows = RowScatter(*key_pair)

    d_normed_got = [shift(v, planes - r) for r, v in zip(others, blocks_low)]
    value_got, output_got, key_got = value_rows.start(), output_rows.start(), key_rows.start()
    up_c, down_a = send_rows(up_2), send_rows(down_0)
    d_normed_own = d_normed_own + dot(d_key_low, w_key, NT)
    value_got, output_got, key_got, d_normed_own, down_1, *rest = fence(
        value_got, output_got, key_got, d_normed_own, down_1, *d_normed_got, *up_c, *down_a
    )
    d_normed_got, up_c, down_a = (rest[k * (planes - 1) : (k + 1) * (planes - 1)] for k in range(3))
    value_rows.finish(value_got)
    output_rows.finish(output_got)
    key_rows.finish(key_got)

    query_got, value_got = query_rows.start(), value_rows.start()
    down_b = send_rows(down_1)
    d_normed = placed([d_normed_own] + [p.astype(F32) for p in d_normed_got])
    scaled = gain_attn * d_normed
    centre = jnp.mean(scaled * x_rows, axis=-1, keepdims=True)
    inv = inverse[:, None]
    d_x = d_mixed + inv * scaled - x_rows * (inv**3 * centre)
    attn_gain_grad = jnp.sum(d_normed * x_rows * inv, axis=0)
    small_grads = jnp.concatenate(
        [
            jnp.stack(
                [attn_gain_grad, query_gain_grad[0], key_gain_grad[0], ffn_gain_grad[0]], axis=1
            ),
            router_grad,
        ],
        axis=1,
    )
    query_got, value_got, d_x, small_grads, down_2, out_first, *down_b = fence(
        query_got, value_got, d_x, small_grads, down_2, out_first, *down_b
    )
    query_rows.finish(query_got)
    value_rows.finish(value_got)
    out_rows = (
        mixed_rows
        + plus(out_keep[0, 0].astype(F32), out_near[0, 0])
        + out_got20.astype(F32)
        + out_first.astype(F32)
        + jnp.concatenate([out_far_a, out_far_b], axis=0).astype(F32)
    )


    def laid(own, *parts):
        for k in range(planes - 1):
            own = own + jnp.concatenate([p[k] for p in parts], axis=0).astype(F32)
        return own

    key_got, query_got, value_got = key_rows.start(), query_rows.start(), value_rows.start()
    by_plane = small_grads.reshape(rows_e, planes, out_group, small_grads.shape[1])

    def plane_rows(r):
        return lax.dynamic_index_in_dim(by_plane, (me + r) % planes, 1, False)

    small_sum = plus(plane_rows(0), *[shift(plane_rows(r), r) for r in others])
    down_c = send_rows(down_2)
    up_grad = laid(up_own, up_a, up_b, up_c)
    key_got, query_got, value_got, small_sum, up_grad, *down_c = fence(
        key_got, query_got, value_got, small_sum, up_grad, *down_c
    )
    key_rows.finish(key_got)
    query_rows.finish(query_got)
    value_rows.finish(value_got)

    key_got, query_got = key_rows.start(), query_rows.start()
    small_rows = RowScatter(
        *split([small_sum.reshape(rows_e, rows_d, -1, small_sum.shape[-1])], *STAGES[0])
    )
    for _ in range(2):
        small_rows.finish(small_rows.start())
    down_grad = laid(down_own, down_a, down_b, down_c)
    key_got, query_got, small_rows.parts, down_grad = fence(
        key_got, query_got, small_rows.parts, down_grad
    )
    key_rows.finish(key_got)
    query_rows.finish(query_got)
    key_rows.finish(key_rows.start())
    for _ in range(2):
        small_rows.finish(small_rows.start())
    small_grads = small_rows.result()
    return (
        out_rows[:prompt_dev].astype(BF16)[None],
        out_rows[prompt_dev:].astype(BF16)[None, None],
        d_x[:prompt_dev][None],
        d_x[prompt_dev:][None, None],
        small_grads[:, 0],
        small_grads[:, 1],
        small_grads[:, 2],
        small_grads[:, 3],
        query_rows.result().astype(F32),
        key_rows.result().astype(F32),
        value_rows.result().astype(F32),
        output_rows.result().astype(F32),
        small_grads[:, 4:],
        gate_grad[None],
        up_grad[None],
        down_grad[None],
    )


def solution(mesh):
    rows = P(("expert", "dp"), "context", None)
    conts = P(("expert", "dp"), "context", None, None)
    experts = P(("expert", "dp"), None, None)
    everywhere = ("expert", "context", "dp")
    in_specs = (
        (rows, conts, rows, conts, rows, conts, P(("expert", "dp"), "context"))
        + (P("context"),) * 4
        + (P("context", None),) * 5
        + (experts,) * 3
    )
    out_specs = (
        (rows, conts, rows, conts)
        + (P(everywhere),) * 4
        + (P(everywhere, None),) * 5
        + (rows,) * 3
    )
    return jax.shard_map(shards, mesh=mesh, in_specs=in_specs, out_specs=out_specs, check_vma=False)
```

```python
import functools
import math

import jax
import jax.numpy as jnp
from jax import lax
from jax.experimental import pallas as pl
from jax.experimental.pallas import tpu as pltpu
from jax.sharding import PartitionSpec as P

HEADS = 16
EPSILON = 1e-05
NEG_LARGE = -1e30
F32 = jnp.float32
BF16 = jnp.bfloat16
PLANE = ("expert", "dp")
VMEM_LIMIT = 48 * 1024 * 1024


def dot(left, right, dims=((1,), (0,)), out=F32):
    return lax.dot_general(left, right, (dims, ((), ())), preferred_element_type=out)


NT = ((1,), (1,))
TN = ((0,), (0,))


def post_kernel(count, *refs):
    parts, (gain_ref, cos_ref, sin_ref, raw_ref, low_ref) = refs[:count], refs[count:]
    raw = parts[0][...]
    for part in parts[1:]:
        raw = raw + part[...].astype(F32)
    raw_ref[...] = raw
    inverse = lax.rsqrt(jnp.mean(raw * raw, axis=-1, keepdims=True) + EPSILON)
    scaled = raw * inverse * gain_ref[...]
    cosine, sine = cos_ref[...], sin_ref[...]
    head = cosine.shape[1]
    for h in range(raw.shape[1] // head):
        piece = scaled[:, h * head : (h + 1) * head]
        turned = piece * cosine + pltpu.roll(piece, head // 2, 1) * sine
        low_ref[:, h * head : (h + 1) * head] = turned.astype(BF16)


def qk_post(parts, gain, cosine, sine):
    rows, width = parts[0].shape
    head = cosine.shape[1]
    step = 64
    row = lambda w: pl.BlockSpec((step, w), lambda i: (i, 0))
    return pl.pallas_call(
        functools.partial(post_kernel, len(parts)),
        grid=(rows // step,),
        in_specs=[row(width)] * len(parts)
        + [pl.BlockSpec((1, width), lambda i: (0, 0)), row(head), row(head)],
        out_specs=[row(width), row(width)],
        out_shape=[
            jax.ShapeDtypeStruct((rows, width), F32),
            jax.ShapeDtypeStruct((rows, width), BF16),
        ],
        compiler_params=pltpu.CompilerParams(vmem_limit_bytes=VMEM_LIMIT),
        name="qk_post",
    )(*parts, gain, cosine, sine)


def post_back_kernel(grad_ref, raw_ref, gain_ref, cos_ref, sin_ref, *refs):
    got, (low_ref, gain_grad_ref, sum_ref) = refs[:-3], refs[-3:]
    sum_ref[...] = grad_ref[...]
    if got:

        @pl.when(pl.program_id(0) == 0)
        def _():
            for ref in got:
                sum_ref[...] += ref[...].astype(F32)

    raw = raw_ref[...]
    inverse = lax.rsqrt(jnp.mean(raw * raw, axis=-1, keepdims=True) + EPSILON)
    cosine, sine = cos_ref[...], sin_ref[...]
    head = cosine.shape[1]
    pieces = []
    for h in range(raw.shape[1] // head):
        piece = sum_ref[:, h * head : (h + 1) * head]
        pieces.append(piece * cosine - pltpu.roll(piece, head // 2, 1) * sine)
    grad = jnp.concatenate(pieces, axis=1)
    scaled = grad * gain_ref[...]
    centre = jnp.mean(scaled * raw, axis=-1, keepdims=True)
    low_ref[...] = (inverse * scaled - raw * (inverse * inverse * inverse * centre)).astype(BF16)
    total = jnp.sum(grad * raw * inverse, axis=0, keepdims=True)

    @pl.when(pl.program_id(0) == 0)
    def _():
        gain_grad_ref[...] = total

    @pl.when(pl.program_id(0) > 0)
    def _():
        gain_grad_ref[...] += total


def qk_post_back(grad, raw, gain, cosine, sine, got=()):
    rows, width = raw.shape
    head = cosine.shape[1]
    step = got[0].shape[0] if got else 64
    row = lambda w: pl.BlockSpec((step, w), lambda i: (i, 0))
    whole = pl.BlockSpec((1, width), lambda i: (0, 0))
    return pl.pallas_call(
        post_back_kernel,
        grid=(rows // step,),
        in_specs=[row(width), row(width), whole, row(head), row(head)]
        + [pl.BlockSpec((step, width), lambda i: (0, 0))] * len(got),
        out_specs=[row(width), whole],
        out_shape=[
            jax.ShapeDtypeStruct((rows, width), BF16),
            jax.ShapeDtypeStruct((1, width), F32),
        ],
        scratch_shapes=[pltpu.VMEM((step, width), F32)],
        compiler_params=pltpu.CompilerParams(vmem_limit_bytes=VMEM_LIMIT),
        name="qk_post_back",
    )(grad, raw, gain, cosine, sine, *got)


def row_specs(items, step):
    pairs = [item if isinstance(item, tuple) else (item,) for item in items]

    def spec(array, at):
        width = array.shape[-1]
        return pl.BlockSpec((None,) * len(at) + (step, width), lambda i: at + (i, 0))

    return [p[0] for p in pairs], [spec(p[0], p[1:]) for p in pairs]


def add_blocks(*items):
    return plus(*[item[0][item[1:]] if isinstance(item, tuple) else item for item in items])


def norm_back_kernel(count, *refs):
    parts = refs[:count]
    (
        d_out_ref, mixed_ref, gain_ref, probs_ref, d_probs_ref, router_ref,
        d_mixed_ref, branch_ref, d_logit_ref, gain_grad_ref,
    ) = refs[count:]
    probs, d_probs = probs_ref[...], d_probs_ref[...]
    centre = jnp.sum(probs * d_probs, axis=1, keepdims=True)
    d_logit = (probs * (d_probs - centre)).astype(BF16)
    d_logit_ref[...] = d_logit
    grad = dot(d_logit, router_ref[...], NT)
    for part in parts:
        grad = grad + part[...].astype(F32)
    mixed = mixed_ref[...]
    inverse = lax.rsqrt(jnp.mean(mixed * mixed, axis=-1, keepdims=True) + EPSILON)
    scaled = grad * gain_ref[...]
    centre = jnp.mean(scaled * mixed, axis=-1, keepdims=True)
    d_mixed = (
        d_out_ref[...].astype(F32)
        + inverse * scaled
        - mixed * (inverse * inverse * inverse * centre)
    )
    d_mixed_ref[...] = d_mixed
    branch_ref[...] = d_mixed.astype(BF16)
    total = jnp.sum(grad * mixed * inverse, axis=0, keepdims=True)

    @pl.when(pl.program_id(0) == 0)
    def _():
        gain_grad_ref[...] = total

    @pl.when(pl.program_id(0) > 0)
    def _():
        gain_grad_ref[...] += total


def norm_back(parts, d_out, mixed, gain, probs, d_probs, router):
    rows, width = mixed.shape
    experts = probs.shape[1]
    step = 64
    row = lambda w: pl.BlockSpec((step, w), lambda i: (i, 0))
    whole = lambda *shape: pl.BlockSpec(shape, lambda i: (0, 0))
    parts, specs = row_specs(parts, step)
    return pl.pallas_call(
        functools.partial(norm_back_kernel, len(parts)),
        grid=(rows // step,),
        in_specs=specs
        + [row(width)] * 2
        + [whole(1, width), row(experts), row(experts), whole(width, experts)],
        out_specs=[row(width), row(width), row(experts), whole(1, width)],
        out_shape=[
            jax.ShapeDtypeStruct((rows, width), F32),
            jax.ShapeDtypeStruct((rows, width), BF16),
            jax.ShapeDtypeStruct((rows, experts), BF16),
            jax.ShapeDtypeStruct((1, width), F32),
        ],
        compiler_params=pltpu.CompilerParams(vmem_limit_bytes=VMEM_LIMIT),
        name="norm_back",
    )(*parts, d_out, mixed, gain, probs, d_probs, router)


def read_mask(meta_ref, rows, keys, prompt_dev, prompt_total):
    row = lax.broadcasted_iota(jnp.int32, (rows, keys), 0)
    key = lax.broadcasted_iota(jnp.int32, (rows, keys), 1)
    is_prompt_row = row < prompt_dev
    is_prompt_key = key < prompt_total
    prompt_limit = jnp.where(is_prompt_row, meta_ref[0] + row + 1, meta_ref[1])
    own_limit = jnp.where(is_prompt_row, 0, row - prompt_dev + 1)
    limit = jnp.where(is_prompt_key, prompt_limit, own_limit + prompt_total)
    return key < limit


def head_probs(query, key, mask):
    scores = jnp.where(mask, dot(query, key, NT) * (query.shape[1] ** -0.5), NEG_LARGE)
    exponent = jnp.exp(scores - jnp.max(scores, axis=-1, keepdims=True))
    return exponent / jnp.sum(exponent, axis=-1, keepdims=True)


def attend_kernel(heads, prompt_dev, prompt_total, meta_ref, q_ref, k_ref, v_ref, out_ref):
    mask = read_mask(meta_ref, q_ref.shape[0], k_ref.shape[0], prompt_dev, prompt_total)
    head = q_ref.shape[1] // heads
    for h in range(heads):
        at = slice(h * head, (h + 1) * head)
        weights = head_probs(q_ref[:, at], k_ref[:, at], mask).astype(BF16)
        out_ref[:, at] = dot(weights, v_ref[:, at]).astype(BF16)


def attend_back_kernel(
    heads, prompt_dev, prompt_total, meta_ref, q_ref, k_ref, v_ref, d_ref,
    dq_ref, dk_ref, dv_ref, dk_low_ref, dv_low_ref, rows_ref,
):
    mask = read_mask(meta_ref, q_ref.shape[0], k_ref.shape[0], prompt_dev, prompt_total)
    head = q_ref.shape[1] // heads
    mine = pl.ds(pl.multiple_of(meta_ref[0], prompt_dev), prompt_dev)

    def store(rows, own_ref, low_ref, at):
        low_ref[:, at] = rows[:prompt_total].astype(BF16)
        rows_ref[...] = rows[:prompt_total]
        own_ref[:prompt_dev, at] = rows_ref[mine, :]
        own_ref[prompt_dev:, at] = rows[prompt_total:]

    for h in range(heads):
        at = slice(h * head, (h + 1) * head)
        query, key, grad = q_ref[:, at], k_ref[:, at], d_ref[:, at]
        probs = head_probs(query, key, mask)
        d_probs = dot(grad, v_ref[:, at], NT)
        centre = jnp.sum(probs * d_probs, axis=-1, keepdims=True)
        d_scores = (probs * (d_probs - centre) * head**-0.5).astype(BF16)
        dq_ref[:, at] = dot(d_scores, key)
        store(dot(d_scores, query, TN), dk_ref, dk_low_ref, at)
        store(dot(probs.astype(BF16), grad, TN), dv_ref, dv_low_ref, at)


def value_kernel(own_ref, *refs):
    got, low_ref = refs[:-1], refs[-1]

    @pl.when(pl.program_id(0) == 0)
    def _():
        total = own_ref[...]
        for ref in got:
            total = total + ref[...].astype(F32)
        low_ref[...] = total.astype(BF16)

    @pl.when(pl.program_id(0) > 0)
    def _():
        low_ref[...] = own_ref[...].astype(BF16)


def value_rows_low(own, got):
    rows, width = own.shape
    step = got[0].shape[0] if got else 64
    row = pl.BlockSpec((step, width), lambda i: (i, 0))
    first = pl.BlockSpec((step, width), lambda i: (0, 0))
    return pl.pallas_call(
        value_kernel,
        grid=(rows // step,),
        in_specs=[row] + [first] * len(got),
        out_specs=row,
        out_shape=jax.ShapeDtypeStruct((rows, width), BF16),
        compiler_params=pltpu.CompilerParams(vmem_limit_bytes=VMEM_LIMIT),
        name="value_rows",
    )(own, *got)


def attention_call(kernel, name, arrays, outs, meta, prompt_dev, prompt_total, scratch=()):
    width = arrays[0].shape[1]
    heads = 4
    spec = lambda a: pl.BlockSpec((a.shape[0], width * heads // HEADS), lambda i, m: (0, i))
    return pl.pallas_call(
        functools.partial(kernel, heads, prompt_dev, prompt_total),
        grid_spec=pltpu.PrefetchScalarGridSpec(
            num_scalar_prefetch=1,
            grid=(HEADS // heads,),
            in_specs=[spec(a) for a in arrays],
            out_specs=[spec(a) for a in outs],
            scratch_shapes=scratch,
        ),
        out_shape=outs,
        compiler_params=pltpu.CompilerParams(vmem_limit_bytes=VMEM_LIMIT),
        name=name,
    )(meta, *arrays)


def expert_kernel(*refs):
    refs = refs[:10] + refs[-10:]
    (
        x0_ref, x1_ref, x2_ref, x3_ref, pick_ref, plain_ref, gate_w_ref, up_w_ref, router_ref, mine_ref,
        in_ref, act_ref, dg_ref, du_ref,
        keep_ref, send_ref, dprob_ref,
        total_ref, dp_ref, prob_ref,
    ) = refs
    step = pl.program_id(0)
    slots = pick_ref.shape[1]

    @pl.when(step == 0)
    def _():
        for s, x_ref in enumerate((x0_ref, x1_ref, x2_ref, x3_ref)):
            in_ref[s * slots : (s + 1) * slots, :] = dot(pick_ref[s], x_ref[...]).astype(BF16)
        logits = dot(in_ref[...], router_ref[...])
        exponent = jnp.exp(logits - jnp.max(logits, axis=1, keepdims=True))
        total = jnp.sum(exponent, axis=1, keepdims=True)
        prob_ref[...] = jnp.sum(exponent * mine_ref[...], axis=1, keepdims=True) / total

    rows = in_ref[...]
    gate_w, up_w = gate_w_ref[...], up_w_ref[...]
    gate_pre = dot(rows, gate_w, NT)
    up_pre = dot(rows, up_w, NT)
    plain = plain_ref[...]
    sigmoid = 1.0 / (1.0 + jnp.exp(-gate_pre))
    silu = gate_pre * sigmoid
    act = silu * up_pre
    prob = prob_ref[...]
    act_ref[...] = (prob * act).astype(BF16)
    d_act = prob * plain
    d_gate = (d_act * up_pre * (sigmoid * (1.0 + gate_pre * (1.0 - sigmoid)))).astype(BF16)
    d_up = (d_act * silu).astype(BF16)
    dg_ref[...] = d_gate
    du_ref[...] = d_up
    d_prob = jnp.sum(act * plain, axis=1, keepdims=True)
    d_in = dot(d_gate, gate_w) + dot(d_up, up_w)

    @pl.when(step == 0)
    def _():
        dp_ref[...] = d_prob
        total_ref[...] = d_in

    @pl.when(step > 0)
    def _():
        dp_ref[...] += d_prob
        total_ref[...] += d_in

    @pl.when(step == pl.num_programs(0) - 1)
    def _():
        values = total_ref[...].astype(BF16)
        for s in range(4):
            at = slice(s * slots, (s + 1) * slots)
            (keep_ref, send_ref)[s % 2][s // 2] = dot(pick_ref[s], values[at, :], TN).astype(BF16)
            dprob_ref[s : s + 1, :] = jnp.sum(
                pick_ref[s].astype(F32) * dp_ref[at, :], axis=0, keepdims=True
            )


def expert_quarter(quarter, blocks, pick, plain, gate_w, up_w, router, mine, kept):
    tokens, width = blocks[0].shape
    hidden = gate_w.shape[0]
    tile = 256
    slots = pick.shape[1]
    rows = 4 * slots
    whole = lambda *shape: pl.BlockSpec(shape, lambda f: (0,) * len(shape))
    any_spec = pl.BlockSpec(memory_space=pl.ANY)
    pair = jax.ShapeDtypeStruct((2, tokens, width), BF16)
    tiled = pl.BlockSpec((rows, tile), lambda f: (quarter, f))
    every = pick.shape[0] * slots
    return pl.pallas_call(
        expert_kernel,
        grid=(hidden // tile,),
        in_specs=[whole(tokens, width)] * 4
        + [
            pl.BlockSpec((4, slots, tokens), lambda f: (quarter, 0, 0)),
            tiled,
            pl.BlockSpec((tile, width), lambda f: (f, 0)),
            pl.BlockSpec((tile, width), lambda f: (f, 0)),
            whole(*router.shape),
            whole(*mine.shape),
        ]
        + [any_spec] * len(kept),
        out_specs=[
            pl.BlockSpec((rows, width), lambda f: (quarter, 0)),
            tiled,
            tiled,
            tiled,
        ]
        + [whole(2, tokens, width)] * 2
        + [whole(4, tokens)],
        out_shape=[
            jax.ShapeDtypeStruct((every, width), BF16),
            jax.ShapeDtypeStruct((every, hidden), BF16),
            jax.ShapeDtypeStruct((every, hidden), BF16),
            jax.ShapeDtypeStruct((every, hidden), BF16),
            pair,
            pair,
            jax.ShapeDtypeStruct((4, tokens), F32),
        ],
        scratch_shapes=[
            pltpu.VMEM((rows, width), F32),
            pltpu.VMEM((rows, 1), F32),
            pltpu.VMEM((rows, 1), F32),
        ],
        input_output_aliases={10 + k: k for k in range(len(kept))},
        compiler_params=pltpu.CompilerParams(vmem_limit_bytes=VMEM_LIMIT),
        name="expert",
    )(*blocks, pick, plain, gate_w, up_w, router, mine, *kept)


def expert_out_kernel(pick_ref, act_ref, down_ref, keep_ref, send_ref, values_ref):
    s = pl.program_id(1)

    @pl.when(s == 0)
    def _():
        values = dot(act_ref[...], down_ref[...]).astype(BF16)
        values_ref[...] = values.reshape(values_ref.shape)

    rows = dot(pick_ref[0], values_ref[s], TN).astype(BF16)

    @pl.when(s % 2 == 0)
    def _():
        keep_ref[0, 0] = rows

    @pl.when(s % 2 == 1)
    def _():
        send_ref[0, 0] = rows


def expert_out(pick, act, down_w):
    hidden, width = down_w.shape
    owners, slots, tokens = pick.shape
    rows = 4 * slots
    block = pl.BlockSpec((1, 1, tokens, width), lambda q, s: (q, s // 2, 0, 0))
    return pl.pallas_call(
        expert_out_kernel,
        grid=(owners // 4, 4),
        in_specs=[
            pl.BlockSpec((1, slots, tokens), lambda q, s: (4 * q + s, 0, 0)),
            pl.BlockSpec((rows, hidden), lambda q, s: (q, 0)),
            pl.BlockSpec((hidden, width), lambda q, s: (0, 0)),
        ],
        out_specs=[block, block],
        out_shape=[jax.ShapeDtypeStruct((owners // 4, 2, tokens, width), BF16)] * 2,
        scratch_shapes=[pltpu.VMEM((4, slots, width), BF16)],
        compiler_params=pltpu.CompilerParams(vmem_limit_bytes=VMEM_LIMIT),
        name="expert_out",
    )(pick, act, down_w)


def cot_kernel(source_ref, c0_ref, c1_ref, c2_ref, c3_ref, pick_ref, down_ref, slot_ref, plain_ref):
    slots = pick_ref.shape[1]

    @pl.when(pl.program_id(1) == 0)
    def _():
        for s, cot_ref in enumerate((c0_ref, c1_ref, c2_ref, c3_ref)):
            slot_ref[s * slots : (s + 1) * slots, :] = dot(pick_ref[s], cot_ref[0]).astype(BF16)

    plain_ref[...] = dot(slot_ref[...], down_ref[...], NT)


def gather_cot(source, all_cot, pick, down_w):
    hidden, width = down_w.shape
    owners, slots, tokens = pick.shape
    rows = 4 * slots
    tile = hidden // 2

    def block(s):
        return pl.BlockSpec((1, tokens, width), lambda q, f, m: (m[4 * q + s], 0, 0))

    return pl.pallas_call(
        cot_kernel,
        grid_spec=pltpu.PrefetchScalarGridSpec(
            num_scalar_prefetch=1,
            grid=(owners // 4, hidden // tile),
            in_specs=[block(s) for s in range(4)]
            + [
                pl.BlockSpec((4, slots, tokens), lambda q, f, m: (q, 0, 0)),
                pl.BlockSpec((tile, width), lambda q, f, m: (f, 0)),
            ],
            out_specs=[
                pl.BlockSpec((rows, width), lambda q, f, m: (q, 0)),
                pl.BlockSpec((rows, tile), lambda q, f, m: (q, f)),
            ],
        ),
        out_shape=[
            jax.ShapeDtypeStruct((owners * slots, width), BF16),
            jax.ShapeDtypeStruct((owners * slots, hidden), F32),
        ],
        compiler_params=pltpu.CompilerParams(vmem_limit_bytes=VMEM_LIMIT),
        name="gather_cot",
    )(source, all_cot, all_cot, all_cot, all_cot, pick, down_w)


def row_grads_kernel(cuts, me_ref, left_ref, right_ref, *outs):
    pieces, own_ref = outs[:-1], outs[-1]
    product = dot(left_ref[...], right_ref[...], TN)
    mine = pl.program_id(1) == me_ref[0]

    @pl.when(mine)
    def _():
        own_ref[...] = product

    @pl.when(jnp.logical_not(mine))
    def _():
        low = product.astype(BF16)
        for k, piece_ref in enumerate(pieces):
            piece_ref[0] = low[cuts[k] : cuts[k + 1], :]


def row_grads(me, planes, left, right, shares):
    count, hidden = left.shape
    width = right.shape[1]
    piece = hidden // planes
    tile = width // 2
    cuts = [piece * sum(shares[:k]) // sum(shares) for k in range(len(shares) + 1)]
    sizes = [high - low for low, high in zip(cuts, cuts[1:])]

    def place(n, p, m):
        ahead = (p - m[0] + planes) % planes
        idle = jnp.where(m[0] == planes - 1, planes - 2, 0)
        return (jnp.where(ahead == 0, idle, ahead - 1), 0, n)

    return pl.pallas_call(
        functools.partial(row_grads_kernel, cuts),
        grid_spec=pltpu.PrefetchScalarGridSpec(
            num_scalar_prefetch=1,
            grid=(width // tile, planes),
            in_specs=[
                pl.BlockSpec((count, piece), lambda n, p, m: (0, p)),
                pl.BlockSpec((count, tile), lambda n, p, m: (0, n)),
            ],
            out_specs=[pl.BlockSpec((1, size, tile), place) for size in sizes]
            + [pl.BlockSpec((piece, tile), lambda n, p, m: (0, n))],
        ),
        out_shape=[jax.ShapeDtypeStruct((planes - 1, size, width), BF16) for size in sizes]
        + [jax.ShapeDtypeStruct((piece, width), F32)],
        compiler_params=pltpu.CompilerParams(vmem_limit_bytes=VMEM_LIMIT),
        name="row_grads",
    )(me.reshape(1).astype(jnp.int32), left, right)


def weight_grad_kernel(planes, core_ref, left_ref, *refs):
    rights, (keep_ref, send_ref) = refs[:-2], refs[-2:]
    rows_e, pairs, size, tile = keep_ref.shape
    tokens = left_ref.shape[0] // planes
    count = len(rights) // planes
    size = size // count
    for k in range(count):
        product = sum(
            dot(left_ref[r * tokens : (r + 1) * tokens, :], rights[k * planes + r][...], TN)
            for r in range(planes)
        )
        split_rows = product.astype(BF16).reshape(rows_e, pairs, 2, size, tile)
        at = slice(k * size, (k + 1) * size)

        @pl.when(core_ref[0] == 0)
        def _():
            keep_ref[:, :, at, :] = split_rows[:, :, 0]
            send_ref[:, :, at, :] = split_rows[:, :, 1]

        @pl.when(core_ref[0] != 0)
        def _():
            keep_ref[:, :, at, :] = split_rows[:, :, 1]
            send_ref[:, :, at, :] = split_rows[:, :, 0]


def weight_grads(left, *rights):
    rows_e, rows_d = lax.axis_size("expert"), lax.axis_size("dp")
    planes = len(rights[0])
    total, part = left.shape
    width = rights[0][0].shape[1]
    tile = width // 4
    size = part // (rows_e * rows_d) * len(rights)
    core = (lax.axis_index("dp") % 2).reshape(1).astype(jnp.int32)
    block = pl.BlockSpec((rows_e, rows_d // 2, size, tile), lambda n, m: (0, 0, 0, n))
    return pl.pallas_call(
        functools.partial(weight_grad_kernel, planes),
        grid_spec=pltpu.PrefetchScalarGridSpec(
            num_scalar_prefetch=1,
            grid=(width // tile,),
            in_specs=[pl.BlockSpec((total, part), lambda n, m: (0, 0))]
            + [pl.BlockSpec((total // planes, tile), lambda n, m: (0, n))] * (planes * len(rights)),
            out_specs=[block, block],
        ),
        out_shape=[jax.ShapeDtypeStruct((rows_e, rows_d // 2, size, width), BF16)] * 2,
        compiler_params=pltpu.CompilerParams(vmem_limit_bytes=VMEM_LIMIT),
        name="weight_grads",
    )(core, left, *[array for right in rights for array in right])


def add_rows_kernel(counts, *refs):
    own_ref, parts, out_ref = refs[0], refs[1:-1], refs[-1]
    step = pl.program_id(0)
    at = 0
    for count, ref in zip(counts, parts):

        @pl.when((step >= at) & (step < at + count))
        def _():
            out_ref[...] = own_ref[...] + ref[...].astype(F32)

        at += count


def add_rows(own, parts):
    width = own.shape[1]
    step = math.gcd(*(p.shape[0] for p in parts))
    counts = [p.shape[0] // step for p in parts]
    starts = [sum(counts[:k]) for k in range(len(counts))]

    def spec(start, count):
        return pl.BlockSpec((step, width), lambda i: (jnp.clip(i - start, 0, count - 1), 0))

    rows = pl.BlockSpec((step, width), lambda i: (i, 0))
    return pl.pallas_call(
        functools.partial(add_rows_kernel, counts),
        grid=(own.shape[0] // step,),
        in_specs=[rows] + [spec(a, c) for a, c in zip(starts, counts)],
        out_specs=rows,
        out_shape=jax.ShapeDtypeStruct(own.shape, F32),
        compiler_params=pltpu.CompilerParams(vmem_limit_bytes=VMEM_LIMIT),
        name="add_rows",
    )(own, *parts)


def swap(value, axis, bit):
    return lax.ppermute(value, axis, [(i, i ^ bit) for i in range(lax.axis_size(axis))])


def plus(*values):
    return sum(v.astype(F32) for v in values).astype(values[0].dtype)


ORDER = [
    (i, j) for x in (0, 2) for z in (0, 2) for i in (z, z + 1) for j in (x, x + 1)
]


def fence(*values):
    return lax.optimization_barrier(values)


def split(values, axis_name, bit, at):
    mine = (lax.axis_index(axis_name) // bit) % 2

    def half(index):
        parts = []
        for value in values:
            shape = value.shape
            pairs = value.reshape(shape[:at] + (shape[at] // 2, 2) + shape[at + 1 :])
            parts.append(lax.dynamic_index_in_dim(pairs, index, at + 1, keepdims=False))
        return plus(*parts)

    return half(mine), half(1 - mine)


STAGES = (("dp", 1, 1), ("dp", 2, 1), ("expert", 1, 0), ("expert", 2, 0))


class RowScatter:
    def __init__(self, keep, send):
        self.keep, self.send = keep, send
        self.stage = 0

    def start(self):
        axis, bit, at = STAGES[self.stage]
        if self.stage:
            self.keep, self.send = split(self.parts, axis, bit, at)
        self.stage += 1
        return swap(self.send, axis, bit)

    def finish(self, received):
        self.parts = (self.keep, received)

    def result(self):
        value = plus(*self.parts)
        return value.reshape(value.shape[-2:])


def shards(
    prompt_in,
    cont_in,
    prompt_cot,
    cont_cot,
    prompt_routes,
    cont_routes,
    prefix,
    attn_gain,
    query_gain,
    key_gain,
    ffn_gain,
    w_query,
    w_key,
    w_value,
    w_output,
    w_router,
    expert_gate,
    expert_up,
    expert_down,
):
    prompt_dev, width = prompt_in.shape[1:]
    cont_len = cont_in.shape[2]
    tokens = prompt_dev + cont_len
    head_dim = width // HEADS
    top_count = prompt_routes.shape[2]
    expert_count = w_router.shape[1]
    hidden = expert_gate.shape[1]
    planes = lax.axis_size("context")
    me = lax.axis_index("context")
    rows_e, rows_d = lax.axis_size("expert"), lax.axis_size("dp")
    owners = rows_e * rows_d
    my_expert = lax.axis_index("expert") * rows_d + lax.axis_index("dp")
    prompt_total = prompt_dev * planes
    most_prompt = 9 * prompt_dev * top_count // (8 * expert_count)
    most_cont = 9 * cont_len * top_count // (8 * expert_count)
    slots = (most_prompt + most_cont + 15) // 16 * 16
    part = width // planes
    out_group = width // (rows_e * planes)

    def shift(value, r):
        return lax.ppermute(value, "context", [(i, (i + r) % planes) for i in range(planes)])

    def block(value, r):
        return lax.dynamic_slice_in_dim(value, ((me + r) % planes) * part, part, axis=1)

    def out_part(value, r):
        at = ((me + r) % planes) * out_group
        return jnp.concatenate(
            [
                lax.dynamic_slice_in_dim(value, e * planes * out_group + at, out_group, axis=1)
                for e in range(rows_e)
            ],
            axis=1,
        )

    def placed(blocks):
        full = jnp.zeros((tokens, width), blocks[0].dtype)
        for r, piece in enumerate(blocks):
            full = lax.dynamic_update_slice_in_dim(full, piece, ((me + r) % planes) * part, axis=1)
        return full

    others = range(1, planes)

    x_low = jnp.concatenate([prompt_in[0], cont_in[0, 0]], axis=0)
    x_rows = x_low.astype(F32)
    inverse = lax.rsqrt(jnp.mean(x_rows * x_rows, axis=-1) + EPSILON)
    x_blocks = [block(x_low, 0)] + [shift(block(x_low, r), r) for r in others]
    inverses = [inverse] + [shift(inverse, r) for r in others]
    gain_part = attn_gain.astype(F32)
    normed_blocks = [
        (piece.astype(F32) * inv[:, None] * gain_part).astype(BF16)
        for piece, inv in zip(x_blocks, inverses)
    ]

    def gathered(value, axis):
        shape = list(value.shape)
        shape[axis] = shape[axis] * planes
        full = jnp.zeros(shape, value.dtype)
        for r in range(planes):
            piece = shift(value, r) if r else value
            at = ((me - r) % planes) * value.shape[axis]
            full = lax.dynamic_update_slice_in_dim(full, piece, at, axis=axis)
        return full

    gains_in = jnp.stack([attn_gain, query_gain, key_gain, ffn_gain])

    d_out_low = jnp.concatenate([prompt_cot[0], cont_cot[0, 0]], axis=0)
    routes = jnp.concatenate([prompt_routes[0], cont_routes[0, 0]], axis=0)
    named = sum(
        (routes[:, k : k + 1] == jnp.arange(expert_count, dtype=jnp.int32)[None, :]).astype(F32)
        for k in range(top_count)
    )
    all_cot = lax.all_gather(d_out_low, PLANE, axis=0, tiled=True)

    start_len = prefix[0, 0]
    prompt_pos = me * prompt_dev + jnp.arange(prompt_dev, dtype=jnp.int32)
    positions = jnp.concatenate([prompt_pos, start_len + jnp.arange(cont_len, dtype=jnp.int32)])
    half_index = jnp.arange(head_dim // 2, dtype=F32)
    angles = positions.astype(F32)[:, None] * (10000.0 ** (-2.0 * half_index / head_dim))[None, :]
    cosine = jnp.cos(angles)
    sine = jnp.sin(angles)
    cosine = jnp.concatenate([cosine, cosine], axis=1)
    sine = jnp.concatenate([-sine, sine], axis=1)
    meta = jnp.stack([me * prompt_dev, start_len]).astype(jnp.int32)

    def project(pieces, weight):
        products = [dot(pieces[r], weight).astype(BF16) for r in others]
        fenced = fence(*pieces, *products)
        pieces, products = fenced[:planes], fenced[planes:]
        sent = [shift(product, planes - r) for r, product in zip(others, products)]
        return [dot(pieces[0], weight)] + sent, pieces

    def products(weight):
        return [dot(normed_blocks[r], weight).astype(BF16) for r in others]

    def shift_back(values):
        return [shift(v, planes - r) for r, v in zip(others, values)]

    key_low, value_low, named, gains_in, w_router, d_out_low, *normed_blocks = fence(
        products(w_key), products(w_value), named, gains_in, w_router, d_out_low, *normed_blocks
    )
    key_got, value_got = shift_back(key_low), shift_back(value_low)
    query_low = products(w_query)
    key_own, value_own = dot(normed_blocks[0], w_key), dot(normed_blocks[0], w_value)
    member = lax.all_to_all(named.T, PLANE, split_axis=0, concat_axis=0, tiled=True)
    gains = gathered(gains_in, 1)
    full_router = gathered(w_router, 0)
    key_got, value_got, query_low, key_own, value_own, member, gains, full_router, *normed_blocks = fence(
        key_got, value_got, query_low, key_own, value_own, member, gains, full_router, *normed_blocks
    )
    gains = gains.astype(F32)
    gain_attn, gain_query, gain_key, gain_ffn = [gains[i : i + 1] for i in range(4)]
    query_parts = [dot(normed_blocks[0], w_query)] + shift_back(query_low)
    key_raw, key_low = qk_post([key_own, *key_got], gain_key, cosine, sine)
    value_low = plus(value_own, *value_got).astype(BF16)
    query_raw, query_low = qk_post(query_parts, gain_query, cosine, sine)

    def with_prompt(rows):
        full = jnp.zeros((prompt_total + cont_len, width), BF16)
        full = lax.dynamic_update_slice_in_dim(full, rows[prompt_dev:], prompt_total, axis=0)
        for r in range(planes):
            piece = rows[:prompt_dev]
            if r:
                piece = shift(piece, planes - r)
            full = lax.dynamic_update_slice_in_dim(
                full, piece, ((me + r) % planes) * prompt_dev, axis=0
            )
        return full

    key_set = with_prompt(key_low)
    value_set = with_prompt(value_low)
    (attended,) = attention_call(
        attend_kernel,
        "attend",
        [query_low, key_set, value_set],
        [jax.ShapeDtypeStruct((tokens, width), BF16)],
        meta,
        prompt_dev,
        prompt_total,
    )

    attended_blocks = [block(attended, 0)] + [shift(block(attended, r), r) for r in others]
    mixed_rows = x_rows + sum(p.astype(F32) for p in project(attended_blocks, w_output)[0])
    inverse2 = lax.rsqrt(jnp.mean(mixed_rows * mixed_rows, axis=-1, keepdims=True) + EPSILON)
    normed2_low = (mixed_rows * inverse2 * gain_ffn).astype(BF16)

    normed_low = (x_rows * inverse[:, None] * gain_attn).astype(BF16)

    logits = dot(normed2_low, full_router)
    shifted = jnp.exp(logits - jnp.max(logits, axis=1, keepdims=True))
    router_probs = shifted / jnp.sum(shifted, axis=1, keepdims=True)

    my_e, my_d = lax.axis_index("expert"), lax.axis_index("dp")
    source = jnp.stack([(my_e ^ i) * rows_d + (my_d ^ j) for i, j in ORDER]).astype(jnp.int32)
    member = jnp.take(member, source, axis=0)

    def ranks(m):
        count = m.shape[1]
        before = jnp.triu(jnp.ones((count, count), BF16), 1)
        return dot(m.astype(BF16), before)

    slot_of = jnp.concatenate(
        [ranks(member[:, :prompt_dev]), ranks(member[:, prompt_dev:]) + most_prompt], axis=1
    )
    slot_of = jnp.where(member > 0, slot_of, -1.0)
    pick = (
        slot_of[:, None, :] == jnp.arange(slots, dtype=F32)[None, :, None]
    ).astype(BF16)
    gate_w, up_w, down_w = expert_gate[0], expert_up[0], expert_down[0]
    mine = (jnp.arange(expert_count, dtype=jnp.int32) == my_expert).astype(F32)[None, :]

    def z1(v):
        return swap(v, "expert", 1)

    def z2(v):
        return swap(v, "expert", 2)

    def core(v):
        return swap(v, "dp", 1)

    def across(v):
        return swap(v, "dp", 2)

    b0, all_cot, normed_low, router_probs = fence(normed2_low, all_cot, normed_low, router_probs)
    b1, b2, x0, c0 = z1(b0), z2(b0), across(b0), core(b0)
    normed_sent = [shift(out_part(normed_low, r), r) for r in others]
    attended_sent = [shift(out_part(attended, r), r) for r in others]
    all_cot = all_cot.reshape(owners, tokens, width)
    slot_cot, d_act_plain = gather_cot(source, all_cot, pick, down_w)
    b1, b2, x0, c0, d_act_plain, *rest = fence(
        b1, b2, x0, c0, d_act_plain, *normed_sent, *attended_sent
    )
    normed_out = jnp.concatenate([out_part(normed_low, 0), *rest[: planes - 1]], axis=0)
    attended_out = jnp.concatenate([out_part(attended, 0), *rest[planes - 1 :]], axis=0)
    b3, x1, c1, x0c = z1(b2), across(b1), core(b1), core(x0)
    b3, x1, c1, x0c = fence(b3, x1, c1, x0c)

    def quarter(q, blocks, kept):
        outs = expert_quarter(q, blocks, pick, d_act_plain, gate_w, up_w, full_router, mine, kept)
        return outs[:4], outs[4], outs[5], outs[6]

    x2, c2, c3, x1c = across(b2), core(b2), core(b3), core(x1)
    kept, keep0, send0, dprob0 = quarter(0, (b0, c0, b1, c1), ())
    x2, c2, c3, x1c, *kept = fence(x2, c2, c3, x1c, *kept)
    x3, x2c = across(b3), core(x2)
    kept, keep2, send2, dprob2 = quarter(2, (x0, x0c, x1, x1c), kept)
    x3, x2c, send2, *kept = fence(x3, x2c, send2, *kept)
    x3c, near2, near0 = core(x3), core(send2), core(send0)
    x3c, near2, near0, *kept = fence(x3c, near2, near0, *kept)
    got21 = across(add_blocks((keep2, 1), (near2, 1)))
    pair20 = add_blocks((keep2, 0), (near2, 0))
    kept, keep3, send3, dprob3 = quarter(3, (x2, x2c, x3, x3c), kept)
    got21, pair20, send3, *kept = fence(got21, pair20, send3, *kept)
    got20, near3 = across(pair20), core(send3)
    kept, keep1, send1, dprob1 = quarter(1, (b2, c2, b3, c3), kept)
    got20, near3, send1, *kept = fence(got20, near3, send1, *kept)
    slot_in, act_low, d_gate, d_up = kept

    piece = hidden // planes

    def send_rows(values):
        return [shift(values[r - 1], r) for r in others]

    first_got, near1 = z1(add_blocks((keep0, 1), (near0, 1), got21)), core(send1)
    pair31, keep3, near3 = fence(add_blocks((keep3, 1), (near3, 1)), keep3, near3)
    got31 = across(pair31)
    pair30 = add_blocks((keep3, 0), (near3, 0))
    *gate_low, gate_own = row_grads(me, planes, d_gate, slot_in, (1, 1))
    towards = jnp.arange(owners, dtype=jnp.int32)
    i_of, j_of = (towards // rows_d) ^ my_e, (towards % rows_d) ^ my_d
    place = (j_of // 2) * 8 + (i_of // 2) * 4 + (i_of % 2) * 2 + j_of % 2
    token_dprob = jnp.take(
        jnp.concatenate([dprob0, dprob1, dprob2, dprob3], axis=0), place, axis=0
    )
    first_got, got31, near1, gate_own, pair30, d_up, slot_in, token_dprob, *gate_low = fence(
        first_got, got31, near1, gate_own, pair30, d_up, slot_in, token_dprob, *gate_low
    )
    dprobs = lax.all_to_all(token_dprob, PLANE, split_axis=0, concat_axis=0, tiled=True).T
    second_got, got30 = z1(add_blocks((keep1, 1), (near1, 1), got31)), across(pair30)
    gate_a = send_rows(gate_low[0])
    *up_low, up_own = row_grads(me, planes, d_up, slot_in, (2, 4, 2))
    second_got, got30, dprobs, act_low, up_own, gate_b, up_0, up_1, up_2, *gate_a = fence(
        second_got, got30, dprobs, act_low, up_own, gate_low[1], *up_low, *gate_a
    )
    far_got = z2(add_blocks((keep1, 0), (near1, 0), got30, second_got))
    gate_b, up_a = send_rows(gate_b), send_rows(up_0)
    out_keep, out_send = expert_out(pick, act_low, down_w)
    far_got, act_low, out_keep, out_send, *rest = fence(
        far_got, act_low, out_keep, out_send, *gate_b, *up_a
    )
    gate_b, up_a = rest[: planes - 1], rest[planes - 1 :]

    out_near = core(out_send)
    d_mixed, branch_low, dlogit_low, ffn_gain_grad = norm_back(
        [(keep0, 0), (near0, 0), got20, first_got, far_got],
        d_out_low,
        mixed_rows,
        gain_ffn,
        router_probs,
        dprobs,
        full_router,
    )
    router_grad = dot(normed2_low, dlogit_low, TN)
    branch_low, act_low, out_near = fence(branch_low, act_low, out_near)

    def out_sum(q, i):
        return add_blocks((out_keep, q, i), (out_near, q, i))

    sent = [shift(branch_low, r) for r in others]
    out31, out_keep, out_near = fence(out_sum(3, 1), out_keep, out_near)
    out_got31, out_got30 = across(out31), across(out_sum(3, 0))
    *down_low, down_own = row_grads(me, planes, act_low, slot_cot, (1, 4, 3))
    out_got31, out_keep, out_near, down_own, down_0, down_1, down_2, branch_low, *sent = fence(
        out_got31, out_keep, out_near, down_own, *down_low, branch_low, *sent
    )
    branches = [branch_low, *sent]
    blocks_low = [dot(branches[r], w_output, NT).astype(BF16) for r in others]
    d_att_blocks = [shift(v, planes - r) for r, v in zip(others, blocks_low)]
    d_att_own = dot(branches[0], w_output, NT).astype(BF16)
    out_second = add_blocks((out_keep, 1, 1), (out_near, 1, 1), out_got31)
    out21 = out_sum(2, 1)
    d_att_own, up_1, out_second, out_got30, out21, gate_own, branch_low, *d_att_blocks = fence(
        d_att_own, up_1, out_second, out_got30, out21, gate_own, branch_low, *d_att_blocks
    )
    branches[0] = branch_low
    d_attended = placed([d_att_own, *d_att_blocks])

    out_got21, out_second = across(out21), z1(out_second)
    up_b = send_rows(up_1)
    output_keep, output_send = weight_grads(attended_out, branches)
    d_queries, d_keys, d_values_own, d_keys_low, d_values_low = attention_call(
        attend_back_kernel,
        "attend_back",
        [query_low, key_set, value_set, d_attended],
        [
            jax.ShapeDtypeStruct((tokens, width), F32),
            jax.ShapeDtypeStruct((tokens, width), F32),
            jax.ShapeDtypeStruct((tokens, width), F32),
            jax.ShapeDtypeStruct((prompt_total, width), BF16),
            jax.ShapeDtypeStruct((prompt_total, width), BF16),
        ],
        meta,
        prompt_dev,
        prompt_total,
        [pltpu.VMEM((prompt_total, head_dim), F32)],
    )
    out20 = out_sum(2, 0)
    (
        out_got21, out_second, output_keep, output_send, out20,
        d_queries, d_keys, d_values_own, d_keys_low, d_values_low, *up_b,
    ) = fence(
        out_got21, out_second, output_keep, output_send, out20,
        d_queries, d_keys, d_values_own, d_keys_low, d_values_low, *up_b,
    )
    output_rows = RowScatter(output_keep, output_send)

    def prompt_sent(rows):
        return [
            shift(
                lax.dynamic_slice_in_dim(
                    rows, ((me + r) % planes) * prompt_dev, prompt_dev, axis=0
                ),
                r,
            )
            for r in others
        ]

    value_prompt, key_prompt = prompt_sent(d_values_low), prompt_sent(d_keys_low)
    out_got20, output_got = across(out20), output_rows.start()
    d_query_low, query_gain_grad = qk_post_back(d_queries, query_raw, gain_query, cosine, sine)
    half = tokens // 2
    query_got_a = [shift(d_query_low[:half], r) for r in others]
    out_far = add_blocks((out_keep, 1, 0), (out_near, 1, 0), out_got30, out_second)
    out_first = add_blocks((out_keep, 0, 1), (out_near, 0, 1), out_got21)
    out_got20, output_got, out_far, out_first, d_query_low, gate_own, *rest = fence(
        out_got20, output_got, out_far, out_first, d_query_low, gate_own,
        *value_prompt, *key_prompt, *query_got_a,
    )
    output_rows.finish(output_got)
    value_prompt, key_prompt, query_got_a = (
        rest[k * (planes - 1) : (k + 1) * (planes - 1)] for k in range(3)
    )
    d_value_low = value_rows_low(d_values_own, value_prompt)

    def spread(low):
        return [shift(low, r) for r in others]

    def total(own, *parts):
        for k in range(planes - 1):
            own = add_rows(own, [p[k] for p in parts])
        return own

    d_value_low, output_rows.parts, *key_prompt = fence(
        d_value_low, output_rows.parts, *key_prompt
    )
    got = spread(d_value_low) + [shift(d_query_low[half:], r) for r in others]
    out_far_a, out_first, output_got = z2(out_far[:half]), z1(out_first), output_rows.start()
    d_normed_own = dot(d_value_low, w_value, NT) + dot(d_query_low, w_query, NT)
    d_key_low, key_gain_grad = qk_post_back(
        d_keys, key_raw, gain_key, cosine, sine, key_prompt
    )
    gate_grad = total(gate_own, gate_a, gate_b)
    out_far_a, out_far_b, out_first, output_got, d_key_low, gate_grad, d_normed_own, *rest = fence(
        out_far_a, out_far[half:], out_first, output_got, d_key_low, gate_grad, d_normed_own, *got
    )
    d_values = rest[: planes - 1]
    d_query_got = [
        jnp.concatenate([top, bottom], axis=0)
        for top, bottom in zip(query_got_a, rest[planes - 1 :])
    ]
    output_rows.finish(output_got)

    got, output_got, out_far_b = spread(d_key_low), output_rows.start(), z2(out_far_b)
    value_pair = weight_grads(normed_out, [d_value_low, *d_values])
    query_pair = weight_grads(normed_out, [d_query_low, *d_query_got])
    partial = [
        dot(d_values[k], w_value, NT) + dot(d_query_got[k], w_query, NT) for k in range(planes - 1)
    ]
    output_got, out_far_b, value_pair, query_pair, up_2, down_0, *rest = fence(
        output_got, out_far_b, value_pair, query_pair, up_2, down_0, *got, *partial
    )
    d_key_got, partial = rest[: planes - 1], rest[planes - 1 :]
    output_rows.finish(output_got)
    value_rows, query_rows = RowScatter(*value_pair), RowScatter(*query_pair)
    value_got, query_got = value_rows.start(), query_rows.start()
    key_pair = weight_grads(normed_out, [d_key_low, *d_key_got])
    blocks_low = [
        (partial[k] + dot(d_key_got[k], w_key, NT)).astype(BF16) for k in range(planes - 1)
    ]
    value_got, query_got, key_pair, d_key_low, *blocks_low = fence(
        value_got, query_got, key_pair, d_key_low, *blocks_low
    )
    value_rows.finish(value_got)
    query_rows.finish(query_got)
    key_rows = RowScatter(*key_pair)

    d_normed_got = [shift(v, planes - r) for r, v in zip(others, blocks_low)]
    value_got, output_got, key_got = value_rows.start(), output_rows.start(), key_rows.start()
    up_c, down_a = send_rows(up_2), send_rows(down_0)
    d_normed_own = d_normed_own + dot(d_key_low, w_key, NT)
    value_got, output_got, key_got, d_normed_own, down_1, *rest = fence(
        value_got, output_got, key_got, d_normed_own, down_1, *d_normed_got, *up_c, *down_a
    )
    d_normed_got, up_c, down_a = (rest[k * (planes - 1) : (k + 1) * (planes - 1)] for k in range(3))
    value_rows.finish(value_got)
    output_rows.finish(output_got)
    key_rows.finish(key_got)

    query_got, value_got = query_rows.start(), value_rows.start()
    down_b = send_rows(down_1)
    d_normed = placed([d_normed_own] + [p.astype(F32) for p in d_normed_got])
    scaled = gain_attn * d_normed
    centre = jnp.mean(scaled * x_rows, axis=-1, keepdims=True)
    inv = inverse[:, None]
    d_x = d_mixed + inv * scaled - x_rows * (inv**3 * centre)
    attn_gain_grad = jnp.sum(d_normed * x_rows * inv, axis=0)
    small_grads = jnp.concatenate(
        [
            jnp.stack(
                [attn_gain_grad, query_gain_grad[0], key_gain_grad[0], ffn_gain_grad[0]], axis=1
            ),
            router_grad,
        ],
        axis=1,
    )
    query_got, value_got, d_x, small_grads, down_2, out_first, *down_b = fence(
        query_got, value_got, d_x, small_grads, down_2, out_first, *down_b
    )
    query_rows.finish(query_got)
    value_rows.finish(value_got)
    out_rows = (
        mixed_rows
        + plus(out_keep[0, 0].astype(F32), out_near[0, 0])
        + out_got20.astype(F32)
        + out_first.astype(F32)
        + jnp.concatenate([out_far_a, out_far_b], axis=0).astype(F32)
    )


    def laid(own, *parts):
        for k in range(planes - 1):
            own = own + jnp.concatenate([p[k] for p in parts], axis=0).astype(F32)
        return own

    key_got, query_got, value_got = key_rows.start(), query_rows.start(), value_rows.start()
    by_plane = small_grads.reshape(rows_e, planes, out_group, small_grads.shape[1])

    def plane_rows(r):
        return lax.dynamic_index_in_dim(by_plane, (me + r) % planes, 1, False)

    small_sum = plus(plane_rows(0), *[shift(plane_rows(r), r) for r in others])
    down_c = send_rows(down_2)
    up_grad = laid(up_own, up_a, up_b, up_c)
    key_got, query_got, value_got, small_sum, up_grad, *down_c = fence(
        key_got, query_got, value_got, small_sum, up_grad, *down_c
    )
    key_rows.finish(key_got)
    query_rows.finish(query_got)
    value_rows.finish(value_got)

    key_got, query_got = key_rows.start(), query_rows.start()
    small_rows = RowScatter(
        *split([small_sum.reshape(rows_e, rows_d, -1, small_sum.shape[-1])], *STAGES[0])
    )
    for _ in range(2):
        small_rows.finish(small_rows.start())
    down_grad = laid(down_own, down_a, down_b, down_c)
    key_got, query_got, small_rows.parts, down_grad = fence(
        key_got, query_got, small_rows.parts, down_grad
    )
    key_rows.finish(key_got)
    query_rows.finish(query_got)
    key_rows.finish(key_rows.start())
    for _ in range(2):
        small_rows.finish(small_rows.start())
    small_grads = small_rows.result()
    return (
        out_rows[:prompt_dev].astype(BF16)[None],
        out_rows[prompt_dev:].astype(BF16)[None, None],
        d_x[:prompt_dev][None],
        d_x[prompt_dev:][None, None],
        small_grads[:, 0],
        small_grads[:, 1],
        small_grads[:, 2],
        small_grads[:, 3],
        query_rows.result().astype(F32),
        key_rows.result().astype(F32),
        value_rows.result().astype(F32),
        output_rows.result().astype(F32),
        small_grads[:, 4:],
        gate_grad[None],
        up_grad[None],
        down_grad[None],
    )


def solution(mesh):
    rows = P(("expert", "dp"), "context", None)
    conts = P(("expert", "dp"), "context", None, None)
    experts = P(("expert", "dp"), None, None)
    everywhere = ("expert", "context", "dp")
    in_specs = (
        (rows, conts, rows, conts, rows, conts, P(("expert", "dp"), "context"))
        + (P("context"),) * 4
        + (P("context", None),) * 5
        + (experts,) * 3
    )
    out_specs = (
        (rows, conts, rows, conts)
        + (P(everywhere),) * 4
        + (P(everywhere, None),) * 5
        + (rows,) * 3
    )
    return jax.shard_map(shards, mesh=mesh, in_specs=in_specs, out_specs=out_specs, check_vma=False)
```
